128 devices in a mesh: gx: 32 (over y, x, core), gy: 4 (over z).
Axes of the slice: x: 4, y: 4, z: 4, core: 2. Of those that a mesh axis runs over, the one named last changes fastest.
Arguments:
- charges: float32 [8192, 256], P(('gx', 'gy')), may hold values from -6 to 6
- points: float32 [8192, 3, 256], P(('gx', 'gy')), may hold values from 0 to 2
- leaf_bases: float32 [8192, 256, 64], P(('gx', 'gy')), may hold values from -0.75 to 0.75
- leaf_transfer: float32 [8192, 64, 64], P(('gx', 'gy')), may hold values from -0.75 to 0.75
- near_target: int32 [8192, 8], P(('gx', 'gy')), may hold values from -1 to 8191, as said below
- far_target: int32 [8192, 16], P(('gx', 'gy')), may hold values from -1 to 8191, as said below
- leaf_coupling: float32 [8192, 16, 64, 64], P(('gx', 'gy')), may hold values from -0.1875 to 0.1875
- cluster_transfer: float32 [128, 64, 64], P(('gx', 'gy')), may hold values from -0.75 to 0.75
- cluster_target: int32 [128, 8], P(('gx', 'gy')), may hold values from -1 to 127, as said below
- cluster_coupling: float32 [128, 8, 64, 64], P(('gx', 'gy')), may hold values from -0.03125 to 0.03125
- group_transfer: float32 [32, 64, 64], replicated, may hold values from -0.75 to 0.75
- group_target: int32 [32, 8], P('gx'), may hold values from -1 to 31, as said below
- group_coupling: float32 [32, 8, 64, 64], P('gx'), may hold values from -0.015625 to 0.015625
- top_target: int32 [8, 4], replicated, may hold values from -1 to 7, as said below
- top_coupling: float32 [8, 4, 64, 64], replicated, may hold values from -0.01171875 to 0.01171875
Outputs:
- potential: float32 [8192, 256], P(('gx', 'gy'))
The draws below stay inside these ranges and needn't reach their ends.
Inputs may be any that keep to these rules, and one draw needn't show every extreme that they name: `near_target`: live slots of a row come first. A live target of leaf i lies among the leaves of i's own device cluster and of the device clusters just before and after it. `far_target`: live slots of a row come first. A live target of leaf i lies among the leaves of the device clusters at most 2 before or after i's own. `cluster_target`: live slots of a row come first. `group_target`: live slots of a row come first. `top_target`: live slots of a row come first.
All inputs are finite; a program needn't handle non-finite values.
Results may differ from the reference program's by a relative error of at most 0.00012.
Values sent between devices are 32-bit elements; how exact they have to be, the bound alone decides.
A program may use at most 128 MiB of HBM per device.

```python
import math
import jax
import jax.numpy as jnp
from jax import lax

LEAF = 256
RANK = 64
NL = 64
NEAR = 8
FAR = 16
FAR1 = 8
FAR2 = 8
FAR3 = 4
SPAN = 2
LEAVES = 8192
CLUSTERS = 128
GROUPS = 32
TOPS = 8
N_GY = 4


def window_targets(key, row_total, slot_total, reach_devices, per_device):
    subkeys = jax.random.split(key, 3)
    row_index = jnp.arange(row_total)
    owner = row_index // per_device
    device_total = row_total // per_device
    lower_bound = jnp.maximum(owner - reach_devices, 0) * per_device
    upper_bound = jnp.minimum(owner + reach_devices + 1, device_total) * per_device
    chosen = jax.random.randint(subkeys[0], (row_total, slot_total), lower_bound[:, None], upper_bound[:, None])
    chosen = chosen.at[0, 0].set(0).at[row_total - 1, 0].set(row_total - 1)
    live_count = jax.random.randint(subkeys[1], (row_total,), 1, slot_total + 1)
    last_count = jax.random.randint(subkeys[2], (), 1, max(slot_total, 2))
    live_count = live_count.at[0].set(slot_total).at[row_total - 1].set(last_count)
    slot_index = jnp.arange(slot_total)
    return jnp.where(slot_index[None, :] < live_count[:, None], chosen, -1).astype(jnp.int32)


def draw_near_target(key, part):
    key = jax.random.fold_in(key, 1)
    return window_targets(key, LEAVES, NEAR, 1, NL)


def draw_far_target(key, part):
    key = jax.random.fold_in(key, 2)
    return window_targets(key, LEAVES, FAR, SPAN, NL)


def draw_cluster_target(key, part):
    key = jax.random.fold_in(key, 3)
    return window_targets(key, CLUSTERS, FAR1, CLUSTERS, 1)


def draw_group_target(key, part):
    key = jax.random.fold_in(key, 4)
    return window_targets(key, GROUPS, FAR2, GROUPS, 1)


def draw_top_target(key, part):
    key = jax.random.fold_in(key, 5)
    return window_targets(key, TOPS, FAR3, TOPS, 1)


def block_scale(key, shape, shards, least, high):
    def one(axis_at, blocks):
        heights = jax.random.uniform(jax.random.fold_in(jax.random.fold_in(key, 6), axis_at), (blocks,), jnp.float32, least / len(shards), high / len(shards))
        return jnp.repeat(jnp.exp(heights), shape[axis_at] // blocks).reshape((-1,) + (1,) * (len(shape) - axis_at - 1))

    loudness = one(*shards[0])
    for cut in shards[1:]:
        loudness = loudness * one(*cut)
    return loudness


def noise(rng, dims, spread, limit, cuts=(), dtype=jnp.bfloat16):
    factor_of = block_scale(rng, dims, cuts, -0.22, 0.18) if cuts else 1.0
    drawn = jax.random.normal(rng, dims, jnp.float32) * spread * factor_of
    return jnp.minimum(jnp.maximum(drawn, -limit), limit).astype(dtype)


def setup_inputs(seed: int = 0) -> dict:
    keys = jax.random.split(jax.random.key(seed), 16)
    charges = noise(keys[0], (LEAVES, LEAF), 1.0, 6.0, ((0, 128),), jnp.float32)
    points = jnp.clip(2.0 * jax.random.uniform(keys[1], (LEAVES, 3, LEAF), jnp.float32) ** block_scale(keys[1], (LEAVES, 3, LEAF), ((0, 128),), -0.2, 0.2), 0.0, 2.0)
    leaf_bases = noise(keys[2], (LEAVES, LEAF, RANK), RANK ** -0.5, 0.75, ((0, 128),), jnp.float32)
    leaf_transfer = noise(keys[3], (LEAVES, RANK, RANK), RANK ** -0.5, 0.75, ((0, 128),), jnp.float32)
    near_target = draw_near_target(jax.random.fold_in(keys[15], 71), 0)
    far_target = draw_far_target(jax.random.fold_in(keys[15], 71), 0)
    leaf_coupling = noise(keys[6], (LEAVES, FAR, RANK, RANK), (RANK * FAR) ** -0.5, 0.1875, ((0, 128),), jnp.float32)
    cluster_transfer = noise(keys[7], (CLUSTERS, RANK, RANK), RANK ** -0.5, 0.75, ((0, 128),), jnp.float32)
    cluster_target = draw_cluster_target(jax.random.fold_in(keys[15], 71), 0)
    cluster_coupling = noise(keys[9], (CLUSTERS, FAR1, RANK, RANK), (RANK * FAR1 * NL) ** -0.5, 0.03125, ((0, 128),), jnp.float32)
    group_transfer = noise(keys[10], (GROUPS, RANK, RANK), RANK ** -0.5, 0.75, (), jnp.float32)
    group_target = draw_group_target(jax.random.fold_in(keys[15], 71), 0)
    group_coupling = noise(keys[12], (GROUPS, FAR2, RANK, RANK), (RANK * FAR2 * NL * N_GY) ** -0.5, 0.015625, ((0, 32),), jnp.float32)
    top_target = draw_top_target(jax.random.fold_in(keys[15], 71), 0)
    top_coupling = noise(keys[14], (TOPS, FAR3, RANK, RANK), (RANK * FAR3 * NL * N_GY * 4) ** -0.5, 0.01171875, (), jnp.float32)
    return dict(charges=charges, points=points, leaf_bases=leaf_bases, leaf_transfer=leaf_transfer, near_target=near_target, far_target=far_target, leaf_coupling=leaf_coupling, cluster_transfer=cluster_transfer, cluster_target=cluster_target, cluster_coupling=cluster_coupling, group_transfer=group_transfer, group_target=group_target, group_coupling=group_coupling, top_target=top_target, top_coupling=top_coupling)


smoothing_sq = 0.01
inverse_four_pi = 1.0 / (4.0 * math.pi)
highest = lax.Precision.HIGHEST

def kernel_sum(target_points, source_points, source_charges):
    distance = jnp.full((source_points.shape[0], target_points.shape[1], source_points.shape[2]), smoothing_sq, jnp.float32)
    for component in range(3):
        offset = target_points[component][None, :, None] - source_points[:, component][:, None, :]
        distance = distance + offset * offset
    return lax.optimization_barrier(jnp.sum(lax.rsqrt(distance) * source_charges[:, None, :], axis=(0, 2))) * inverse_four_pi

def couple_level(coupling, targets, moments):
    usable = (targets >= 0).astype(jnp.float32)
    picked = moments[jnp.maximum(targets, 0)] * usable[..., None]
    return jnp.einsum('nfrs,nfs->nr', coupling, picked, precision=highest)

def reference(charges, points, leaf_bases, leaf_transfer, near_target, far_target, leaf_coupling, cluster_transfer, cluster_target, cluster_coupling, group_transfer, group_target, group_coupling, top_target, top_coupling):
    usable = (near_target >= 0).astype(jnp.float32)
    clipped = jnp.maximum(near_target, 0)

    def near_leaf(inputs):
        target_points, slot_ids, weights = inputs
        return kernel_sum(target_points, points[slot_ids], charges[slot_ids] * weights[:, None])
    near_part = lax.map(near_leaf, (points, clipped, usable))
    leaf_moments = jnp.einsum('ipr,ip->ir', leaf_bases, charges, precision=highest)
    cluster_moments = jnp.einsum('dlrs,dlr->ds', leaf_transfer.reshape(CLUSTERS, NL, RANK, RANK), leaf_moments.reshape(CLUSTERS, NL, RANK), precision=highest)
    group_moments = jnp.einsum('gkrs,gkr->gs', cluster_transfer.reshape(GROUPS, N_GY, RANK, RANK), cluster_moments.reshape(GROUPS, N_GY, RANK), precision=highest)
    top_moments = jnp.einsum('hkrs,hkr->hs', group_transfer.reshape(TOPS, 4, RANK, RANK), group_moments.reshape(TOPS, 4, RANK), precision=highest)
    top_local = couple_level(top_coupling, top_target, top_moments)
    group_local = couple_level(group_coupling, group_target, group_moments) + jnp.einsum('grs,gs->gr', group_transfer, jnp.repeat(top_local, 4, axis=0), precision=highest)
    cluster_local = couple_level(cluster_coupling, cluster_target, cluster_moments) + jnp.einsum('drs,ds->dr', cluster_transfer, jnp.repeat(group_local, N_GY, axis=0), precision=highest)
    leaf_local = couple_level(leaf_coupling, far_target, leaf_moments) + jnp.einsum('irs,is->ir', leaf_transfer, jnp.repeat(cluster_local, NL, axis=0), precision=highest)
    far_part = jnp.einsum('ipr,ir->ip', leaf_bases, leaf_local, precision=highest)
    return near_part + far_part
```

```python
import functools
import math

import jax
import jax.numpy as jnp
from jax import lax
from jax.experimental import pallas as pl
from jax.experimental.pallas import tpu as pltpu
from jax.sharding import PartitionSpec as P

MESH = pl.DeviceIdType.MESH
F32 = jnp.float32
BF16 = jnp.bfloat16
SMOOTHING = 0.01
INVERSE_FOUR_PI = 1.0 / (4.0 * math.pi)

LEAVES = 64
POINTS = 256
RANK = 64
NEAR = 8
FAR = 16
TERMS = 32
PAIRS = LEAVES * NEAR
GROUP = 8
CHUNK = 8
DEVICES = 128
BLOCK = 8
BLOCKS = DEVICES // BLOCK
BLANK = 3 * LEAVES


def split3(value):
    high = value.astype(BF16).astype(F32)
    rest = value - high
    middle = rest.astype(BF16).astype(F32)
    low = (rest - middle).astype(BF16).astype(F32)
    return high, middle, low


def centred(points):
    shifted = [p - 1.0 for p in points]
    norm = shifted[0] * shifted[0] + shifted[1] * shifted[1] + shifted[2] * shifted[2]
    return [split3(u) for u in shifted], norm


def source_terms(parts, norm):
    rows = []
    for high, middle, low in parts:
        high, middle, low = -2.0 * high, -2.0 * middle, -2.0 * low
        rows += [high, high, high, middle, middle, low]
    one = jnp.ones_like(norm)
    return rows + list(split3(norm + SMOOTHING)) + [one, one, one]


def target_terms(parts, norm):
    rows = []
    for high, middle, low in parts:
        rows += [high, middle, low, high, middle, high]
    one = jnp.ones_like(norm)
    return rows + [one, one, one] + list(split3(norm))


def by_leaf(rows):
    blank = jnp.zeros_like(rows[0])
    return jnp.swapaxes(jnp.stack(rows + [blank] * (TERMS - len(rows)), axis=0), 0, 1)


def eye():
    shape = (RANK, RANK)
    return (lax.broadcasted_iota(jnp.int32, shape, 0) == lax.broadcasted_iota(jnp.int32, shape, 1)).astype(F32)


def to_column(row, unit):
    return jnp.sum(unit * row, axis=1, keepdims=True)


def to_row(column, unit):
    return jnp.sum(unit * column, axis=0, keepdims=True)


def exchange_kernel(
    charges, points, near, far, cluster_transfer, bases_hbm, transfer_hbm,
    source_out, target_out, charge_out, moment_out, every_out, far_out, pair_out,
    bases, transfer, halo_charges, halo_points, window, every,
    load_sems, halo_send, halo_recv, moment_send, moment_recv, one_send, one_recv, two_send, two_recv,
):
    gx, gy = lax.axis_index("gx"), lax.axis_index("gy")
    device = gx * 4 + gy

    def place(index):
        return (index // 4, index % 4)

    def beside(distance):
        return place((device + distance + DEVICES) % DEVICES)

    place_in_block = device % BLOCK
    block = device // BLOCK
    chunks = LEAVES // CHUNK

    def load_copies(c):
        span = pl.ds(c * CHUNK, CHUNK)
        return (
            pltpu.make_async_copy(bases_hbm.at[span], bases.at[span], load_sems.at[0, c]),
            pltpu.make_async_copy(transfer_hbm.at[span], transfer.at[span], load_sems.at[1, c]),
        )

    @pl.loop(0, chunks)
    def _(c):
        for copy in load_copies(c):
            copy.start()

    barrier = pltpu.get_barrier_semaphore()
    for distance in (1, -1, 2, -2):
        pl.semaphore_signal(barrier, inc=1, device_id=beside(distance), device_id_type=MESH)

    def block_mate(k):
        return place(block * BLOCK + (place_in_block + k) % BLOCK)

    def far_mate(k):
        return place(((block + k) % BLOCKS) * BLOCK + place_in_block)

    @pl.loop(1, BLOCK)
    def _(k):
        pl.semaphore_signal(barrier, inc=1, device_id=block_mate(k), device_id_type=MESH)

    @pl.loop(1, BLOCKS)
    def _(k):
        pl.semaphore_signal(barrier, inc=1, device_id=far_mate(k), device_id_type=MESH)

    pl.semaphore_wait(barrier, 4 + BLOCK - 1 + BLOCKS - 1)

    def halo_copies():
        copies = []
        for side, distance in ((0, 1), (1, -1)):
            for kind, (source, landing) in enumerate(((charges, halo_charges), (points, halo_points))):
                copies.append(
                    pltpu.make_async_remote_copy(
                        src_ref=source,
                        dst_ref=landing.at[side],
                        send_sem=halo_send.at[side, kind],
                        recv_sem=halo_recv.at[side, kind],
                        device_id=beside(distance),
                        device_id_type=MESH,
                    )
                )
        return copies

    halo = halo_copies()
    for copy in halo:
        copy.start()

    lane = lax.broadcasted_iota(jnp.int32, (RANK, LEAVES), 1)

    def moment_chunk(c, carry):
        columns, total = carry
        for copy in load_copies(c):
            copy.wait()
        weights = charges[pl.ds(pl.multiple_of(c * CHUNK, CHUNK), CHUNK), :]
        for k in range(CHUNK):
            product = bases[c * CHUNK + k] * weights[k : k + 1, :]
            column = jnp.sum(product[:, :128] + product[:, 128:], axis=1, keepdims=True)
            columns = jnp.where(lane == c * CHUNK + k, column, columns)
            total = total + transfer[c * CHUNK + k] * column
        return columns, total

    columns, total = lax.fori_loop(
        0, chunks, moment_chunk, (jnp.zeros((RANK, LEAVES), F32), jnp.zeros((RANK, RANK), F32))
    )
    window[2] = columns.T
    unit = eye()
    cluster_row = jnp.sum(total, axis=0, keepdims=True)
    lifted_row = jnp.sum(cluster_transfer[0] * to_column(cluster_row, unit), axis=0, keepdims=True)
    every[device, 0:1, 0:RANK] = cluster_row
    every[device, 0:1, RANK : 2 * RANK] = lifted_row

    def one_copy(k):
        return pltpu.make_async_remote_copy(
            src_ref=every.at[device],
            dst_ref=every.at[device],
            send_sem=one_send.at[k],
            recv_sem=one_recv.at[k],
            device_id=block_mate(k),
            device_id_type=MESH,
        )

    def two_copy(k):
        rows = pl.ds(block * BLOCK, BLOCK)
        return pltpu.make_async_remote_copy(
            src_ref=every.at[rows],
            dst_ref=every.at[rows],
            send_sem=two_send.at[k],
            recv_sem=two_recv.at[k],
            device_id=far_mate(k),
            device_id_type=MESH,
        )

    @pl.loop(1, BLOCK)
    def _(k):
        one_copy(k).start()

    def moment_copies():
        copies = []
        for n, distance in enumerate((2, 1, -1, -2)):
            slot = (0, 1, 3, 4)[n]
            copies.append(
                pltpu.make_async_remote_copy(
                    src_ref=window.at[2],
                    dst_ref=window.at[slot],
                    send_sem=moment_send.at[n],
                    recv_sem=moment_recv.at[n],
                    device_id=beside(distance),
                    device_id_type=MESH,
                )
            )
        return copies

    moments = moment_copies()
    for copy in moments:
        copy.start()

    @pl.loop(0, chunks)
    def _(c):
        span = pl.ds(pl.multiple_of(c * CHUNK, CHUNK), CHUNK)
        parts, norm = centred([points[n, span, :] for n in range(3)])
        source_out[pl.ds(LEAVES + c * CHUNK, CHUNK)] = by_leaf(source_terms(parts, norm)).astype(BF16)
        target = by_leaf(target_terms(parts, norm))
        for k in range(CHUNK):
            target_out[c * CHUNK + k] = target[k].T.astype(BF16)

    charge_out[LEAVES : 2 * LEAVES] = charges[...]
    charge_out[3 * LEAVES :] = jnp.zeros((8, POINTS), F32)
    term = lax.broadcasted_iota(jnp.int32, (TERMS, POINTS), 0)
    source_out[BLANK] = jnp.where(term == 18, 1.0, 0.0).astype(BF16)

    far_targets = far[...]
    far_out[...] = jnp.where(far_targets >= 0, far_targets - (device - 2) * LEAVES, 5 * LEAVES)

    slots = near[...]
    live = (slots >= 0).astype(F32)
    before = (
        lax.broadcasted_iota(jnp.int32, (LEAVES, LEAVES), 0) < lax.broadcasted_iota(jnp.int32, (LEAVES, LEAVES), 1)
    ).astype(BF16)
    rank_in_slot = jnp.dot(live.astype(BF16), before, preferred_element_type=F32)
    in_slot = jnp.sum(live, axis=1, keepdims=True)
    leaf_row = lax.broadcasted_iota(jnp.int32, (1, LEAVES), 1)
    code = (leaf_row * 256 + slots - (device - 1) * LEAVES).astype(F32)
    position_row = lax.broadcasted_iota(jnp.int32, (1, PAIRS), 1).astype(F32)
    found = jnp.zeros((LEAVES, PAIRS), F32)
    start = jnp.zeros((1, 1), F32)
    positions = []
    for s in range(NEAR):
        positions.append(jnp.where(live[s : s + 1] > 0, rank_in_slot[s : s + 1] + start, -1.0))
        start = start + in_slot[s : s + 1]
    table = jnp.concatenate(positions + [code], axis=0).T
    for s in range(NEAR):
        found = jnp.where(table[:, s : s + 1] == position_row, table[:, NEAR + s : NEAR + s + 1], found)
    pairs = jnp.sum(found, axis=0, keepdims=True)
    pair_out[0:1] = jnp.where(position_row < start, pairs, float(BLANK)).astype(jnp.int32)
    far_live = jnp.sum((far_targets >= 0).astype(F32), axis=0, keepdims=True).astype(jnp.int32)
    pair_out[1:2] = jnp.concatenate(
        [far_live, jnp.broadcast_to(start.astype(jnp.int32), (1, PAIRS - LEAVES))], axis=1
    )

    @pl.loop(1, BLOCK)
    def _(k):
        one_copy(k).wait_recv()

    @pl.loop(1, BLOCKS)
    def _(k):
        two_copy(k).start()

    for side in range(2):
        halo[2 * side].wait_recv()
        halo[2 * side + 1].wait_recv()
        first = 2 * LEAVES * side

        @pl.loop(0, chunks)
        def _(c):
            span = pl.ds(pl.multiple_of(c * CHUNK, CHUNK), CHUNK)
            parts, norm = centred([halo_points[side, n, span, :] for n in range(3)])
            source_out[pl.ds(first + c * CHUNK, CHUNK)] = by_leaf(source_terms(parts, norm)).astype(BF16)

        charge_out[first : first + LEAVES] = halo_charges[side]

    for copy in moments:
        copy.wait_recv()
    for n in range(5):
        moment_out[n * LEAVES : (n + 1) * LEAVES] = window[n]
    moment_out[5 * LEAVES :] = jnp.zeros((8, RANK), F32)

    @pl.loop(1, BLOCKS)
    def _(k):
        two_copy(k).wait_recv()

    every_out[...] = every[...]

    @pl.loop(1, BLOCK)
    def _(k):
        one_copy(k).wait_send()

    @pl.loop(1, BLOCKS)
    def _(k):
        two_copy(k).wait_send()

    for copy in halo + moments:
        copy.wait_send()


def local_kernel(
    pairs, far, cluster_target, group_target, top_target,
    source, target, charges, moments, every,
    cluster_transfer, cluster_coupling, group_coupling,
    bases_hbm, transfer_hbm, group_transfer_hbm, top_coupling_hbm, coupling_hbm,
    out,
    near_total, coupling, bases, transfer, group_transfer, top_coupling, group_moments, top_moments,
    coupling_sems, sems,
):
    gx = lax.axis_index("gx")
    top = gx // 4

    def coupling_copy(i):
        count = pairs[1, i]
        return pltpu.make_async_copy(
            coupling_hbm.at[i, pl.ds(0, count)], coupling.at[i, pl.ds(0, count)], coupling_sems.at[i]
        )

    loads = [
        pltpu.make_async_copy(group_transfer_hbm, group_transfer, sems.at[0]),
        pltpu.make_async_copy(top_coupling_hbm.at[top], top_coupling, sems.at[1]),
        pltpu.make_async_copy(transfer_hbm, transfer, sems.at[2]),
        pltpu.make_async_copy(bases_hbm, bases, sems.at[3]),
    ]
    for copy in loads:
        copy.start()

    @pl.loop(0, LEAVES)
    def _(i):
        @pl.when(pairs[1, i] > 0)
        def _():
            coupling_copy(i).start()

    @pl.loop(0, LEAVES)
    def _(i):
        near_total[i] = jnp.zeros((POINTS, 128), F32)

    @pl.loop(0, (pairs[1, LEAVES] + GROUP - 1) // GROUP)
    def _(g):
        for k in range(GROUP):
            code = pairs[0, g * GROUP + k]
            i, j = code // 256, code % 256
            distance = jnp.dot(target[i], source[j], preferred_element_type=F32)
            weighted = lax.rsqrt(distance) * charges[pl.ds(j, 1), :]
            near_total[i] += weighted[:, :128] + weighted[:, 128:]

    unit = eye()
    for copy in loads:
        copy.wait()

    for g in range(32):
        group_moments[g : g + 1] = (
            every[4 * g, :, RANK:] + every[4 * g + 1, :, RANK:] + every[4 * g + 2, :, RANK:] + every[4 * g + 3, :, RANK:]
        )
    for h in range(8):
        total = jnp.zeros((RANK, RANK), F32)
        for k in range(4):
            g = 4 * h + k
            total = total + group_transfer[g] * to_column(group_moments[g : g + 1], unit)
        top_moments[h : h + 1] = jnp.sum(total, axis=0, keepdims=True)

    def masked(t):
        return jnp.where(t >= 0, 1.0, 0.0).astype(F32), jnp.maximum(t, 0)

    total = jnp.zeros((RANK, RANK), F32)
    for f in range(4):
        weight, t = masked(top_target[top, f])
        total = total + top_coupling[f] * (top_moments[pl.ds(t, 1), :] * weight)
    top_local = to_row(jnp.sum(total, axis=1, keepdims=True), unit)
    total = group_transfer[gx] * top_local
    for f in range(8):
        weight, t = masked(group_target[0, f])
        total = total + group_coupling[0, f] * (group_moments[pl.ds(t, 1), :] * weight)
    group_local = to_row(jnp.sum(total, axis=1, keepdims=True), unit)
    total = cluster_transfer[0] * group_local
    for f in range(8):
        weight, t = masked(cluster_target[0, f])
        total = total + cluster_coupling[0, f] * (every[t, :, :RANK] * weight)
    cluster_local = to_row(jnp.sum(total, axis=1, keepdims=True), unit)

    @pl.loop(0, LEAVES // 2)
    def _(step):
        for k in range(2):
            i = step * 2 + k

            @pl.when(pairs[1, i] > 0)
            def _():
                coupling_copy(i).wait()

            total = transfer[i] * cluster_local
            total = lax.fori_loop(
                0, pairs[1, i], lambda f, total: total + coupling[i, f] * moments[pl.ds(far[f, i], 1), :], total
            )
            leaf_local = jnp.sum(total, axis=1, keepdims=True)
            far_part = jnp.sum(bases[i] * leaf_local, axis=0, keepdims=True)
            near_part = jnp.sum(near_total[i].T, axis=0, keepdims=True)
            out[pl.ds(i, 1), :] = near_part * INVERSE_FOUR_PI + far_part


def local(
    charges, points, leaf_bases, leaf_transfer, near_target, far_target, leaf_coupling, cluster_transfer,
    cluster_target, cluster_coupling, group_transfer, group_target, group_coupling, top_target, top_coupling,
):
    vmem = pl.BlockSpec(memory_space=pltpu.VMEM)
    smem = pl.BlockSpec(memory_space=pltpu.SMEM)
    anywhere = pl.BlockSpec(memory_space=pl.ANY)
    dma = pltpu.SemaphoreType.DMA
    bases = jnp.swapaxes(leaf_bases, 1, 2)
    source, target, all_charges, moments, every, far, pairs = pl.pallas_call(
        exchange_kernel,
        out_shape=(
            jax.ShapeDtypeStruct((3 * LEAVES + 1, TERMS, POINTS), BF16),
            jax.ShapeDtypeStruct((LEAVES, POINTS, TERMS), BF16),
            jax.ShapeDtypeStruct((3 * LEAVES + 8, POINTS), F32),
            jax.ShapeDtypeStruct((5 * LEAVES + 8, RANK), F32),
            jax.ShapeDtypeStruct((DEVICES, 1, 2 * RANK), F32),
            jax.ShapeDtypeStruct((FAR, LEAVES), jnp.int32),
            jax.ShapeDtypeStruct((2, PAIRS), jnp.int32),
        ),
        in_specs=[vmem] * 5 + [anywhere] * 2,
        out_specs=[vmem] * 7,
        scratch_shapes=[
            pltpu.VMEM((LEAVES, RANK, POINTS), F32),
            pltpu.VMEM((LEAVES, RANK, RANK), F32),
            pltpu.VMEM((2, LEAVES, POINTS), F32),
            pltpu.VMEM((2, 3, LEAVES, POINTS), F32),
            pltpu.VMEM((5, LEAVES, RANK), F32),
            pltpu.VMEM((DEVICES, 1, 2 * RANK), F32),
            dma((2, LEAVES // CHUNK)),
            dma((2, 2)),
            dma((2, 2)),
            dma((4,)),
            dma((4,)),
            dma((BLOCK,)),
            dma((BLOCK,)),
            dma((BLOCKS,)),
            dma((BLOCKS,)),
        ],
        compiler_params=pltpu.CompilerParams(
            collective_id=0, has_side_effects=True, vmem_limit_bytes=48 << 20
        ),
        name="exchange",
    )(
        charges,
        jnp.transpose(points, (1, 0, 2)),
        near_target.T,
        far_target.T,
        cluster_transfer,
        bases,
        leaf_transfer,
    )
    return pl.pallas_call(
        local_kernel,
        out_shape=jax.ShapeDtypeStruct((LEAVES, POINTS), F32),
        in_specs=[smem] * 5 + [vmem] * 8 + [anywhere] * 5,
        out_specs=vmem,
        scratch_shapes=[
            pltpu.VMEM((LEAVES, POINTS, 128), F32),
            pltpu.VMEM((LEAVES, FAR, RANK, RANK), F32),
            pltpu.VMEM((LEAVES, RANK, POINTS), F32),
            pltpu.VMEM((LEAVES, RANK, RANK), F32),
            pltpu.VMEM((32, RANK, RANK), F32),
            pltpu.VMEM((4, RANK, RANK), F32),
            pltpu.VMEM((32, RANK), F32),
            pltpu.VMEM((8, RANK), F32),
            dma((LEAVES,)),
            dma((4,)),
        ],
        compiler_params=pltpu.CompilerParams(vmem_limit_bytes=62 << 20),
        name="local",
    )(
        pairs, far, cluster_target, group_target, top_target,
        source, target, all_charges, moments, every,
        cluster_transfer, cluster_coupling, group_coupling,
        bases, leaf_transfer, group_transfer, top_coupling, leaf_coupling,
    )


def solution(mesh):
    leaf = ("gx", "gy")
    return jax.shard_map(
        local,
        mesh=mesh,
        in_specs=(
            P(leaf, None),
            P(leaf, None, None),
            P(leaf, None, None),
            P(leaf, None, None),
            P(leaf, None),
            P(leaf, None),
            P(leaf, None, None, None),
            P(leaf, None, None),
            P(leaf, None),
            P(leaf, None, None, None),
            P(),
            P("gx", None),
            P("gx", None, None, None),
            P(),
            P(),
        ),
        out_specs=P(leaf, None),
        check_vma=False,
    )
```

```python
import functools
import math

import jax
import jax.numpy as jnp
from jax import lax
from jax.experimental import pallas as pl
from jax.experimental.pallas import tpu as pltpu
from jax.sharding import PartitionSpec as P

MESH = pl.DeviceIdType.MESH
F32 = jnp.float32
BF16 = jnp.bfloat16
SMOOTHING = 0.01
INVERSE_FOUR_PI = 1.0 / (4.0 * math.pi)

LEAVES = 64
POINTS = 256
RANK = 64
NEAR = 8
FAR = 16
TERMS = 32
PAIRS = LEAVES * NEAR
GROUP = 8
CHUNK = 8
FAR_LEAVES = 2
DEVICES = 128
BLOCK = 8
BLOCKS = DEVICES // BLOCK
BLANK = 3 * LEAVES


def split3(value):
    high = value.astype(BF16).astype(F32)
    rest = value - high
    middle = rest.astype(BF16).astype(F32)
    low = (rest - middle).astype(BF16).astype(F32)
    return high, middle, low


def centred(points):
    shifted = [p - 1.0 for p in points]
    norm = shifted[0] * shifted[0] + shifted[1] * shifted[1] + shifted[2] * shifted[2]
    return [split3(u) for u in shifted], norm


def source_terms(parts, norm):
    rows = []
    for high, middle, low in parts:
        high, middle, low = -2.0 * high, -2.0 * middle, -2.0 * low
        rows += [high, high, high, middle, middle, low]
    one = jnp.ones_like(norm)
    return rows + list(split3(norm + SMOOTHING)) + [one, one, one]


def target_terms(parts, norm):
    rows = []
    for high, middle, low in parts:
        rows += [high, middle, low, high, middle, high]
    one = jnp.ones_like(norm)
    return rows + [one, one, one] + list(split3(norm))


def by_leaf(rows):
    blank = jnp.zeros_like(rows[0])
    return jnp.swapaxes(jnp.stack(rows + [blank] * (TERMS - len(rows)), axis=0), 0, 1)


def eye():
    shape = (RANK, RANK)
    return (lax.broadcasted_iota(jnp.int32, shape, 0) == lax.broadcasted_iota(jnp.int32, shape, 1)).astype(F32)


def to_column(row, unit):
    return jnp.sum(unit * row, axis=1, keepdims=True)


def to_row(column, unit):
    return jnp.sum(unit * column, axis=0, keepdims=True)


def exchange_kernel(
    charges_hbm, points_hbm, near_hbm, far_hbm, cluster_transfer_hbm, bases_hbm, transfer_hbm,
    source_out, target_out, charge_out, moment_out, every_out, far_out, pair_out, bases, transfer,
    charges, points, near, far, cluster_transfer, halo_charges, halo_points, window, every,
    load_sems, small_sems, halo_send, halo_recv, moment_send, moment_recv, one_send, one_recv, two_send, two_recv,
):
    gx, gy = lax.axis_index("gx"), lax.axis_index("gy")
    device = gx * 4 + gy

    def place(index):
        return (index // 4, index % 4)

    def beside(distance):
        return place((device + distance + DEVICES) % DEVICES)

    place_in_block = device % BLOCK
    block = device // BLOCK
    chunks = LEAVES // CHUNK

    def load_copies(c):
        span = pl.ds(c * CHUNK, CHUNK)
        return (
            pltpu.make_async_copy(bases_hbm.at[span], bases.at[span], load_sems.at[0, c]),
            pltpu.make_async_copy(transfer_hbm.at[span], transfer.at[span], load_sems.at[1, c]),
        )

    small = [
        pltpu.make_async_copy(source, landing, small_sems.at[n])
        for n, (source, landing) in enumerate(
            (
                (charges_hbm, charges),
                (points_hbm, points),
                (near_hbm, near),
                (far_hbm, far),
                (cluster_transfer_hbm, cluster_transfer),
            )
        )
    ]
    for copy in small:
        copy.start()

    @pl.loop(0, chunks)
    def _(c):
        for copy in load_copies(c):
            copy.start()

    barrier = pltpu.get_barrier_semaphore()
    for distance in (1, -1, 2, -2):
        pl.semaphore_signal(barrier, inc=1, device_id=beside(distance), device_id_type=MESH)

    def block_mate(k):
        return place(block * BLOCK + (place_in_block + k) % BLOCK)

    def far_mate(k):
        return place(((block + k) % BLOCKS) * BLOCK + place_in_block)

    @pl.loop(1, BLOCK)
    def _(k):
        pl.semaphore_signal(barrier, inc=1, device_id=block_mate(k), device_id_type=MESH)

    @pl.loop(1, BLOCKS)
    def _(k):
        pl.semaphore_signal(barrier, inc=1, device_id=far_mate(k), device_id_type=MESH)

    for copy in small:
        copy.wait()
    pl.semaphore_wait(barrier, 4 + BLOCK - 1 + BLOCKS - 1)

    def halo_copies():
        copies = []
        for side, distance in ((0, 1), (1, -1)):
            for kind, (source, landing) in enumerate(((charges, halo_charges), (points, halo_points))):
                copies.append(
                    pltpu.make_async_remote_copy(
                        src_ref=source,
                        dst_ref=landing.at[side],
                        send_sem=halo_send.at[side, kind],
                        recv_sem=halo_recv.at[side, kind],
                        device_id=beside(distance),
                        device_id_type=MESH,
                    )
                )
        return copies

    halo = halo_copies()
    for copy in halo:
        copy.start()

    lane = lax.broadcasted_iota(jnp.int32, (RANK, LEAVES), 1)

    def moment_chunk(c, carry):
        columns, total = carry
        for copy in load_copies(c):
            copy.wait()
        weights = charges[pl.ds(pl.multiple_of(c * CHUNK, CHUNK), CHUNK), :]
        for k in range(CHUNK):
            product = bases[c * CHUNK + k] * weights[k : k + 1, :]
            column = jnp.sum(product[:, :128] + product[:, 128:], axis=1, keepdims=True)
            columns = jnp.where(lane == c * CHUNK + k, column, columns)
            total = total + transfer[c * CHUNK + k] * column
        return columns, total

    columns, total = lax.fori_loop(
        0, chunks, moment_chunk, (jnp.zeros((RANK, LEAVES), F32), jnp.zeros((RANK, RANK), F32))
    )
    window[2] = columns.T
    unit = eye()
    cluster_row = jnp.sum(total, axis=0, keepdims=True)
    lifted_row = jnp.sum(cluster_transfer[0] * to_column(cluster_row, unit), axis=0, keepdims=True)
    every[device, 0:1, 0:RANK] = cluster_row
    every[device, 0:1, RANK : 2 * RANK] = lifted_row

    def one_copy(k):
        return pltpu.make_async_remote_copy(
            src_ref=every.at[device],
            dst_ref=every.at[device],
            send_sem=one_send.at[k],
            recv_sem=one_recv.at[k],
            device_id=block_mate(k),
            device_id_type=MESH,
        )

    def two_copy(k):
        rows = pl.ds(block * BLOCK, BLOCK)
        return pltpu.make_async_remote_copy(
            src_ref=every.at[rows],
            dst_ref=every.at[rows],
            send_sem=two_send.at[k],
            recv_sem=two_recv.at[k],
            device_id=far_mate(k),
            device_id_type=MESH,
        )

    @pl.loop(1, BLOCK)
    def _(k):
        one_copy(k).start()

    def moment_copies():
        copies = []
        for n, distance in enumerate((2, 1, -1, -2)):
            slot = (0, 1, 3, 4)[n]
            copies.append(
                pltpu.make_async_remote_copy(
                    src_ref=window.at[2],
                    dst_ref=window.at[slot],
                    send_sem=moment_send.at[n],
                    recv_sem=moment_recv.at[n],
                    device_id=beside(distance),
                    device_id_type=MESH,
                )
            )
        return copies

    moments = moment_copies()
    for copy in moments:
        copy.start()

    @pl.loop(0, chunks)
    def _(c):
        span = pl.ds(pl.multiple_of(c * CHUNK, CHUNK), CHUNK)
        parts, norm = centred([points[n, span, :] for n in range(3)])
        source_out[pl.ds(LEAVES + c * CHUNK, CHUNK)] = by_leaf(source_terms(parts, norm)).astype(BF16)
        target = by_leaf(target_terms(parts, norm))
        for k in range(CHUNK):
            target_out[c * CHUNK + k] = target[k].T.astype(BF16)

    charge_out[LEAVES : 2 * LEAVES] = charges[...]
    charge_out[3 * LEAVES :] = jnp.zeros((8, POINTS), F32)
    term = lax.broadcasted_iota(jnp.int32, (TERMS, POINTS), 0)
    source_out[BLANK] = jnp.where(term == 18, 1.0, 0.0).astype(BF16)

    far_targets = far[...]
    far_out[...] = jnp.where(far_targets >= 0, far_targets - (device - 2) * LEAVES, 5 * LEAVES)

    slots = near[...]
    live = (slots >= 0).astype(F32)
    before = (
        lax.broadcasted_iota(jnp.int32, (LEAVES, LEAVES), 0) < lax.broadcasted_iota(jnp.int32, (LEAVES, LEAVES), 1)
    ).astype(BF16)
    rank_in_slot = jnp.dot(live.astype(BF16), before, preferred_element_type=F32)
    in_slot = jnp.sum(live, axis=1, keepdims=True)
    leaf_row = lax.broadcasted_iota(jnp.int32, (1, LEAVES), 1)
    code = (leaf_row * 256 + slots - (device - 1) * LEAVES).astype(F32)
    position_row = lax.broadcasted_iota(jnp.int32, (1, PAIRS), 1).astype(F32)
    found = jnp.zeros((LEAVES, PAIRS), F32)
    start = jnp.zeros((1, 1), F32)
    positions = []
    for s in range(NEAR):
        positions.append(jnp.where(live[s : s + 1] > 0, rank_in_slot[s : s + 1] + start, -1.0))
        start = start + in_slot[s : s + 1]
    table = jnp.concatenate(positions + [code], axis=0).T
    for s in range(NEAR):
        found = jnp.where(table[:, s : s + 1] == position_row, table[:, NEAR + s : NEAR + s + 1], found)
    pairs = jnp.sum(found, axis=0, keepdims=True)
    pair_out[0:1, 0:PAIRS] = jnp.where(position_row < start, pairs, float(BLANK)).astype(jnp.int32)
    pair_out[0:1, PAIRS:] = jnp.full((1, 128), BLANK, jnp.int32)
    far_live = jnp.sum((far_targets >= 0).astype(F32), axis=0, keepdims=True).astype(jnp.int32)
    pair_out[1:2, 0:PAIRS] = jnp.concatenate(
        [far_live, jnp.broadcast_to(start.astype(jnp.int32), (1, PAIRS - LEAVES))], axis=1
    )

    @pl.loop(1, BLOCK)
    def _(k):
        one_copy(k).wait_recv()

    @pl.loop(1, BLOCKS)
    def _(k):
        two_copy(k).start()

    for side in range(2):
        halo[2 * side].wait_recv()
        halo[2 * side + 1].wait_recv()
        first = 2 * LEAVES * side

        @pl.loop(0, chunks)
        def _(c):
            span = pl.ds(pl.multiple_of(c * CHUNK, CHUNK), CHUNK)
            parts, norm = centred([halo_points[side, n, span, :] for n in range(3)])
            source_out[pl.ds(first + c * CHUNK, CHUNK)] = by_leaf(source_terms(parts, norm)).astype(BF16)

        charge_out[first : first + LEAVES] = halo_charges[side]

    for copy in moments:
        copy.wait_recv()
    for n in range(5):
        moment_out[n * LEAVES : (n + 1) * LEAVES] = window[n]
    moment_out[5 * LEAVES :] = jnp.zeros((8, RANK), F32)

    @pl.loop(1, BLOCKS)
    def _(k):
        two_copy(k).wait_recv()

    every_out[...] = every[...]

    @pl.loop(1, BLOCK)
    def _(k):
        one_copy(k).wait_send()

    @pl.loop(1, BLOCKS)
    def _(k):
        two_copy(k).wait_send()

    for copy in halo + moments:
        copy.wait_send()


def local_kernel(
    source, target, charges, moments, every, far_vmem, pairs_vmem, bases, transfer,
    cluster_target_hbm, group_target_hbm, top_target_hbm, cluster_transfer_hbm, cluster_coupling_hbm,
    group_coupling_hbm, group_transfer_hbm, top_coupling_hbm, coupling_hbm,
    out,
    near_total, ahead, coupling, cluster_transfer, cluster_coupling, group_coupling, group_transfer, top_coupling,
    group_moments, top_moments, pairs, far, cluster_target, group_target, top_target,
    coupling_sems, sems,
):
    gx = lax.axis_index("gx")
    top = gx // 4

    loads = [
        pltpu.make_async_copy(source_ref, landing, sems.at[n])
        for n, (source_ref, landing) in enumerate(
            (
                (pairs_vmem, pairs),
                (far_vmem, far),
                (cluster_target_hbm, cluster_target),
                (group_target_hbm, group_target),
                (top_target_hbm, top_target),
                (cluster_transfer_hbm, cluster_transfer),
                (cluster_coupling_hbm, cluster_coupling),
                (group_coupling_hbm, group_coupling),
                (group_transfer_hbm, group_transfer),
                (top_coupling_hbm.at[top], top_coupling),
            )
        )
    ]
    for copy in loads:
        copy.start()

    @pl.loop(0, LEAVES // 4)
    def _(c):
        for k in range(4):
            near_total[c * 4 + k] = jnp.zeros((POINTS, 128), F32)

    coupling[LEAVES * FAR] = jnp.zeros((RANK, RANK), F32)
    for copy in loads[:2]:
        copy.wait()

    def coupling_copy(i):
        count = jnp.maximum(pairs[1, i], 1)
        return pltpu.make_async_copy(
            coupling_hbm.at[pl.ds(i * FAR, count)], coupling.at[pl.ds(i * FAR, count)], coupling_sems.at[i]
        )

    @pl.loop(0, LEAVES)
    def _(i):
        coupling_copy(i).start()

    def squares(p):
        code = pairs[0, p]
        return jnp.dot(target[code // 256], source[code % 256], preferred_element_type=F32)

    def add_near(p, square):
        code = pairs[0, p]
        weighted = lax.rsqrt(square) * charges[pl.ds(code % 256, 1), :]
        near_total[code // 256] += weighted[:, :128] + weighted[:, 128:]

    def near_group(g):
        add_near(g * GROUP, ahead[...])
        for k in range(1, GROUP):
            add_near(g * GROUP + k, squares(g * GROUP + k))
        ahead[...] = squares(g * GROUP + GROUP)

    def far_leaf(i):
        count = pairs[1, i]
        total = None
        for f in range(FAR):
            index = jnp.where(f < count, i * FAR + f, LEAVES * FAR)
            term = coupling[index] * moments[pl.ds(far[f, i], 1), :]
            total = term if total is None else total + term
        coupling[i * FAR] = total

    ahead[...] = squares(0)
    shared = LEAVES // FAR_LEAVES

    @pl.loop(0, shared)
    def _(g):
        for k in range(FAR_LEAVES):
            coupling_copy(g * FAR_LEAVES + k).wait()
        for k in range(FAR_LEAVES):
            far_leaf(g * FAR_LEAVES + k)
        near_group(g)

    @pl.loop(shared, jnp.maximum((pairs[1, LEAVES] + GROUP - 1) // GROUP, shared))
    def _(g):
        near_group(g)

    unit = eye()
    for copy in loads[2:]:
        copy.wait()

    for g in range(32):
        group_moments[g : g + 1] = (
            every[4 * g, :, RANK:] + every[4 * g + 1, :, RANK:] + every[4 * g + 2, :, RANK:] + every[4 * g + 3, :, RANK:]
        )
    for h in range(8):
        total = jnp.zeros((RANK, RANK), F32)
        for k in range(4):
            g = 4 * h + k
            total = total + group_transfer[g] * to_column(group_moments[g : g + 1], unit)
        top_moments[h : h + 1] = jnp.sum(total, axis=0, keepdims=True)

    def masked(t):
        return jnp.where(t >= 0, 1.0, 0.0).astype(F32), jnp.maximum(t, 0)

    total = jnp.zeros((RANK, RANK), F32)
    for f in range(4):
        weight, t = masked(top_target[f, top])
        total = total + top_coupling[f] * (top_moments[pl.ds(t, 1), :] * weight)
    top_local = to_row(jnp.sum(total, axis=1, keepdims=True), unit)
    total = group_transfer[gx] * top_local
    for f in range(8):
        weight, t = masked(group_target[0, f])
        total = total + group_coupling[0, f] * (group_moments[pl.ds(t, 1), :] * weight)
    group_local = to_row(jnp.sum(total, axis=1, keepdims=True), unit)
    total = cluster_transfer[0] * group_local
    for f in range(8):
        weight, t = masked(cluster_target[0, f])
        total = total + cluster_coupling[0, f] * (every[t, :, :RANK] * weight)
    cluster_local = to_row(jnp.sum(total, axis=1, keepdims=True), unit)

    @pl.loop(0, LEAVES // CHUNK)
    def _(c):
        rows = []
        for k in range(CHUNK):
            i = c * CHUNK + k
            total = transfer[i] * cluster_local + coupling[i * FAR]
            leaf_local = jnp.sum(total, axis=1, keepdims=True)
            far_part = jnp.sum(bases[i] * leaf_local, axis=0, keepdims=True)
            near_part = jnp.sum(near_total[i].T, axis=0, keepdims=True)
            rows.append(near_part * INVERSE_FOUR_PI + far_part)
        out[pl.ds(pl.multiple_of(c * CHUNK, CHUNK), CHUNK), :] = jnp.concatenate(rows, axis=0)


def local(
    charges, points, leaf_bases, leaf_transfer, near_target, far_target, leaf_coupling, cluster_transfer,
    cluster_target, cluster_coupling, group_transfer, group_target, group_coupling, top_target, top_coupling,
):
    vmem = pl.BlockSpec(memory_space=pltpu.VMEM)
    anywhere = pl.BlockSpec(memory_space=pl.ANY)
    dma = pltpu.SemaphoreType.DMA

    def in_hbm(*arrays):
        return [pltpu.with_memory_space_constraint(array, pltpu.HBM) for array in arrays]

    handed = pl.pallas_call(
        exchange_kernel,
        out_shape=(
            pltpu.VMEM((3 * LEAVES + 1, TERMS, POINTS), BF16),
            pltpu.VMEM((LEAVES, POINTS, TERMS), BF16),
            pltpu.VMEM((3 * LEAVES + 8, POINTS), F32),
            pltpu.VMEM((5 * LEAVES + 8, RANK), F32),
            pltpu.VMEM((DEVICES, 1, 2 * RANK), F32),
            pltpu.VMEM((FAR, LEAVES), jnp.int32),
            pltpu.VMEM((2, PAIRS + 128), jnp.int32),
            pltpu.VMEM((LEAVES, RANK, POINTS), F32),
            pltpu.VMEM((LEAVES, RANK, RANK), F32),
        ),
        in_specs=[anywhere] * 7,
        out_specs=[vmem] * 9,
        scratch_shapes=[
            pltpu.VMEM((LEAVES, POINTS), F32),
            pltpu.VMEM((3, LEAVES, POINTS), F32),
            pltpu.VMEM((NEAR, LEAVES), jnp.int32),
            pltpu.VMEM((FAR, LEAVES), jnp.int32),
            pltpu.VMEM((1, RANK, RANK), F32),
            pltpu.VMEM((2, LEAVES, POINTS), F32),
            pltpu.VMEM((2, 3, LEAVES, POINTS), F32),
            pltpu.VMEM((5, LEAVES, RANK), F32),
            pltpu.VMEM((DEVICES, 1, 2 * RANK), F32),
            dma((2, LEAVES // CHUNK)),
            dma((5,)),
            dma((2, 2)),
            dma((2, 2)),
            dma((4,)),
            dma((4,)),
            dma((BLOCK,)),
            dma((BLOCK,)),
            dma((BLOCKS,)),
            dma((BLOCKS,)),
        ],
        compiler_params=pltpu.CompilerParams(
            collective_id=0, has_side_effects=True, vmem_limit_bytes=24 << 20
        ),
        name="exchange",
    )(
        *in_hbm(
            charges,
            jnp.transpose(points, (1, 0, 2)),
            near_target.T,
            far_target.T,
            cluster_transfer,
            jnp.swapaxes(leaf_bases, 1, 2),
            leaf_transfer,
        )
    )
    return pl.pallas_call(
        local_kernel,
        out_shape=jax.ShapeDtypeStruct((LEAVES, POINTS), F32),
        in_specs=[vmem] * 9 + [anywhere] * 9,
        out_specs=vmem,
        scratch_shapes=[
            pltpu.VMEM((LEAVES, POINTS, 128), F32),
            pltpu.VMEM((POINTS, POINTS), F32),
            pltpu.VMEM((LEAVES * FAR + 1, RANK, RANK), F32),
            pltpu.VMEM((1, RANK, RANK), F32),
            pltpu.VMEM((1, 8, RANK, RANK), F32),
            pltpu.VMEM((1, 8, RANK, RANK), F32),
            pltpu.VMEM((32, RANK, RANK), F32),
            pltpu.VMEM((4, RANK, RANK), F32),
            pltpu.VMEM((32, RANK), F32),
            pltpu.VMEM((8, RANK), F32),
            pltpu.SMEM((2, PAIRS + 128), jnp.int32),
            pltpu.SMEM((FAR, LEAVES), jnp.int32),
            pltpu.SMEM((1, 8), jnp.int32),
            pltpu.SMEM((1, 8), jnp.int32),
            pltpu.SMEM((4, 8), jnp.int32),
            dma((LEAVES,)),
            dma((10,)),
        ],
        compiler_params=pltpu.CompilerParams(vmem_limit_bytes=49 << 20),
        name="local",
    )(
        *[pltpu.with_memory_space_constraint(array, pltpu.VMEM) for array in handed],
        *in_hbm(
            cluster_target,
            group_target,
            top_target.T,
            cluster_transfer,
            cluster_coupling,
            group_coupling,
            group_transfer,
            top_coupling,
            leaf_coupling.reshape(LEAVES * FAR, RANK, RANK),
        ),
    )


def solution(mesh):
    leaf = ("gx", "gy")
    return jax.shard_map(
        local,
        mesh=mesh,
        in_specs=(
            P(leaf, None),
            P(leaf, None, None),
            P(leaf, None, None),
            P(leaf, None, None),
            P(leaf, None),
            P(leaf, None),
            P(leaf, None, None, None),
            P(leaf, None, None),
            P(leaf, None),
            P(leaf, None, None, None),
            P(),
            P("gx", None),
            P("gx", None, None, None),
            P(),
            P(),
        ),
        out_specs=P(leaf, None),
        check_vma=False,
    )
```

```python
import functools
import math

import jax
import jax.numpy as jnp
from jax import lax
from jax.experimental import pallas as pl
from jax.experimental.pallas import tpu as pltpu
from jax.sharding import PartitionSpec as P

MESH = pl.DeviceIdType.MESH
F32 = jnp.float32
BF16 = jnp.bfloat16
SMOOTHING = 0.01
INVERSE_FOUR_PI = 1.0 / (4.0 * math.pi)

LEAVES = 64
POINTS = 256
RANK = 64
NEAR = 8
FAR = 16
TERMS = 32
PAIRS = LEAVES * NEAR
GROUP = 16
OWN = 2
CHUNK = 8
RING = 32
FAR_LEAVES = 8
DEVICES = 128
BLOCK = 8
BLOCKS = DEVICES // BLOCK
BLANK = 3 * LEAVES


def split3(value):
    high = value.astype(BF16).astype(F32)
    rest = value - high
    middle = rest.astype(BF16).astype(F32)
    low = (rest - middle).astype(BF16).astype(F32)
    return high, middle, low


def centred(points):
    shifted = [p - 1.0 for p in points]
    norm = shifted[0] * shifted[0] + shifted[1] * shifted[1] + shifted[2] * shifted[2]
    return [split3(u) for u in shifted], norm


def source_terms(parts, norm):
    rows = []
    for high, middle, low in parts:
        high, middle, low = -2.0 * high, -2.0 * middle, -2.0 * low
        rows += [high, high, high, middle, middle, low]
    one = jnp.ones_like(norm)
    return rows + list(split3(norm + SMOOTHING)) + [one, one, one]


def target_terms(parts, norm):
    rows = []
    for high, middle, low in parts:
        rows += [high, middle, low, high, middle, high]
    one = jnp.ones_like(norm)
    return rows + [one, one, one] + list(split3(norm))


def by_leaf(rows):
    blank = jnp.zeros_like(rows[0])
    return jnp.swapaxes(jnp.stack(rows + [blank] * (TERMS - len(rows)), axis=0), 0, 1)


def eye():
    shape = (RANK, RANK)
    return (lax.broadcasted_iota(jnp.int32, shape, 0) == lax.broadcasted_iota(jnp.int32, shape, 1)).astype(F32)


def to_column(row, unit):
    return jnp.sum(unit * row, axis=1, keepdims=True)


def to_row(column, unit):
    return jnp.sum(unit * column, axis=0, keepdims=True)


def near_group(g, pair):
    for k in range(GROUP):
        pair(g * GROUP + k)


def folded(square, charge):
    weighted = lax.rsqrt(square) * charge
    return weighted[:, :128] + weighted[:, 128:]


def exchange_kernel(
    charges_hbm, points_hbm, near_hbm, far_hbm, cluster_transfer_hbm, bases_hbm, transfer_hbm,
    source_out, target_out, charge_out, moment_out, every_out, far_out, pair_out, bases, transfer, near_out,
    choice_vector, choice, charges, points, near, far, cluster_transfer, halo_charges, halo_points, window, every,
    choice_sem, load_sems, small_sems, halo_send, halo_recv, moment_send, moment_recv, one_send, one_recv, two_send, two_recv,
):
    gx, gy = lax.axis_index("gx"), lax.axis_index("gy")
    device = gx * 4 + gy

    def place(index):
        return (index // 4, index % 4)

    def beside(distance):
        return place((device + distance + DEVICES) % DEVICES)

    place_in_block = device % BLOCK
    block = device // BLOCK
    chunks = LEAVES // CHUNK

    def load_copies(c):
        span = pl.ds(c * CHUNK, CHUNK)
        return (
            pltpu.make_async_copy(bases_hbm.at[span], bases.at[span], load_sems.at[0, c]),
            pltpu.make_async_copy(transfer_hbm.at[span], transfer.at[span], load_sems.at[1, c]),
        )

    small = [
        pltpu.make_async_copy(source, landing, small_sems.at[n])
        for n, (source, landing) in enumerate(
            (
                (charges_hbm, charges),
                (points_hbm, points),
                (near_hbm, near),
                (far_hbm, far),
                (cluster_transfer_hbm, cluster_transfer),
            )
        )
    ]
    for copy in small:
        copy.start()

    @pl.loop(0, chunks)
    def _(c):
        for copy in load_copies(c):
            copy.start()

    barrier = pltpu.get_barrier_semaphore()
    for distance in (1, -1, 2, -2):
        pl.semaphore_signal(barrier, inc=1, device_id=beside(distance), device_id_type=MESH)

    def block_mate(k):
        return place(block * BLOCK + (place_in_block + k) % BLOCK)

    def far_mate(k):
        return place(((block + k) % BLOCKS) * BLOCK + place_in_block)

    @pl.loop(1, BLOCK)
    def _(k):
        pl.semaphore_signal(barrier, inc=1, device_id=block_mate(k), device_id_type=MESH)

    @pl.loop(1, BLOCKS)
    def _(k):
        pl.semaphore_signal(barrier, inc=1, device_id=far_mate(k), device_id_type=MESH)

    for copy in small:
        copy.wait()
    far_targets = far[...]
    far_out[...] = jnp.where(far_targets >= 0, far_targets - (device - 2) * LEAVES, 5 * LEAVES)

    slots = near[...]
    local_slots = slots - device * LEAVES
    own = jnp.where((local_slots >= 0) & (local_slots < LEAVES), 1, 0)
    live_rows = []
    own_before = jnp.zeros((1, LEAVES), jnp.int32)
    chosen = [jnp.full((1, LEAVES), BLANK, jnp.int32) for _ in range(OWN)]
    for s in range(NEAR):
        is_own = own[s : s + 1] > 0
        for n in range(OWN):
            chosen[n] = jnp.where(is_own & (own_before == n), local_slots[s : s + 1] + LEAVES, chosen[n])
        left = jnp.where(is_own & (own_before < OWN), 0.0, 1.0)
        live_rows.append(jnp.where(slots[s : s + 1] >= 0, left, 0.0))
        own_before = own_before + own[s : s + 1]
    for n in range(OWN):
        choice_vector[n : n + 1, 0:LEAVES] = chosen[n]
    choice_copy = pltpu.make_async_copy(choice_vector, choice, choice_sem)
    choice_copy.start()
    live = jnp.concatenate(live_rows, axis=0)
    before = (
        lax.broadcasted_iota(jnp.int32, (LEAVES, LEAVES), 0) < lax.broadcasted_iota(jnp.int32, (LEAVES, LEAVES), 1)
    ).astype(BF16)
    rank_in_slot = jnp.dot(live.astype(BF16), before, preferred_element_type=F32)
    in_slot = jnp.sum(live, axis=1, keepdims=True)
    leaf_row = lax.broadcasted_iota(jnp.int32, (1, LEAVES), 1)
    code = (leaf_row * 256 + slots - (device - 1) * LEAVES).astype(F32)
    position_row = lax.broadcasted_iota(jnp.int32, (1, PAIRS), 1).astype(F32)
    found = jnp.zeros((LEAVES, PAIRS), F32)
    start = jnp.zeros((1, 1), F32)
    positions = []
    for s in range(NEAR):
        positions.append(jnp.where(live[s : s + 1] > 0, rank_in_slot[s : s + 1] + start, -1.0))
        start = start + in_slot[s : s + 1]
    table = jnp.concatenate(positions + [code], axis=0).T
    for s in range(NEAR):
        found = jnp.where(table[:, s : s + 1] == position_row, table[:, NEAR + s : NEAR + s + 1], found)
    pairs = jnp.sum(found, axis=0, keepdims=True)
    pair_out[0:1, 0:PAIRS] = jnp.where(position_row < start, pairs, float(BLANK)).astype(jnp.int32)
    pair_out[0:1, PAIRS:] = jnp.full((1, 128), BLANK, jnp.int32)
    far_live = jnp.sum((far_targets >= 0).astype(F32), axis=0, keepdims=True).astype(jnp.int32)
    pair_out[1:2, 0:PAIRS] = jnp.concatenate(
        [far_live, jnp.broadcast_to(start.astype(jnp.int32), (1, PAIRS - LEAVES))], axis=1
    )

    pl.semaphore_wait(barrier, 4 + BLOCK - 1 + BLOCKS - 1)

    def halo_copies():
        copies = []
        for side, distance in ((0, 1), (1, -1)):
            for kind, (source, landing) in enumerate(((charges, halo_charges), (points, halo_points))):
                copies.append(
                    pltpu.make_async_remote_copy(
                        src_ref=source,
                        dst_ref=landing.at[side],
                        send_sem=halo_send.at[side, kind],
                        recv_sem=halo_recv.at[side, kind],
                        device_id=beside(distance),
                        device_id_type=MESH,
                    )
                )
        return copies

    halo = halo_copies()
    for copy in halo:
        copy.start()

    lane = lax.broadcasted_iota(jnp.int32, (RANK, LEAVES), 1)

    def moment_chunk(c, carry):
        columns, total = carry
        for copy in load_copies(c):
            copy.wait()
        weights = charges[pl.ds(pl.multiple_of(c * CHUNK, CHUNK), CHUNK), :]
        for k in range(CHUNK):
            product = bases[c * CHUNK + k] * weights[k : k + 1, :]
            column = jnp.sum(product[:, :128] + product[:, 128:], axis=1, keepdims=True)
            columns = jnp.where(lane == c * CHUNK + k, column, columns)
            total = total + transfer[c * CHUNK + k] * column
        return columns, total

    columns, total = lax.fori_loop(
        0, chunks, moment_chunk, (jnp.zeros((RANK, LEAVES), F32), jnp.zeros((RANK, RANK), F32))
    )
    moment_rows = columns.T
    window[2] = jnp.concatenate([moment_rows[: LEAVES // 2], moment_rows[LEAVES // 2 :]], axis=1)
    unit = eye()
    cluster_row = jnp.sum(total, axis=0, keepdims=True)
    lifted_row = jnp.sum(cluster_transfer[0] * to_column(cluster_row, unit), axis=0, keepdims=True)
    every[device, 0:1, 0:RANK] = cluster_row
    every[device, 0:1, RANK : 2 * RANK] = lifted_row

    def one_copy(k):
        return pltpu.make_async_remote_copy(
            src_ref=every.at[device],
            dst_ref=every.at[device],
            send_sem=one_send.at[k],
            recv_sem=one_recv.at[k],
            device_id=block_mate(k),
            device_id_type=MESH,
        )

    def two_copy(k):
        rows = pl.ds(block * BLOCK, BLOCK)
        return pltpu.make_async_remote_copy(
            src_ref=every.at[rows],
            dst_ref=every.at[rows],
            send_sem=two_send.at[k],
            recv_sem=two_recv.at[k],
            device_id=far_mate(k),
            device_id_type=MESH,
        )

    @pl.loop(1, BLOCK)
    def _(k):
        one_copy(k).start()

    def moment_copies():
        copies = []
        for n, distance in enumerate((2, 1, -1, -2)):
            slot = (0, 1, 3, 4)[n]
            copies.append(
                pltpu.make_async_remote_copy(
                    src_ref=window.at[2],
                    dst_ref=window.at[slot],
                    send_sem=moment_send.at[n],
                    recv_sem=moment_recv.at[n],
                    device_id=beside(distance),
                    device_id_type=MESH,
                )
            )
        return copies

    moments = moment_copies()
    for copy in moments:
        copy.start()

    @pl.loop(0, chunks)
    def _(c):
        span = pl.ds(pl.multiple_of(c * CHUNK, CHUNK), CHUNK)
        parts, norm = centred([points[n, span, :] for n in range(3)])
        source_out[pl.ds(LEAVES + c * CHUNK, CHUNK)] = by_leaf(source_terms(parts, norm)).astype(BF16)
        target = by_leaf(target_terms(parts, norm))
        for k in range(CHUNK):
            target_out[c * CHUNK + k] = target[k].T.astype(BF16)

    charge_out[LEAVES : 2 * LEAVES] = charges[...]
    charge_out[3 * LEAVES :] = jnp.zeros((8, POINTS), F32)
    term = lax.broadcasted_iota(jnp.int32, (TERMS, POINTS), 0)
    source_out[BLANK] = jnp.where(term == 18, 1.0, 0.0).astype(BF16)

    choice_copy.wait()

    def own_pair(n, i):
        j = jnp.clip(choice[n, i], 0, BLANK)
        part = folded(
            jnp.dot(target_out[i], source_out[j], preferred_element_type=F32), charge_out[pl.ds(j, 1), :]
        )
        if n == 0:
            near_out[i] = part
        else:
            near_out[i] += part

    @pl.loop(0, LEAVES // GROUP)
    def _(g):
        near_group(g, functools.partial(own_pair, 0))

    @pl.loop(1, BLOCK)
    def _(k):
        one_copy(k).wait_recv()

    @pl.loop(1, BLOCKS)
    def _(k):
        two_copy(k).start()

    for n in range(1, OWN):

        @pl.loop(0, LEAVES // GROUP)
        def _(g):
            near_group(g, functools.partial(own_pair, n))

    for side in range(2):
        halo[2 * side].wait_recv()
        halo[2 * side + 1].wait_recv()
        first = 2 * LEAVES * side

        @pl.loop(0, chunks)
        def _(c):
            span = pl.ds(pl.multiple_of(c * CHUNK, CHUNK), CHUNK)
            parts, norm = centred([halo_points[side, n, span, :] for n in range(3)])
            source_out[pl.ds(first + c * CHUNK, CHUNK)] = by_leaf(source_terms(parts, norm)).astype(BF16)

        charge_out[first : first + LEAVES] = halo_charges[side]

    for copy in moments:
        copy.wait_recv()
    for n in range(5):
        moment_out[n * LEAVES : n * LEAVES + LEAVES // 2] = window[n][:, :RANK]
        moment_out[n * LEAVES + LEAVES // 2 : (n + 1) * LEAVES] = window[n][:, RANK:]
    moment_out[5 * LEAVES :] = jnp.zeros((8, RANK), F32)

    @pl.loop(1, BLOCKS)
    def _(k):
        two_copy(k).wait_recv()

    every_out[...] = every[...]

    @pl.loop(1, BLOCK)
    def _(k):
        one_copy(k).wait_send()

    @pl.loop(1, BLOCKS)
    def _(k):
        two_copy(k).wait_send()

    for copy in halo + moments:
        copy.wait_send()


def local_kernel(
    source, target, charges, moments, every, far_vmem, pairs_vmem, bases, transfer, near_first,
    cluster_target_hbm, group_target_hbm, top_target_hbm, cluster_transfer_hbm, cluster_coupling_hbm,
    group_coupling_hbm, group_transfer_hbm, top_coupling_hbm, coupling_hbm,
    out,
    near_total, parts, coupling, far_total, cluster_transfer, cluster_coupling, group_coupling, group_transfer, top_coupling,
    group_moments, top_moments, pairs, far, cluster_target, group_target, top_target,
    coupling_sems, sems,
):
    gx = lax.axis_index("gx")
    top = gx // 4

    loads = [
        pltpu.make_async_copy(source_ref, landing, sems.at[n])
        for n, (source_ref, landing) in enumerate(
            (
                (pairs_vmem, pairs),
                (far_vmem, far),
                (cluster_target_hbm, cluster_target),
                (group_target_hbm, group_target),
                (top_target_hbm, top_target),
                (cluster_transfer_hbm, cluster_transfer),
                (cluster_coupling_hbm, cluster_coupling),
                (group_coupling_hbm, group_coupling),
                (group_transfer_hbm, group_transfer),
                (top_coupling_hbm.at[top], top_coupling),
            )
        )
    ]
    for copy in loads:
        copy.start()

    @pl.loop(0, LEAVES // 4)
    def _(c):
        for k in range(4):
            near_total[c * 4 + k] = near_first[c * 4 + k]

    for k in range(GROUP):
        parts[k] = jnp.zeros((POINTS, 128), F32)

    coupling[RING * FAR] = jnp.zeros((RANK, RANK), F32)
    for copy in loads[:2]:
        copy.wait()

    def coupling_copy(i):
        count = jnp.maximum(pairs[1, i], 1)
        return pltpu.make_async_copy(
            coupling_hbm.at[pl.ds(i * FAR, count)],
            coupling.at[pl.ds((i % RING) * FAR, count)],
            coupling_sems.at[i % RING],
        )

    @pl.loop(0, RING)
    def _(i):
        coupling_copy(i).start()

    def add_parts(g):
        for k in range(GROUP):
            near_total[pairs[0, g * GROUP + k] // 256] += parts[k]

    def listed_group(g, beside):
        add_parts(jnp.maximum(g - 1, 0))
        for k in range(GROUP):
            code = pairs[0, g * GROUP + k]
            i, j = code // 256, code % 256
            square = jnp.dot(target[i], source[j], preferred_element_type=F32)
            parts[k] = folded(square, charges[pl.ds(j, 1), :])
            beside(k)

    def far_leaf(i):
        count = pairs[1, i]
        total = None
        for f in range(FAR):
            index = jnp.where(f < count, (i % RING) * FAR + f, RING * FAR)
            term = coupling[index] * moments[pl.ds(far[f, i], 1), :]
            total = term if total is None else total + term
        far_total[i] = total

    shared = LEAVES // FAR_LEAVES

    def far_step(g):
        for k in range(FAR_LEAVES):
            coupling_copy(g * FAR_LEAVES + k).wait()

        def beside(k):
            if k % (GROUP // FAR_LEAVES) == 0:
                far_leaf(g * FAR_LEAVES + k // (GROUP // FAR_LEAVES))

        listed_group(g, beside)

    refilled = shared - RING // FAR_LEAVES

    @pl.loop(0, refilled)
    def _(g):
        far_step(g)
        for k in range(FAR_LEAVES):
            coupling_copy(g * FAR_LEAVES + k + RING).start()

    @pl.loop(refilled, shared)
    def _(g):
        far_step(g)

    groups = jnp.maximum((pairs[1, LEAVES] + GROUP - 1) // GROUP, shared + 1)

    @pl.loop(shared, groups - 1)
    def _(g):
        listed_group(g, lambda k: None)

    unit = eye()
    for copy in loads[2:]:
        copy.wait()

    for g in range(32):
        group_moments[g : g + 1] = (
            every[4 * g, :, RANK:] + every[4 * g + 1, :, RANK:] + every[4 * g + 2, :, RANK:] + every[4 * g + 3, :, RANK:]
        )
    for h in range(8):
        total = jnp.zeros((RANK, RANK), F32)
        for k in range(4):
            g = 4 * h + k
            total = total + group_transfer[g] * to_column(group_moments[g : g + 1], unit)
        top_moments[h : h + 1] = jnp.sum(total, axis=0, keepdims=True)

    def masked(t):
        return jnp.where(t >= 0, 1.0, 0.0).astype(F32), jnp.maximum(t, 0)

    total = jnp.zeros((RANK, RANK), F32)
    for f in range(4):
        weight, t = masked(top_target[f, top])
        total = total + top_coupling[f] * (top_moments[pl.ds(t, 1), :] * weight)
    top_local = to_row(jnp.sum(total, axis=1, keepdims=True), unit)
    total = group_transfer[gx] * top_local
    for f in range(8):
        weight, t = masked(group_target[0, f])
        total = total + group_coupling[0, f] * (group_moments[pl.ds(t, 1), :] * weight)
    group_local = to_row(jnp.sum(total, axis=1, keepdims=True), unit)
    total = cluster_transfer[0] * group_local
    for f in range(8):
        weight, t = masked(cluster_target[0, f])
        total = total + cluster_coupling[0, f] * (every[t, :, :RANK] * weight)
    cluster_local = to_row(jnp.sum(total, axis=1, keepdims=True), unit)

    listed_group(groups - 1, lambda k: None)
    add_parts(groups - 1)

    lane = lax.broadcasted_iota(jnp.int32, (POINTS, 128), 1)

    def merged(first, second, distance):
        here = (lane & distance) == 0
        return jnp.where(here, first, second) + pltpu.roll(jnp.where(here, second, first), 128 - distance, axis=1)

    @pl.loop(0, LEAVES // CHUNK)
    def _(c):
        rows = []
        for k in range(CHUNK):
            i = c * CHUNK + k
            total = transfer[i] * cluster_local + far_total[i]
            leaf_local = jnp.sum(total, axis=1, keepdims=True)
            rows.append(jnp.sum(bases[i] * leaf_local, axis=0, keepdims=True))
        totals = [near_total[c * CHUNK + k] for k in range(CHUNK)]
        for distance in (1, 2, 4):
            totals = [merged(totals[n], totals[n + 1], distance) for n in range(0, len(totals), 2)]
        near_part = jnp.sum(totals[0].T.reshape(128 // CHUNK, CHUNK, POINTS), axis=0)
        out[pl.ds(pl.multiple_of(c * CHUNK, CHUNK), CHUNK), :] = near_part * INVERSE_FOUR_PI + jnp.concatenate(
            rows, axis=0
        )


def local(
    charges, points, leaf_bases, leaf_transfer, near_target, far_target, leaf_coupling, cluster_transfer,
    cluster_target, cluster_coupling, group_transfer, group_target, group_coupling, top_target, top_coupling,
):
    vmem = pl.BlockSpec(memory_space=pltpu.VMEM)
    anywhere = pl.BlockSpec(memory_space=pl.ANY)
    dma = pltpu.SemaphoreType.DMA

    def in_hbm(*arrays):
        return [pltpu.with_memory_space_constraint(array, pltpu.HBM) for array in arrays]

    handed = pl.pallas_call(
        exchange_kernel,
        out_shape=(
            pltpu.VMEM((3 * LEAVES + 1, TERMS, POINTS), BF16),
            pltpu.VMEM((LEAVES, POINTS, TERMS), BF16),
            pltpu.VMEM((3 * LEAVES + 8, POINTS), F32),
            pltpu.VMEM((5 * LEAVES + 8, RANK), F32),
            pltpu.VMEM((DEVICES, 1, 2 * RANK), F32),
            pltpu.VMEM((FAR, LEAVES), jnp.int32),
            pltpu.VMEM((2, PAIRS + 128), jnp.int32),
            pltpu.VMEM((LEAVES, RANK, POINTS), F32),
            pltpu.VMEM((LEAVES, RANK, RANK), F32),
            pltpu.VMEM((LEAVES, POINTS, 128), F32),
        ),
        in_specs=[anywhere] * 7,
        out_specs=[vmem] * 10,
        scratch_shapes=[
            pltpu.VMEM((8, 128), jnp.int32),
            pltpu.SMEM((8, 128), jnp.int32),
            pltpu.VMEM((LEAVES, POINTS), F32),
            pltpu.VMEM((3, LEAVES, POINTS), F32),
            pltpu.VMEM((NEAR, LEAVES), jnp.int32),
            pltpu.VMEM((FAR, LEAVES), jnp.int32),
            pltpu.VMEM((1, RANK, RANK), F32),
            pltpu.VMEM((2, LEAVES, POINTS), F32),
            pltpu.VMEM((2, 3, LEAVES, POINTS), F32),
            pltpu.VMEM((5, LEAVES // 2, 2 * RANK), F32),
            pltpu.VMEM((DEVICES, 1, 2 * RANK), F32),
            dma,
            dma((2, LEAVES // CHUNK)),
            dma((5,)),
            dma((2, 2)),
            dma((2, 2)),
            dma((4,)),
            dma((4,)),
            dma((BLOCK,)),
            dma((BLOCK,)),
            dma((BLOCKS,)),
            dma((BLOCKS,)),
        ],
        compiler_params=pltpu.CompilerParams(
            collective_id=0, has_side_effects=True, vmem_limit_bytes=32 << 20
        ),
        name="exchange",
    )(
        *in_hbm(
            charges,
            jnp.transpose(points, (1, 0, 2)),
            near_target.T,
            far_target.T,
            cluster_transfer,
            jnp.swapaxes(leaf_bases, 1, 2),
            leaf_transfer,
        )
    )
    return pl.pallas_call(
        local_kernel,
        out_shape=jax.ShapeDtypeStruct((LEAVES, POINTS), F32),
        in_specs=[vmem] * 10 + [anywhere] * 9,
        out_specs=vmem,
        scratch_shapes=[
            pltpu.VMEM((LEAVES, POINTS, 128), F32),
            pltpu.VMEM((GROUP, POINTS, 128), F32),
            pltpu.VMEM((RING * FAR + 1, RANK, RANK), F32),
            pltpu.VMEM((LEAVES, RANK, RANK), F32),
            pltpu.VMEM((1, RANK, RANK), F32),
            pltpu.VMEM((1, 8, RANK, RANK), F32),
            pltpu.VMEM((1, 8, RANK, RANK), F32),
            pltpu.VMEM((32, RANK, RANK), F32),
            pltpu.VMEM((4, RANK, RANK), F32),
            pltpu.VMEM((32, RANK), F32),
            pltpu.VMEM((8, RANK), F32),
            pltpu.SMEM((2, PAIRS + 128), jnp.int32),
            pltpu.SMEM((FAR, LEAVES), jnp.int32),
            pltpu.SMEM((1, 8), jnp.int32),
            pltpu.SMEM((1, 8), jnp.int32),
            pltpu.SMEM((4, 8), jnp.int32),
            dma((RING,)),
            dma((10,)),
        ],
        compiler_params=pltpu.CompilerParams(vmem_limit_bytes=36 << 20),
        name="local",
    )(
        *[pltpu.with_memory_space_constraint(array, pltpu.VMEM) for array in handed],
        *in_hbm(
            cluster_target,
            group_target,
            top_target.T,
            cluster_transfer,
            cluster_coupling,
            group_coupling,
            group_transfer,
            top_coupling,
            leaf_coupling.reshape(LEAVES * FAR, RANK, RANK),
        ),
    )


def solution(mesh):
    leaf = ("gx", "gy")
    return jax.shard_map(
        local,
        mesh=mesh,
        in_specs=(
            P(leaf, None),
            P(leaf, None, None),
            P(leaf, None, None),
            P(leaf, None, None),
            P(leaf, None),
            P(leaf, None),
            P(leaf, None, None, None),
            P(leaf, None, None),
            P(leaf, None),
            P(leaf, None, None, None),
            P(),
            P("gx", None),
            P("gx", None, None, None),
            P(),
            P(),
        ),
        out_specs=P(leaf, None),
        check_vma=False,
    )
```

```python
import functools
import math

import jax
import jax.numpy as jnp
from jax import lax
from jax.experimental import pallas as pl
from jax.experimental.pallas import tpu as pltpu
from jax.sharding import PartitionSpec as P

MESH = pl.DeviceIdType.MESH
F32 = jnp.float32
BF16 = jnp.bfloat16
SMOOTHING = 0.01
INVERSE_FOUR_PI = 1.0 / (4.0 * math.pi)

LEAVES = 64
POINTS = 256
RANK = 64
NEAR = 8
FAR = 16
TERMS = 32
PAIRS = LEAVES * NEAR
GROUP = 16
OWN = 1
CHUNK = 8
DEVICES = 128
STAGES = ((1, 4), (4, 4), (16, 8))
HALO_PARTS = 2
BLANK = 3 * LEAVES


def split3(value):
    high = value.astype(BF16).astype(F32)
    rest = value - high
    middle = rest.astype(BF16).astype(F32)
    low = (rest - middle).astype(BF16).astype(F32)
    return high, middle, low


def centred(points):
    shifted = [p - 1.0 for p in points]
    norm = shifted[0] * shifted[0] + shifted[1] * shifted[1] + shifted[2] * shifted[2]
    return [split3(u) for u in shifted], norm


def source_terms(parts, norm):
    rows = []
    for high, middle, low in parts:
        high, middle, low = -2.0 * high, -2.0 * middle, -2.0 * low
        rows += [high, high, high, middle, middle, low]
    one = jnp.ones_like(norm)
    return rows + list(split3(norm + SMOOTHING)) + [one, one, one]


def target_terms(parts, norm):
    rows = []
    for high, middle, low in parts:
        rows += [high, middle, low, high, middle, high]
    one = jnp.ones_like(norm)
    return rows + [one, one, one] + list(split3(norm))


def by_leaf(rows):
    blank = jnp.zeros_like(rows[0])
    return jnp.swapaxes(jnp.stack(rows + [blank] * (TERMS - len(rows)), axis=0), 0, 1)


def eye():
    shape = (RANK, RANK)
    return (lax.broadcasted_iota(jnp.int32, shape, 0) == lax.broadcasted_iota(jnp.int32, shape, 1)).astype(F32)


def to_column(row, unit):
    return jnp.sum(unit * row, axis=1, keepdims=True)


def to_row(column, unit):
    return jnp.sum(unit * column, axis=0, keepdims=True)


def merged(first, second, distance):
    lane = lax.broadcasted_iota(jnp.int32, first.shape, 1)
    here = (lane & distance) == 0
    return jnp.where(here, first, second) + pltpu.roll(jnp.where(here, second, first), 128 - distance, axis=1)


def lane_sums(parts):
    parts = [parts[k] for k in range(CHUNK)]
    for distance in (1, 2, 4):
        parts = [merged(parts[n], parts[n + 1], distance) for n in range(0, len(parts), 2)]
    return jnp.sum(parts[0].T.reshape(128 // CHUNK, CHUNK, POINTS), axis=0)


def folded(square, charge):
    weighted = lax.rsqrt(square) * charge
    return weighted[:, :128] + weighted[:, 128:]


def exchange_kernel(
    charges_hbm, points_hbm, near_hbm, far_hbm, cluster_transfer_hbm, bases_hbm, transfer_hbm, coupling_hbm,
    source_out, target_out, charge_out, every_out, pair_out, bases, transfer, near_out, far_out,
    coupling, far_vector, far_rows, moment_rows, choice_vector, choice, own, near, far, cluster_transfer, halo, window, every,
    coupling_sems, far_sem, choice_sem, load_sems, small_sems, halo_send, halo_recv, moment_send, moment_recv, every_send, every_recv,
):
    gx, gy = lax.axis_index("gx"), lax.axis_index("gy")
    device = gx * 4 + gy

    def place(index):
        return (index // 4, index % 4)

    def beside(distance):
        return place((device + distance + DEVICES) % DEVICES)

    chunks = LEAVES // CHUNK

    def load_copies(c):
        span = pl.ds(c * CHUNK, CHUNK)
        return (
            pltpu.make_async_copy(bases_hbm.at[span], bases.at[span], load_sems.at[0, c]),
            pltpu.make_async_copy(transfer_hbm.at[span], transfer.at[span], load_sems.at[1, c]),
        )

    small = [
        pltpu.make_async_copy(source, landing, small_sems.at[n])
        for n, (source, landing) in enumerate(
            (
                (charges_hbm, own.at[0]),
                (points_hbm, own.at[pl.ds(1, 3)]),
                (near_hbm, near),
                (far_hbm, far),
                (cluster_transfer_hbm, cluster_transfer),
            )
        )
    ]
    for copy in small:
        copy.start()

    @pl.loop(0, chunks)
    def _(c):
        for copy in load_copies(c):
            copy.start()

    def coupling_copy(c):
        span = pl.ds(c * CHUNK * FAR, CHUNK * FAR)
        return pltpu.make_async_copy(coupling_hbm.at[span], coupling.at[span], coupling_sems.at[c])

    @pl.loop(0, chunks)
    def _(c):
        coupling_copy(c).start()

    barrier = pltpu.get_barrier_semaphore()
    for distance in (1, -1, 2, -2):
        pl.semaphore_signal(barrier, inc=1, device_id=beside(distance), device_id_type=MESH)

    def mate(stage, k):
        unit, count = STAGES[stage]
        position = (device // unit) % count
        return place(device + ((position + k) % count - position) * unit)

    for stage in range(len(STAGES)):

        @pl.loop(1, STAGES[stage][1])
        def _(k):
            pl.semaphore_signal(barrier, inc=1, device_id=mate(stage, k), device_id_type=MESH)

    for copy in small:
        copy.wait()
    far_targets = far[...]
    far_vector[...] = jnp.where(far_targets >= 0, far_targets - (device - 2) * LEAVES, 5 * LEAVES).T
    far_copy = pltpu.make_async_copy(far_vector, far_rows, far_sem)
    far_copy.start()

    slots = near[...]
    local_slots = slots - device * LEAVES
    is_here = jnp.where((local_slots >= 0) & (local_slots < LEAVES), 1, 0)
    live_rows = []
    own_before = jnp.zeros((1, LEAVES), jnp.int32)
    chosen = [jnp.full((1, LEAVES), BLANK, jnp.int32) for _ in range(OWN)]
    for s in range(NEAR):
        is_own = is_here[s : s + 1] > 0
        for n in range(OWN):
            chosen[n] = jnp.where(is_own & (own_before == n), local_slots[s : s + 1] + LEAVES, chosen[n])
        left = jnp.where(is_own & (own_before < OWN), 0.0, 1.0)
        live_rows.append(jnp.where(slots[s : s + 1] >= 0, left, 0.0))
        own_before = own_before + is_here[s : s + 1]
    for n in range(OWN):
        choice_vector[n : n + 1, 0:LEAVES] = chosen[n]
    choice_copy = pltpu.make_async_copy(choice_vector, choice, choice_sem)
    choice_copy.start()
    live = jnp.concatenate(live_rows, axis=0)
    before = (
        lax.broadcasted_iota(jnp.int32, (LEAVES, LEAVES), 0) < lax.broadcasted_iota(jnp.int32, (LEAVES, LEAVES), 1)
    ).astype(BF16)
    rank_in_slot = jnp.dot(live.astype(BF16), before, preferred_element_type=F32)
    in_slot = jnp.sum(live, axis=1, keepdims=True)
    leaf_row = lax.broadcasted_iota(jnp.int32, (1, LEAVES), 1)
    code = (leaf_row * 256 + slots - (device - 1) * LEAVES).astype(F32)
    position_row = lax.broadcasted_iota(jnp.int32, (1, PAIRS), 1).astype(F32)
    found = jnp.zeros((LEAVES, PAIRS), F32)
    start = jnp.zeros((1, 1), F32)
    positions = []
    for s in range(NEAR):
        positions.append(jnp.where(live[s : s + 1] > 0, rank_in_slot[s : s + 1] + start, -1.0))
        start = start + in_slot[s : s + 1]
    table = jnp.concatenate(positions + [code], axis=0).T
    for s in range(NEAR):
        found = jnp.where(table[:, s : s + 1] == position_row, table[:, NEAR + s : NEAR + s + 1], found)
    pairs = jnp.sum(found, axis=0, keepdims=True)
    pair_out[0:1, 0:PAIRS] = jnp.where(position_row < start, pairs, float(BLANK)).astype(jnp.int32)
    pair_out[0:1, PAIRS:] = jnp.full((1, 128), BLANK, jnp.int32)
    pair_out[1:2, 0:128] = jnp.broadcast_to(start.astype(jnp.int32), (1, 128))
    pl.semaphore_wait(barrier, 4 + sum(count - 1 for _, count in STAGES))

    part_leaves = LEAVES // HALO_PARTS
    copies_of_halo = [
        [
            pltpu.make_async_remote_copy(
                src_ref=own.at[:, pl.ds(part * part_leaves, part_leaves)],
                dst_ref=halo.at[side, :, pl.ds(part * part_leaves, part_leaves)],
                send_sem=halo_send.at[part, side],
                recv_sem=halo_recv.at[part, side],
                device_id=beside(distance),
                device_id_type=MESH,
            )
            for side, distance in ((0, 1), (1, -1))
        ]
        for part in range(HALO_PARTS)
    ]
    for copies in copies_of_halo:
        for copy in copies:
            copy.start()

    lane = lax.broadcasted_iota(jnp.int32, (RANK, LEAVES), 1)

    def moment_chunk(c, carry):
        columns, total = carry
        for copy in load_copies(c):
            copy.wait()
        weights = own[0, pl.ds(pl.multiple_of(c * CHUNK, CHUNK), CHUNK), :]
        for k in range(CHUNK):
            product = bases[c * CHUNK + k] * weights[k : k + 1, :]
            column = jnp.sum(product[:, :128] + product[:, 128:], axis=1, keepdims=True)
            columns = jnp.where(lane == c * CHUNK + k, column, columns)
            total = total + transfer[c * CHUNK + k] * column
        return columns, total

    columns, total = lax.fori_loop(
        0, chunks, moment_chunk, (jnp.zeros((RANK, LEAVES), F32), jnp.zeros((RANK, RANK), F32))
    )
    rows = columns.T
    window[2] = jnp.concatenate([rows[: LEAVES // 2], rows[LEAVES // 2 :]], axis=1)
    unit = eye()
    cluster_row = jnp.sum(total, axis=0, keepdims=True)
    lifted_row = jnp.sum(cluster_transfer[0] * to_column(cluster_row, unit), axis=0, keepdims=True)
    every[device, 0:1, 0:RANK] = cluster_row
    every[device, 0:1, RANK : 2 * RANK] = lifted_row

    def every_copy(stage, k):
        unit, _ = STAGES[stage]
        rows = pl.ds((device // unit) * unit, unit)
        return pltpu.make_async_remote_copy(
            src_ref=every.at[rows],
            dst_ref=every.at[rows],
            send_sem=every_send.at[stage, k],
            recv_sem=every_recv.at[stage, k],
            device_id=mate(stage, k),
            device_id_type=MESH,
        )

    def start_stage(stage):
        for k in range(1, STAGES[stage][1]):
            every_copy(stage, k).start()

    def finish_stage(stage):
        for k in range(1, STAGES[stage][1]):
            every_copy(stage, k).wait_recv()

    start_stage(0)

    def moment_copies():
        copies = []
        for n, distance in enumerate((2, 1, -1, -2)):
            slot = (0, 1, 3, 4)[n]
            copies.append(
                pltpu.make_async_remote_copy(
                    src_ref=window.at[2],
                    dst_ref=window.at[slot],
                    send_sem=moment_send.at[n],
                    recv_sem=moment_recv.at[n],
                    device_id=beside(distance),
                    device_id_type=MESH,
                )
            )
        return copies

    moments = moment_copies()
    for copy in moments:
        copy.start()

    @pl.loop(0, chunks)
    def _(c):
        span = pl.ds(pl.multiple_of(c * CHUNK, CHUNK), CHUNK)
        parts, norm = centred([own[n, span, :] for n in range(1, 4)])
        source_out[pl.ds(LEAVES + c * CHUNK, CHUNK)] = by_leaf(source_terms(parts, norm)).astype(BF16)
        target = by_leaf(target_terms(parts, norm))
        for k in range(CHUNK):
            target_out[c * CHUNK + k] = target[k].T.astype(BF16)

    charge_out[LEAVES : 2 * LEAVES] = own[0]
    charge_out[3 * LEAVES :] = jnp.zeros((8, POINTS), F32)
    term = lax.broadcasted_iota(jnp.int32, (TERMS, POINTS), 0)
    source_out[BLANK] = jnp.where(term == 18, 1.0, 0.0).astype(BF16)

    finish_stage(0)
    start_stage(1)

    choice_copy.wait()

    @pl.loop(0, LEAVES // GROUP)
    def _(g):
        for k in range(GROUP):
            i = g * GROUP + k
            for n in range(OWN):
                j = jnp.clip(choice[n, i], 0, BLANK)
                square = jnp.dot(target_out[i], source_out[j], preferred_element_type=F32)
                part = folded(square, charge_out[pl.ds(j, 1), :])
                if n == 0:
                    near_out[i] = part
                else:
                    near_out[i] += part

    finish_stage(1)
    start_stage(2)

    for copy in moments:
        copy.wait_recv()
    for n in range(5):
        moment_rows[n * LEAVES : n * LEAVES + LEAVES // 2] = window[n][:, :RANK]
        moment_rows[n * LEAVES + LEAVES // 2 : (n + 1) * LEAVES] = window[n][:, RANK:]
    moment_rows[5 * LEAVES :] = jnp.zeros((8, RANK), F32)
    far_copy.wait()

    def far_chunk(c):
        coupling_copy(c).wait()
        for k in range(CHUNK):
            i = c * CHUNK + k
            total = None
            for f in range(FAR):
                row = jnp.clip(far_rows[i, f], 0, 5 * LEAVES)
                term = coupling[i * FAR + f] * moment_rows[pl.ds(row, 1), :]
                total = term if total is None else total + term
            far_out[i] = total

    early = chunks * 5 // 8
    pl.loop(0, early)(far_chunk)

    for part in range(HALO_PARTS):
        for side in range(2):
            copies_of_halo[part][side].wait_recv()
            first = 2 * LEAVES * side

            @pl.loop(part * part_leaves // CHUNK, (part + 1) * part_leaves // CHUNK)
            def _(c):
                span = pl.ds(pl.multiple_of(c * CHUNK, CHUNK), CHUNK)
                parts, norm = centred([halo[side, n, span, :] for n in range(1, 4)])
                source_out[pl.ds(first + c * CHUNK, CHUNK)] = by_leaf(source_terms(parts, norm)).astype(BF16)

    charge_out[0:LEAVES] = halo[0, 0]
    charge_out[2 * LEAVES : 3 * LEAVES] = halo[1, 0]

    pl.loop(early, chunks)(far_chunk)

    finish_stage(2)
    every_out[...] = every[...]

    for stage in range(len(STAGES)):
        for k in range(1, STAGES[stage][1]):
            every_copy(stage, k).wait_send()
    for copy in sum(copies_of_halo, []) + moments:
        copy.wait_send()


def local_kernel(
    source, target, charges, every, pairs_vmem, bases, transfer, near_first, far_total,
    cluster_target_hbm, group_target_hbm, top_target_hbm, cluster_transfer_hbm, cluster_coupling_hbm,
    group_coupling_hbm, group_transfer_hbm, top_coupling_hbm,
    out, near_total,
    parts, cluster_transfer, cluster_coupling, group_coupling, group_transfer, top_coupling,
    group_moments, top_moments, pairs, cluster_target, group_target, top_target,
    sems,
):
    gx = lax.axis_index("gx")
    top = gx // 4

    loads = [
        pltpu.make_async_copy(source_ref, landing, sems.at[n])
        for n, (source_ref, landing) in enumerate(
            (
                (pairs_vmem, pairs),
                (cluster_target_hbm, cluster_target),
                (group_target_hbm, group_target),
                (top_target_hbm, top_target),
                (cluster_transfer_hbm, cluster_transfer),
                (cluster_coupling_hbm, cluster_coupling),
                (group_coupling_hbm, group_coupling),
                (group_transfer_hbm, group_transfer),
                (top_coupling_hbm.at[top], top_coupling),
            )
        )
    ]
    for copy in loads:
        copy.start()

    for k in range(GROUP):
        parts[k] = jnp.zeros((POINTS, 128), F32)
    loads[0].wait()

    def add_parts(g):
        for k in range(GROUP):
            near_total[pairs[0, g * GROUP + k] // 256] += parts[k]

    def listed_group(g):
        add_parts(jnp.maximum(g - 1, 0))
        for k in range(GROUP):
            code = pairs[0, g * GROUP + k]
            i, j = code // 256, code % 256
            square = jnp.dot(target[i], source[j], preferred_element_type=F32)
            parts[k] = folded(square, charges[pl.ds(j, 1), :])

    groups = (pairs[1, 0] + GROUP - 1) // GROUP

    @pl.loop(0, groups)
    def _(g):
        listed_group(g)

    add_parts(jnp.maximum(groups - 1, 0))

    unit = eye()
    for copy in loads[1:]:
        copy.wait()

    for g in range(32):
        group_moments[g : g + 1] = (
            every[4 * g, :, RANK:] + every[4 * g + 1, :, RANK:] + every[4 * g + 2, :, RANK:] + every[4 * g + 3, :, RANK:]
        )
    for h in range(8):
        total = jnp.zeros((RANK, RANK), F32)
        for k in range(4):
            g = 4 * h + k
            total = total + group_transfer[g] * to_column(group_moments[g : g + 1], unit)
        top_moments[h : h + 1] = jnp.sum(total, axis=0, keepdims=True)

    def masked(t):
        return jnp.where(t >= 0, 1.0, 0.0).astype(F32), jnp.maximum(t, 0)

    total = jnp.zeros((RANK, RANK), F32)
    for f in range(4):
        weight, t = masked(top_target[f, top])
        total = total + top_coupling[f] * (top_moments[pl.ds(t, 1), :] * weight)
    top_local = to_row(jnp.sum(total, axis=1, keepdims=True), unit)
    total = group_transfer[gx] * top_local
    for f in range(8):
        weight, t = masked(group_target[0, f])
        total = total + group_coupling[0, f] * (group_moments[pl.ds(t, 1), :] * weight)
    group_local = to_row(jnp.sum(total, axis=1, keepdims=True), unit)
    total = cluster_transfer[0] * group_local
    for f in range(8):
        weight, t = masked(cluster_target[0, f])
        total = total + cluster_coupling[0, f] * (every[t, :, :RANK] * weight)
    cluster_local = to_row(jnp.sum(total, axis=1, keepdims=True), unit)

    @pl.loop(0, LEAVES // CHUNK)
    def _(c):
        rows = []
        for k in range(CHUNK):
            i = c * CHUNK + k
            total = transfer[i] * cluster_local + far_total[i]
            leaf_local = jnp.sum(total, axis=1, keepdims=True)
            rows.append(jnp.sum(bases[i] * leaf_local, axis=0, keepdims=True))
        near_part = lane_sums(near_total.at[pl.ds(c * CHUNK, CHUNK)])
        out[pl.ds(pl.multiple_of(c * CHUNK, CHUNK), CHUNK), :] = near_part * INVERSE_FOUR_PI + jnp.concatenate(
            rows, axis=0
        )


def local(
    charges, points, leaf_bases, leaf_transfer, near_target, far_target, leaf_coupling, cluster_transfer,
    cluster_target, cluster_coupling, group_transfer, group_target, group_coupling, top_target, top_coupling,
):
    vmem = pl.BlockSpec(memory_space=pltpu.VMEM)
    anywhere = pl.BlockSpec(memory_space=pl.ANY)
    dma = pltpu.SemaphoreType.DMA

    def in_hbm(*arrays):
        return [pltpu.with_memory_space_constraint(array, pltpu.HBM) for array in arrays]

    handed = pl.pallas_call(
        exchange_kernel,
        out_shape=(
            pltpu.VMEM((3 * LEAVES + 1, TERMS, POINTS), BF16),
            pltpu.VMEM((LEAVES, POINTS, TERMS), BF16),
            pltpu.VMEM((3 * LEAVES + 8, POINTS), F32),
            pltpu.VMEM((DEVICES, 1, 2 * RANK), F32),
            pltpu.VMEM((2, PAIRS + 128), jnp.int32),
            pltpu.VMEM((LEAVES, RANK, POINTS), F32),
            pltpu.VMEM((LEAVES, RANK, RANK), F32),
            pltpu.VMEM((LEAVES, POINTS, 128), F32),
            pltpu.VMEM((LEAVES, RANK, RANK), F32),
        ),
        in_specs=[anywhere] * 8,
        out_specs=[vmem] * 9,
        scratch_shapes=[
            pltpu.VMEM((LEAVES * FAR, RANK, RANK), F32),
            pltpu.VMEM((LEAVES, FAR), jnp.int32),
            pltpu.SMEM((LEAVES, FAR), jnp.int32),
            pltpu.VMEM((5 * LEAVES + 8, RANK), F32),
            pltpu.VMEM((8, 128), jnp.int32),
            pltpu.SMEM((8, 128), jnp.int32),
            pltpu.VMEM((4, LEAVES, POINTS), F32),
            pltpu.VMEM((NEAR, LEAVES), jnp.int32),
            pltpu.VMEM((FAR, LEAVES), jnp.int32),
            pltpu.VMEM((1, RANK, RANK), F32),
            pltpu.VMEM((2, 4, LEAVES, POINTS), F32),
            pltpu.VMEM((5, LEAVES // 2, 2 * RANK), F32),
            pltpu.VMEM((DEVICES, 1, 2 * RANK), F32),
            dma((LEAVES // CHUNK,)),
            dma,
            dma,
            dma((2, LEAVES // CHUNK)),
            dma((5,)),
            dma((HALO_PARTS, 2)),
            dma((HALO_PARTS, 2)),
            dma((4,)),
            dma((4,)),
            dma((len(STAGES), 8)),
            dma((len(STAGES), 8)),
        ],
        compiler_params=pltpu.CompilerParams(
            collective_id=0, has_side_effects=True, vmem_limit_bytes=36 << 20
        ),
        name="exchange",
    )(
        *in_hbm(
            charges,
            jnp.transpose(points, (1, 0, 2)),
            near_target.T,
            far_target.T,
            cluster_transfer,
            jnp.swapaxes(leaf_bases, 1, 2),
            leaf_transfer,
            leaf_coupling.reshape(LEAVES * FAR, RANK, RANK),
        )
    )
    return pl.pallas_call(
        local_kernel,
        out_shape=(jax.ShapeDtypeStruct((LEAVES, POINTS), F32), pltpu.VMEM((LEAVES, POINTS, 128), F32)),
        in_specs=[vmem] * 9 + [anywhere] * 8,
        out_specs=[vmem] * 2,
        input_output_aliases={7: 1},
        scratch_shapes=[
            pltpu.VMEM((GROUP, POINTS, 128), F32),
            pltpu.VMEM((1, RANK, RANK), F32),
            pltpu.VMEM((1, 8, RANK, RANK), F32),
            pltpu.VMEM((1, 8, RANK, RANK), F32),
            pltpu.VMEM((32, RANK, RANK), F32),
            pltpu.VMEM((4, RANK, RANK), F32),
            pltpu.VMEM((32, RANK), F32),
            pltpu.VMEM((8, RANK), F32),
            pltpu.SMEM((2, PAIRS + 128), jnp.int32),
            pltpu.SMEM((1, 8), jnp.int32),
            pltpu.SMEM((1, 8), jnp.int32),
            pltpu.SMEM((4, 8), jnp.int32),
            dma((9,)),
        ],
        compiler_params=pltpu.CompilerParams(vmem_limit_bytes=36 << 20),
        name="local",
    )(
        *[pltpu.with_memory_space_constraint(array, pltpu.VMEM) for array in handed],
        *in_hbm(
            cluster_target,
            group_target,
            top_target.T,
            cluster_transfer,
            cluster_coupling,
            group_coupling,
            group_transfer,
            top_coupling,
        ),
    )[0]


def solution(mesh):
    leaf = ("gx", "gy")
    return jax.shard_map(
        local,
        mesh=mesh,
        in_specs=(
            P(leaf, None),
            P(leaf, None, None),
            P(leaf, None, None),
            P(leaf, None, None),
            P(leaf, None),
            P(leaf, None),
            P(leaf, None, None, None),
            P(leaf, None, None),
            P(leaf, None),
            P(leaf, None, None, None),
            P(),
            P("gx", None),
            P("gx", None, None, None),
            P(),
            P(),
        ),
        out_specs=P(leaf, None),
        check_vma=False,
    )
```

```python
import functools
import math

import jax
import jax.numpy as jnp
from jax import lax
from jax.experimental import pallas as pl
from jax.experimental.pallas import tpu as pltpu
from jax.sharding import PartitionSpec as P

MESH = pl.DeviceIdType.MESH
F32 = jnp.float32
BF16 = jnp.bfloat16
SMOOTHING = 0.01
INVERSE_FOUR_PI = 1.0 / (4.0 * math.pi)

LEAVES = 64
POINTS = 256
RANK = 64
NEAR = 8
FAR = 16
TERMS = 32
PAIRS = LEAVES * NEAR
GROUP = 16
OWN = 2
CHUNK = 8
DEVICES = 128
STAGES = ((1, 8), (8, 4), (32, 4))
HALO_PARTS = 2
BLANK = 3 * LEAVES


def split3(value):
    high = value.astype(BF16).astype(F32)
    rest = value - high
    middle = rest.astype(BF16).astype(F32)
    low = (rest - middle).astype(BF16).astype(F32)
    return high, middle, low


def centred(points):
    shifted = [p - 1.0 for p in points]
    norm = shifted[0] * shifted[0] + shifted[1] * shifted[1] + shifted[2] * shifted[2]
    return [split3(u) for u in shifted], norm


def source_terms(parts, norm):
    rows = []
    for high, middle, low in parts:
        high, middle, low = -2.0 * high, -2.0 * middle, -2.0 * low
        rows += [high, high, high, middle, middle, low]
    one = jnp.ones_like(norm)
    return rows + list(split3(norm + SMOOTHING)) + [one, one, one]


def target_terms(parts, norm):
    rows = []
    for high, middle, low in parts:
        rows += [high, middle, low, high, middle, high]
    one = jnp.ones_like(norm)
    return rows + [one, one, one] + list(split3(norm))


def by_leaf(rows):
    blank = jnp.zeros_like(rows[0])
    return jnp.swapaxes(jnp.stack(rows + [blank] * (TERMS - len(rows)), axis=0), 0, 1)


def eye():
    shape = (RANK, RANK)
    return (lax.broadcasted_iota(jnp.int32, shape, 0) == lax.broadcasted_iota(jnp.int32, shape, 1)).astype(F32)


def to_column(row, unit):
    return jnp.sum(unit * row, axis=1, keepdims=True)


def to_row(column, unit):
    return jnp.sum(unit * column, axis=0, keepdims=True)


def lane_sums(parts):
    lane = lax.broadcasted_iota(jnp.int32, (128, 128), 1)
    total = jnp.zeros((POINTS, 128), F32)
    for k in range(0, CHUNK, 2):
        ones = jnp.concatenate([jnp.where(lane == k + n, 1.0, 0.0) for n in range(2)], axis=0).astype(BF16)
        pair = jnp.concatenate([parts[k], parts[k + 1]], axis=1)
        high = pair.astype(BF16)
        low = (pair - high.astype(F32)).astype(BF16)
        total = total + jnp.dot(high, ones, preferred_element_type=F32) + jnp.dot(low, ones, preferred_element_type=F32)
    return total.T[:CHUNK]


def folded(square, charge):
    weighted = lax.rsqrt(square) * charge
    return weighted[:, :128] + weighted[:, 128:]


def exchange_kernel(
    charges_hbm, points_hbm, near_hbm, far_hbm, cluster_transfer_hbm, bases_hbm, transfer_hbm, coupling_hbm,
    source_out, target_out, charge_out, every_out, pair_out, bases, transfer, near_out, far_out,
    coupling, far_vector, far_rows, moment_rows, choice_vector, choice, own, near, far, cluster_transfer, halo, window, every,
    coupling_sems, far_sem, choice_sem, load_sems, small_sems, halo_send, halo_recv, moment_send, moment_recv, every_send, every_recv,
):
    gx, gy = lax.axis_index("gx"), lax.axis_index("gy")
    device = gx * 4 + gy

    def place(index):
        return (index // 4, index % 4)

    def beside(distance):
        return place((device + distance + DEVICES) % DEVICES)

    chunks = LEAVES // CHUNK

    def load_copies(c):
        span = pl.ds(c * CHUNK, CHUNK)
        return (
            pltpu.make_async_copy(bases_hbm.at[span], bases.at[span], load_sems.at[0, c]),
            pltpu.make_async_copy(transfer_hbm.at[span], transfer.at[span], load_sems.at[1, c]),
        )

    small = [
        pltpu.make_async_copy(source, landing, small_sems.at[n])
        for n, (source, landing) in enumerate(
            (
                (charges_hbm, own.at[0]),
                (points_hbm, own.at[pl.ds(1, 3)]),
                (near_hbm, near),
                (far_hbm, far),
                (cluster_transfer_hbm, cluster_transfer),
            )
        )
    ]
    for copy in small:
        copy.start()

    @pl.loop(0, chunks)
    def _(c):
        for copy in load_copies(c):
            copy.start()

    def coupling_copy(c):
        span = pl.ds(c * CHUNK * FAR, CHUNK * FAR)
        return pltpu.make_async_copy(coupling_hbm.at[span], coupling.at[span], coupling_sems.at[c])

    @pl.loop(0, chunks)
    def _(c):
        coupling_copy(c).start()

    barrier = pltpu.get_barrier_semaphore()
    for distance in (1, -1, 2, -2):
        pl.semaphore_signal(barrier, inc=1, device_id=beside(distance), device_id_type=MESH)

    row = gy * (DEVICES // 4) + gx

    def mate(stage, k):
        unit, count = STAGES[stage]
        position = (row // unit) % count
        there = row + ((position + k) % count - position) * unit
        return (there % (DEVICES // 4), there // (DEVICES // 4))

    for stage in range(len(STAGES)):

        @pl.loop(1, STAGES[stage][1])
        def _(k):
            pl.semaphore_signal(barrier, inc=1, device_id=mate(stage, k), device_id_type=MESH)

    for copy in small:
        copy.wait()
    far_targets = far[...]
    far_vector[...] = jnp.where(far_targets >= 0, far_targets - (device - 2) * LEAVES, 5 * LEAVES).T
    far_copy = pltpu.make_async_copy(far_vector, far_rows, far_sem)
    far_copy.start()

    slots = near[...]
    local_slots = slots - device * LEAVES
    is_here = jnp.where((local_slots >= 0) & (local_slots < LEAVES), 1, 0)
    live_rows = []
    own_before = jnp.zeros((1, LEAVES), jnp.int32)
    chosen = [jnp.full((1, LEAVES), BLANK, jnp.int32) for _ in range(OWN)]
    for s in range(NEAR):
        is_own = is_here[s : s + 1] > 0
        for n in range(OWN):
            chosen[n] = jnp.where(is_own & (own_before == n), local_slots[s : s + 1] + LEAVES, chosen[n])
        left = jnp.where(is_own & (own_before < OWN), 0.0, 1.0)
        live_rows.append(jnp.where(slots[s : s + 1] >= 0, left, 0.0))
        own_before = own_before + is_here[s : s + 1]
    for n in range(OWN):
        choice_vector[n : n + 1, 0:LEAVES] = chosen[n]
    choice_copy = pltpu.make_async_copy(choice_vector, choice, choice_sem)
    choice_copy.start()
    live = jnp.concatenate(live_rows, axis=0)
    before = (
        lax.broadcasted_iota(jnp.int32, (LEAVES, LEAVES), 0) < lax.broadcasted_iota(jnp.int32, (LEAVES, LEAVES), 1)
    ).astype(BF16)
    rank_in_slot = jnp.dot(live.astype(BF16), before, preferred_element_type=F32)
    in_slot = jnp.sum(live, axis=1, keepdims=True)
    leaf_row = lax.broadcasted_iota(jnp.int32, (1, LEAVES), 1)
    code = (leaf_row * 256 + slots - (device - 1) * LEAVES).astype(F32)
    position_row = lax.broadcasted_iota(jnp.int32, (1, PAIRS), 1).astype(F32)
    found = jnp.zeros((LEAVES, PAIRS), F32)
    start = jnp.zeros((1, 1), F32)
    positions = []
    for s in range(NEAR):
        positions.append(jnp.where(live[s : s + 1] > 0, rank_in_slot[s : s + 1] + start, -1.0))
        start = start + in_slot[s : s + 1]
    table = jnp.concatenate(positions + [code], axis=0).T
    for s in range(NEAR):
        found = jnp.where(table[:, s : s + 1] == position_row, table[:, NEAR + s : NEAR + s + 1], found)
    pairs = jnp.sum(found, axis=0, keepdims=True)
    pair_out[0:1, 0:PAIRS] = jnp.where(position_row < start, pairs, float(BLANK)).astype(jnp.int32)
    pair_out[0:1, PAIRS:] = jnp.full((1, 128), BLANK, jnp.int32)
    pair_out[1:2, 0:128] = jnp.broadcast_to(start.astype(jnp.int32), (1, 128))
    pl.semaphore_wait(barrier, 4 + sum(count - 1 for _, count in STAGES))

    part_leaves = LEAVES // HALO_PARTS
    copies_of_halo = [
        [
            pltpu.make_async_remote_copy(
                src_ref=own.at[:, pl.ds(part * part_leaves, part_leaves)],
                dst_ref=halo.at[side, :, pl.ds(part * part_leaves, part_leaves)],
                send_sem=halo_send.at[part, side],
                recv_sem=halo_recv.at[part, side],
                device_id=beside(distance),
                device_id_type=MESH,
            )
            for side, distance in ((0, 1), (1, -1))
        ]
        for part in range(HALO_PARTS)
    ]
    for copy in copies_of_halo[0]:
        copy.start()

    lane = lax.broadcasted_iota(jnp.int32, (RANK, LEAVES), 1)

    def moment_chunk(c, carry):
        columns, total = carry
        for copy in load_copies(c):
            copy.wait()
        weights = own[0, pl.ds(pl.multiple_of(c * CHUNK, CHUNK), CHUNK), :]
        for k in range(CHUNK):
            product = bases[c * CHUNK + k] * weights[k : k + 1, :]
            column = jnp.sum(product[:, :128] + product[:, 128:], axis=1, keepdims=True)
            columns = jnp.where(lane == c * CHUNK + k, column, columns)
            total = total + transfer[c * CHUNK + k] * column
        return columns, total

    columns, total = lax.fori_loop(
        0, chunks, moment_chunk, (jnp.zeros((RANK, LEAVES), F32), jnp.zeros((RANK, RANK), F32))
    )
    rows = columns.T
    window[2] = jnp.concatenate([rows[: LEAVES // 2], rows[LEAVES // 2 :]], axis=1)
    unit = eye()
    cluster_row = jnp.sum(total, axis=0, keepdims=True)
    lifted_row = jnp.sum(cluster_transfer[0] * to_column(cluster_row, unit), axis=0, keepdims=True)
    every[row, 0:1, 0:RANK] = cluster_row
    every[row, 0:1, RANK : 2 * RANK] = lifted_row

    def every_copy(stage, k):
        unit, _ = STAGES[stage]
        rows = pl.ds((row // unit) * unit, unit)
        return pltpu.make_async_remote_copy(
            src_ref=every.at[rows],
            dst_ref=every.at[rows],
            send_sem=every_send.at[stage, k],
            recv_sem=every_recv.at[stage, k],
            device_id=mate(stage, k),
            device_id_type=MESH,
        )

    def start_stage(stage):
        for k in range(1, STAGES[stage][1]):
            every_copy(stage, k).start()

    def finish_stage(stage):
        for k in range(1, STAGES[stage][1]):
            every_copy(stage, k).wait_recv()

    start_stage(0)

    def moment_copies():
        copies = []
        for n, distance in enumerate((2, 1, -1, -2)):
            slot = (0, 1, 3, 4)[n]
            copies.append(
                pltpu.make_async_remote_copy(
                    src_ref=window.at[2],
                    dst_ref=window.at[slot],
                    send_sem=moment_send.at[n],
                    recv_sem=moment_recv.at[n],
                    device_id=beside(distance),
                    device_id_type=MESH,
                )
            )
        return copies

    moments = moment_copies()
    for copy in moments:
        copy.start()
    for copies in copies_of_halo[1:]:
        for copy in copies:
            copy.start()

    @pl.loop(0, chunks)
    def _(c):
        span = pl.ds(pl.multiple_of(c * CHUNK, CHUNK), CHUNK)
        parts, norm = centred([own[n, span, :] for n in range(1, 4)])
        source_out[pl.ds(LEAVES + c * CHUNK, CHUNK)] = by_leaf(source_terms(parts, norm)).astype(BF16)
        target = by_leaf(target_terms(parts, norm))
        for k in range(CHUNK):
            target_out[c * CHUNK + k] = target[k].T.astype(BF16)

    charge_out[LEAVES : 2 * LEAVES] = own[0]
    charge_out[3 * LEAVES :] = jnp.zeros((8, POINTS), F32)
    term = lax.broadcasted_iota(jnp.int32, (TERMS, POINTS), 0)
    source_out[BLANK] = jnp.where(term == 18, 1.0, 0.0).astype(BF16)

    finish_stage(0)
    start_stage(1)

    choice_copy.wait()

    for n in range(OWN):

        @pl.loop(0, LEAVES // GROUP)
        def _(g):
            for k in range(GROUP):
                i = g * GROUP + k
                j = jnp.clip(choice[n, i], 0, BLANK)
                square = jnp.dot(target_out[i], source_out[j], preferred_element_type=F32)
                part = folded(square, charge_out[pl.ds(j, 1), :])
                if n == 0:
                    near_out[i] = part
                else:
                    near_out[i] += part

        if n == 0:
            finish_stage(1)
            start_stage(2)

    for copy in moments:
        copy.wait_recv()
    for n in range(5):
        moment_rows[n * LEAVES : n * LEAVES + LEAVES // 2] = window[n][:, :RANK]
        moment_rows[n * LEAVES + LEAVES // 2 : (n + 1) * LEAVES] = window[n][:, RANK:]
    moment_rows[5 * LEAVES :] = jnp.zeros((8, RANK), F32)
    far_copy.wait()

    def far_chunk(c):
        coupling_copy(c).wait()
        for k in range(CHUNK):
            i = c * CHUNK + k
            total = None
            for f in range(FAR):
                slot = jnp.clip(far_rows[i, f], 0, 5 * LEAVES)
                term = coupling[i * FAR + f] * moment_rows[pl.ds(slot, 1), :]
                total = term if total is None else total + term
            far_out[i] = total

    early = chunks * 5 // 8
    pl.loop(0, early)(far_chunk)

    for part in range(HALO_PARTS):
        for side in range(2):
            copies_of_halo[part][side].wait_recv()
            first = 2 * LEAVES * side

            @pl.loop(part * part_leaves // CHUNK, (part + 1) * part_leaves // CHUNK)
            def _(c):
                span = pl.ds(pl.multiple_of(c * CHUNK, CHUNK), CHUNK)
                parts, norm = centred([halo[side, n, span, :] for n in range(1, 4)])
                source_out[pl.ds(first + c * CHUNK, CHUNK)] = by_leaf(source_terms(parts, norm)).astype(BF16)

    charge_out[0:LEAVES] = halo[0, 0]
    charge_out[2 * LEAVES : 3 * LEAVES] = halo[1, 0]

    pl.loop(early, chunks)(far_chunk)

    finish_stage(2)
    every_out[...] = every[...]

    for stage in range(len(STAGES)):
        for k in range(1, STAGES[stage][1]):
            every_copy(stage, k).wait_send()
    for copy in sum(copies_of_halo, []) + moments:
        copy.wait_send()


def local_kernel(
    source, target, charges, every, pairs_vmem, bases, transfer, near_first, far_total,
    cluster_target_hbm, group_target_hbm, top_target_hbm, cluster_transfer_hbm, cluster_coupling_hbm,
    group_coupling_hbm, group_transfer_hbm, top_coupling_hbm,
    out, near_total,
    parts, cluster_transfer, cluster_coupling, group_coupling, group_transfer, top_coupling,
    group_moments, pairs, cluster_target, group_target, top_target,
    sems,
):
    gx = lax.axis_index("gx")
    top = gx // 4

    loads = [
        pltpu.make_async_copy(source_ref, landing, sems.at[n])
        for n, (source_ref, landing) in enumerate(
            (
                (pairs_vmem, pairs),
                (cluster_target_hbm, cluster_target),
                (group_target_hbm, group_target),
                (top_target_hbm, top_target),
                (cluster_transfer_hbm, cluster_transfer),
                (cluster_coupling_hbm, cluster_coupling),
                (group_coupling_hbm, group_coupling),
                (group_transfer_hbm, group_transfer),
                (top_coupling_hbm.at[top], top_coupling),
            )
        )
    ]
    for copy in loads:
        copy.start()

    for k in range(GROUP):
        parts[k] = jnp.zeros((POINTS, 128), F32)
    loads[0].wait()

    def add_parts(g):
        for k in range(GROUP):
            near_total[pairs[0, g * GROUP + k] // 256] += parts[k]

    def listed_group(g):
        add_parts(jnp.maximum(g - 1, 0))
        for k in range(GROUP):
            code = pairs[0, g * GROUP + k]
            i, j = code // 256, code % 256
            square = jnp.dot(target[i], source[j], preferred_element_type=F32)
            parts[k] = folded(square, charges[pl.ds(j, 1), :])

    groups = (pairs[1, 0] + GROUP - 1) // GROUP

    @pl.loop(0, groups)
    def _(g):
        listed_group(g)

    add_parts(jnp.maximum(groups - 1, 0))

    unit = eye()
    for copy in loads[1:]:
        copy.wait()

    quarter = DEVICES // 4
    group_moments[...] = sum(every[pl.ds(k * quarter, quarter), 0, :][:, RANK:] for k in range(4))
    def masked(t):
        return jnp.where(t >= 0, 1.0, 0.0).astype(F32), jnp.maximum(t, 0)

    total = jnp.zeros((RANK, RANK), F32)
    for f in range(4):
        weight, t = masked(top_target[f, top])
        lifted = jnp.zeros((RANK, RANK), F32)
        for k in range(4):
            g = 4 * t + k
            lifted = lifted + group_transfer[g] * to_column(group_moments[pl.ds(g, 1), :], unit)
        total = total + top_coupling[f] * (jnp.sum(lifted, axis=0, keepdims=True) * weight)
    top_local = to_row(jnp.sum(total, axis=1, keepdims=True), unit)
    total = group_transfer[gx] * top_local
    for f in range(8):
        weight, t = masked(group_target[0, f])
        total = total + group_coupling[0, f] * (group_moments[pl.ds(t, 1), :] * weight)
    group_local = to_row(jnp.sum(total, axis=1, keepdims=True), unit)
    total = cluster_transfer[0] * group_local
    for f in range(8):
        weight, t = masked(cluster_target[0, f])
        total = total + cluster_coupling[0, f] * (every[(t % 4) * quarter + t // 4, :, :RANK] * weight)
    cluster_local = to_row(jnp.sum(total, axis=1, keepdims=True), unit)

    @pl.loop(0, LEAVES // CHUNK)
    def _(c):
        rows = []
        for k in range(CHUNK):
            i = c * CHUNK + k
            total = transfer[i] * cluster_local + far_total[i]
            leaf_local = jnp.sum(total, axis=1, keepdims=True)
            rows.append(jnp.sum(bases[i] * leaf_local, axis=0, keepdims=True))
        near_part = lane_sums(near_total.at[pl.ds(c * CHUNK, CHUNK)])
        out[pl.ds(pl.multiple_of(c * CHUNK, CHUNK), CHUNK), :] = near_part * INVERSE_FOUR_PI + jnp.concatenate(
            rows, axis=0
        )


def local(
    charges, points, leaf_bases, leaf_transfer, near_target, far_target, leaf_coupling, cluster_transfer,
    cluster_target, cluster_coupling, group_transfer, group_target, group_coupling, top_target, top_coupling,
):
    vmem = pl.BlockSpec(memory_space=pltpu.VMEM)
    anywhere = pl.BlockSpec(memory_space=pl.ANY)
    dma = pltpu.SemaphoreType.DMA

    def in_hbm(*arrays):
        return [pltpu.with_memory_space_constraint(array, pltpu.HBM) for array in arrays]

    handed = pl.pallas_call(
        exchange_kernel,
        out_shape=(
            pltpu.VMEM((3 * LEAVES + 1, TERMS, POINTS), BF16),
            pltpu.VMEM((LEAVES, POINTS, TERMS), BF16),
            pltpu.VMEM((3 * LEAVES + 8, POINTS), F32),
            pltpu.VMEM((DEVICES, 1, 2 * RANK), F32),
            pltpu.VMEM((2, PAIRS + 128), jnp.int32),
            pltpu.VMEM((LEAVES, RANK, POINTS), F32),
            pltpu.VMEM((LEAVES, RANK, RANK), F32),
            pltpu.VMEM((LEAVES, POINTS, 128), F32),
            pltpu.VMEM((LEAVES, RANK, RANK), F32),
        ),
        in_specs=[anywhere] * 8,
        out_specs=[vmem] * 9,
        scratch_shapes=[
            pltpu.VMEM((LEAVES * FAR, RANK, RANK), F32),
            pltpu.VMEM((LEAVES, FAR), jnp.int32),
            pltpu.SMEM((LEAVES, FAR), jnp.int32),
            pltpu.VMEM((5 * LEAVES + 8, RANK), F32),
            pltpu.VMEM((8, 128), jnp.int32),
            pltpu.SMEM((8, 128), jnp.int32),
            pltpu.VMEM((4, LEAVES, POINTS), F32),
            pltpu.VMEM((NEAR, LEAVES), jnp.int32),
            pltpu.VMEM((FAR, LEAVES), jnp.int32),
            pltpu.VMEM((1, RANK, RANK), F32),
            pltpu.VMEM((2, 4, LEAVES, POINTS), F32),
            pltpu.VMEM((5, LEAVES // 2, 2 * RANK), F32),
            pltpu.VMEM((DEVICES, 1, 2 * RANK), F32),
            dma((LEAVES // CHUNK,)),
            dma,
            dma,
            dma((2, LEAVES // CHUNK)),
            dma((5,)),
            dma((HALO_PARTS, 2)),
            dma((HALO_PARTS, 2)),
            dma((4,)),
            dma((4,)),
            dma((len(STAGES), 8)),
            dma((len(STAGES), 8)),
        ],
        compiler_params=pltpu.CompilerParams(
            collective_id=0, has_side_effects=True, vmem_limit_bytes=36 << 20
        ),
        name="exchange",
    )(
        *in_hbm(
            charges,
            jnp.transpose(points, (1, 0, 2)),
            near_target.T,
            far_target.T,
            cluster_transfer,
            jnp.swapaxes(leaf_bases, 1, 2),
            leaf_transfer,
            leaf_coupling.reshape(LEAVES * FAR, RANK, RANK),
        )
    )
    return pl.pallas_call(
        local_kernel,
        out_shape=(jax.ShapeDtypeStruct((LEAVES, POINTS), F32), pltpu.VMEM((LEAVES, POINTS, 128), F32)),
        in_specs=[vmem] * 9 + [anywhere] * 8,
        out_specs=[vmem] * 2,
        input_output_aliases={7: 1},
        scratch_shapes=[
            pltpu.VMEM((GROUP, POINTS, 128), F32),
            pltpu.VMEM((1, RANK, RANK), F32),
            pltpu.VMEM((1, 8, RANK, RANK), F32),
            pltpu.VMEM((1, 8, RANK, RANK), F32),
            pltpu.VMEM((32, RANK, RANK), F32),
            pltpu.VMEM((4, RANK, RANK), F32),
            pltpu.VMEM((32, RANK), F32),
            pltpu.SMEM((2, PAIRS + 128), jnp.int32),
            pltpu.SMEM((1, 8), jnp.int32),
            pltpu.SMEM((1, 8), jnp.int32),
            pltpu.SMEM((4, 8), jnp.int32),
            dma((9,)),
        ],
        compiler_params=pltpu.CompilerParams(vmem_limit_bytes=36 << 20),
        name="local",
    )(
        *[pltpu.with_memory_space_constraint(array, pltpu.VMEM) for array in handed],
        *in_hbm(
            cluster_target,
            group_target,
            top_target.T,
            cluster_transfer,
            cluster_coupling,
            group_coupling,
            group_transfer,
            top_coupling,
        ),
    )[0]


def solution(mesh):
    leaf = ("gx", "gy")
    return jax.shard_map(
        local,
        mesh=mesh,
        in_specs=(
            P(leaf, None),
            P(leaf, None, None),
            P(leaf, None, None),
            P(leaf, None, None),
            P(leaf, None),
            P(leaf, None),
            P(leaf, None, None, None),
            P(leaf, None, None),
            P(leaf, None),
            P(leaf, None, None, None),
            P(),
            P("gx", None),
            P("gx", None, None, None),
            P(),
            P(),
        ),
        out_specs=P(leaf, None),
        check_vma=False,
    )
```

```python
import functools
import math

import jax
import jax.numpy as jnp
from jax import lax
from jax.experimental import pallas as pl
from jax.experimental.pallas import tpu as pltpu
from jax.sharding import PartitionSpec as P

MESH = pl.DeviceIdType.MESH
F32 = jnp.float32
BF16 = jnp.bfloat16
SMOOTHING = 0.01
INVERSE_FOUR_PI = 1.0 / (4.0 * math.pi)

LEAVES = 64
POINTS = 256
RANK = 64
NEAR = 8
FAR = 16
TERMS = 32
PAIRS = LEAVES * NEAR
GROUP = 16
OWN = 2
CHUNK = 8
DEVICES = 128
STAGES = ((1, 8), (8, 4), (32, 4))
HALO_PARTS = 2
BLANK = 3 * LEAVES


def split3(value):
    high = value.astype(BF16).astype(F32)
    rest = value - high
    middle = rest.astype(BF16).astype(F32)
    low = (rest - middle).astype(BF16).astype(F32)
    return high, middle, low


def centred(points):
    shifted = [p - 1.0 for p in points]
    norm = shifted[0] * shifted[0] + shifted[1] * shifted[1] + shifted[2] * shifted[2]
    return [split3(u) for u in shifted], norm


def source_terms(parts, norm):
    rows = []
    for high, middle, low in parts:
        high, middle, low = -2.0 * high, -2.0 * middle, -2.0 * low
        rows += [high, high, high, middle, middle, low]
    one = jnp.ones_like(norm)
    return rows + list(split3(norm + SMOOTHING)) + [one, one, one]


def target_terms(parts, norm):
    rows = []
    for high, middle, low in parts:
        rows += [high, middle, low, high, middle, high]
    one = jnp.ones_like(norm)
    return rows + [one, one, one] + list(split3(norm))


def by_leaf(rows):
    blank = jnp.zeros_like(rows[0])
    return jnp.swapaxes(jnp.stack(rows + [blank] * (TERMS - len(rows)), axis=0), 0, 1)


def eye():
    shape = (RANK, RANK)
    return (lax.broadcasted_iota(jnp.int32, shape, 0) == lax.broadcasted_iota(jnp.int32, shape, 1)).astype(F32)


def to_column(row, unit):
    return jnp.sum(unit * row, axis=1, keepdims=True)


def to_row(column, unit):
    return jnp.sum(unit * column, axis=0, keepdims=True)


def lane_sums(parts, first):
    odd = lax.broadcasted_iota(jnp.int32, (POINTS, 128), 1) % 2
    source = lax.broadcasted_iota(jnp.int32, (256, 128), 0)
    column = lax.broadcasted_iota(jnp.int32, (256, 128), 1) - first
    total = None
    for k in range(0, CHUNK, 4):
        halves = []
        for n in (k, k + 2):
            here, there = parts[n], parts[n + 1]
            halves.append(jnp.where(odd == 0, here, there) + pltpu.roll(jnp.where(odd == 0, there, here), 127, axis=1))
        values = jnp.concatenate(halves, axis=1)
        high = values.astype(BF16)
        low = (values - high.astype(F32)).astype(BF16)
        ones = jnp.where(k + source // 128 * 2 + source % 2 == column, 1.0, 0.0).astype(BF16)
        for piece in (high, low):
            term = jnp.dot(piece, ones, preferred_element_type=F32)
            total = term if total is None else total + term
    return total


def folded(square, charge):
    weighted = lax.rsqrt(square) * charge
    return weighted[:, :128] + weighted[:, 128:]


def exchange_kernel(
    charges_hbm, points_hbm, near_hbm, far_hbm, cluster_transfer_hbm, bases_hbm, transfer_hbm, coupling_hbm,
    source_out, target_out, charge_out, every_out, pair_out, bases, transfer, near_out, far_out,
    coupling, far_vector, far_rows, moment_rows, choice_vector, choice, own, near, far, cluster_transfer, halo, window, every,
    coupling_sems, far_sem, choice_sem, load_sems, small_sems, halo_send, halo_recv, moment_send, moment_recv, every_send, every_recv,
):
    gx, gy = lax.axis_index("gx"), lax.axis_index("gy")
    device = gx * 4 + gy

    def place(index):
        return (index // 4, index % 4)

    def beside(distance):
        return place((device + distance + DEVICES) % DEVICES)

    chunks = LEAVES // CHUNK

    def load_copies(c):
        span = pl.ds(c * CHUNK, CHUNK)
        return (
            pltpu.make_async_copy(bases_hbm.at[span], bases.at[span], load_sems.at[0, c]),
            pltpu.make_async_copy(transfer_hbm.at[span], transfer.at[span], load_sems.at[1, c]),
        )

    small = [
        pltpu.make_async_copy(source, landing, small_sems.at[n])
        for n, (source, landing) in enumerate(
            (
                (charges_hbm, own.at[0]),
                (points_hbm, own.at[pl.ds(1, 3)]),
                (near_hbm, near),
                (far_hbm, far),
                (cluster_transfer_hbm, cluster_transfer),
            )
        )
    ]
    for copy in small:
        copy.start()

    @pl.loop(0, chunks)
    def _(c):
        for copy in load_copies(c):
            copy.start()

    def coupling_copy(c):
        span = pl.ds(c * CHUNK * FAR, CHUNK * FAR)
        return pltpu.make_async_copy(coupling_hbm.at[span], coupling.at[span], coupling_sems.at[c])

    @pl.loop(0, chunks)
    def _(c):
        coupling_copy(c).start()

    barrier = pltpu.get_barrier_semaphore()
    for distance in (1, -1, 2, -2):
        pl.semaphore_signal(barrier, inc=1, device_id=beside(distance), device_id_type=MESH)

    row = gy * (DEVICES // 4) + gx

    def mate(stage, k):
        unit, count = STAGES[stage]
        position = (row // unit) % count
        there = row + ((position + k) % count - position) * unit
        return (there % (DEVICES // 4), there // (DEVICES // 4))

    for stage in range(len(STAGES)):

        @pl.loop(1, STAGES[stage][1])
        def _(k):
            pl.semaphore_signal(barrier, inc=1, device_id=mate(stage, k), device_id_type=MESH)

    for copy in small:
        copy.wait()
    far_targets = far[...]
    far_vector[...] = jnp.where(far_targets >= 0, far_targets - (device - 2) * LEAVES, 5 * LEAVES).T
    far_copy = pltpu.make_async_copy(far_vector, far_rows, far_sem)
    far_copy.start()

    slots = near[...]
    local_slots = slots - device * LEAVES
    is_here = jnp.where((local_slots >= 0) & (local_slots < LEAVES), 1, 0)
    live_rows = []
    own_before = jnp.zeros((1, LEAVES), jnp.int32)
    chosen = [jnp.full((1, LEAVES), BLANK, jnp.int32) for _ in range(OWN)]
    for s in range(NEAR):
        is_own = is_here[s : s + 1] > 0
        for n in range(OWN):
            chosen[n] = jnp.where(is_own & (own_before == n), local_slots[s : s + 1] + LEAVES, chosen[n])
        left = jnp.where(is_own & (own_before < OWN), 0.0, 1.0)
        live_rows.append(jnp.where(slots[s : s + 1] >= 0, left, 0.0))
        own_before = own_before + is_here[s : s + 1]
    for n in range(OWN):
        choice_vector[n : n + 1, 0:LEAVES] = chosen[n]
    choice_copy = pltpu.make_async_copy(choice_vector, choice, choice_sem)
    choice_copy.start()
    live = jnp.concatenate(live_rows, axis=0)
    before = (
        lax.broadcasted_iota(jnp.int32, (LEAVES, LEAVES), 0) < lax.broadcasted_iota(jnp.int32, (LEAVES, LEAVES), 1)
    ).astype(BF16)
    rank_in_slot = jnp.dot(live.astype(BF16), before, preferred_element_type=F32)
    in_slot = jnp.sum(live, axis=1, keepdims=True)
    leaf_row = lax.broadcasted_iota(jnp.int32, (1, LEAVES), 1)
    code = (leaf_row * 256 + slots - (device - 1) * LEAVES).astype(F32)
    position_row = lax.broadcasted_iota(jnp.int32, (1, PAIRS), 1).astype(F32)
    found = jnp.zeros((LEAVES, PAIRS), F32)
    start = jnp.zeros((1, 1), F32)
    positions = []
    for s in range(NEAR):
        positions.append(jnp.where(live[s : s + 1] > 0, rank_in_slot[s : s + 1] + start, -1.0))
        start = start + in_slot[s : s + 1]
    table = jnp.concatenate(positions + [code], axis=0).T
    for s in range(NEAR):
        found = jnp.where(table[:, s : s + 1] == position_row, table[:, NEAR + s : NEAR + s + 1], found)
    pairs = jnp.sum(found, axis=0, keepdims=True)
    pair_out[0:1, 0:PAIRS] = jnp.where(position_row < start, pairs, float(BLANK)).astype(jnp.int32)
    pair_out[0:1, PAIRS:] = jnp.full((1, 128), BLANK, jnp.int32)
    pair_out[1:2, 0:128] = jnp.broadcast_to(start.astype(jnp.int32), (1, 128))
    @pl.loop(0, chunks)
    def _(c):
        span = pl.ds(pl.multiple_of(c * CHUNK, CHUNK), CHUNK)
        parts, norm = centred([own[n, span, :] for n in range(1, 4)])
        source_out[pl.ds(LEAVES + c * CHUNK, CHUNK)] = by_leaf(source_terms(parts, norm)).astype(BF16)
        target = by_leaf(target_terms(parts, norm)).astype(BF16)
        for k in range(CHUNK):
            target_out[c * CHUNK + k] = target[k].T

    charge_out[LEAVES : 2 * LEAVES] = own[0]
    charge_out[3 * LEAVES :] = jnp.zeros((8, POINTS), F32)
    term = lax.broadcasted_iota(jnp.int32, (TERMS, POINTS), 0)
    source_out[BLANK] = jnp.where(term == 18, 1.0, 0.0).astype(BF16)

    pl.semaphore_wait(barrier, 4 + sum(count - 1 for _, count in STAGES))

    part_leaves = LEAVES // HALO_PARTS
    copies_of_halo = [
        [
            pltpu.make_async_remote_copy(
                src_ref=own.at[:, pl.ds(part * part_leaves, part_leaves)],
                dst_ref=halo.at[side, :, pl.ds(part * part_leaves, part_leaves)],
                send_sem=halo_send.at[part, side],
                recv_sem=halo_recv.at[part, side],
                device_id=beside(distance),
                device_id_type=MESH,
            )
            for side, distance in ((0, 1), (1, -1))
        ]
        for part in range(HALO_PARTS)
    ]
    for copy in copies_of_halo[0]:
        copy.start()

    lane = lax.broadcasted_iota(jnp.int32, (RANK, LEAVES), 1)

    def moment_chunk(c, carry):
        columns, total = carry
        for copy in load_copies(c):
            copy.wait()
        weights = own[0, pl.ds(pl.multiple_of(c * CHUNK, CHUNK), CHUNK), :]
        for k in range(CHUNK):
            product = bases[c * CHUNK + k] * weights[k : k + 1, :]
            column = jnp.sum(product[:, :128] + product[:, 128:], axis=1, keepdims=True)
            columns = jnp.where(lane == c * CHUNK + k, column, columns)
            total = total + transfer[c * CHUNK + k] * column
        return columns, total

    columns, total = lax.fori_loop(
        0, chunks, moment_chunk, (jnp.zeros((RANK, LEAVES), F32), jnp.zeros((RANK, RANK), F32))
    )
    rows = columns.T
    window[2] = jnp.concatenate([rows[: LEAVES // 2], rows[LEAVES // 2 :]], axis=1)
    unit = eye()
    cluster_row = jnp.sum(total, axis=0, keepdims=True)
    lifted_row = jnp.sum(cluster_transfer[0] * to_column(cluster_row, unit), axis=0, keepdims=True)
    every[row, 0:1, 0:RANK] = cluster_row
    every[row, 0:1, RANK : 2 * RANK] = lifted_row

    def every_copy(stage, k):
        unit, _ = STAGES[stage]
        rows = pl.ds((row // unit) * unit, unit)
        return pltpu.make_async_remote_copy(
            src_ref=every.at[rows],
            dst_ref=every.at[rows],
            send_sem=every_send.at[stage, k],
            recv_sem=every_recv.at[stage, k],
            device_id=mate(stage, k),
            device_id_type=MESH,
        )

    def start_stage(stage):
        for k in range(1, STAGES[stage][1]):
            every_copy(stage, k).start()

    def finish_stage(stage):
        for k in range(1, STAGES[stage][1]):
            every_copy(stage, k).wait_recv()

    start_stage(0)

    def moment_copies():
        copies = []
        for n, distance in enumerate((2, 1, -1, -2)):
            slot = (0, 1, 3, 4)[n]
            copies.append(
                pltpu.make_async_remote_copy(
                    src_ref=window.at[2],
                    dst_ref=window.at[slot],
                    send_sem=moment_send.at[n],
                    recv_sem=moment_recv.at[n],
                    device_id=beside(distance),
                    device_id_type=MESH,
                )
            )
        return copies

    moments = moment_copies()
    for copy in moments:
        copy.start()
    for copies in copies_of_halo[1:]:
        for copy in copies:
            copy.start()

    choice_copy.wait()

    for n in range(OWN):

        @pl.loop(0, LEAVES // GROUP)
        def _(g):
            for k in range(GROUP):
                i = g * GROUP + k
                j = jnp.clip(choice[n, i], 0, BLANK)
                square = jnp.dot(target_out[i], source_out[j], preferred_element_type=F32)
                part = folded(square, charge_out[pl.ds(j, 1), :])
                if n == 0:
                    near_out[i] = part
                else:
                    near_out[i] += part

        if n == 0:
            finish_stage(0)
            start_stage(1)

    finish_stage(1)
    start_stage(2)

    for copy in moments:
        copy.wait_recv()
    for n in range(5):
        moment_rows[n * LEAVES : n * LEAVES + LEAVES // 2] = window[n][:, :RANK]
        moment_rows[n * LEAVES + LEAVES // 2 : (n + 1) * LEAVES] = window[n][:, RANK:]
    moment_rows[5 * LEAVES :] = jnp.zeros((8, RANK), F32)
    far_copy.wait()

    def far_chunk(c):
        coupling_copy(c).wait()
        for k in range(CHUNK):
            i = c * CHUNK + k
            total = None
            for f in range(FAR):
                slot = jnp.clip(far_rows[i, f], 0, 5 * LEAVES)
                term = coupling[i * FAR + f] * moment_rows[pl.ds(slot, 1), :]
                total = term if total is None else total + term
            far_out[i] = total

    early = chunks * 5 // 8
    pl.loop(0, early)(far_chunk)

    for part in range(HALO_PARTS):
        for side in range(2):
            copies_of_halo[part][side].wait_recv()
            first = 2 * LEAVES * side

            @pl.loop(part * part_leaves // CHUNK, (part + 1) * part_leaves // CHUNK)
            def _(c):
                span = pl.ds(pl.multiple_of(c * CHUNK, CHUNK), CHUNK)
                parts, norm = centred([halo[side, n, span, :] for n in range(1, 4)])
                source_out[pl.ds(first + c * CHUNK, CHUNK)] = by_leaf(source_terms(parts, norm)).astype(BF16)

    charge_out[0:LEAVES] = halo[0, 0]
    charge_out[2 * LEAVES : 3 * LEAVES] = halo[1, 0]

    pl.loop(early, chunks)(far_chunk)

    finish_stage(2)
    every_out[...] = every[...]

    for stage in range(len(STAGES)):
        for k in range(1, STAGES[stage][1]):
            every_copy(stage, k).wait_send()
    for copy in sum(copies_of_halo, []) + moments:
        copy.wait_send()


def local_kernel(
    source, target, charges, every, pairs_vmem, bases, transfer, near_first, far_total,
    cluster_target_hbm, group_target_hbm, top_target_hbm, cluster_transfer_hbm, cluster_coupling_hbm,
    group_coupling_hbm, group_transfer_hbm, top_coupling_hbm,
    out, near_total,
    parts, near_columns, cluster_transfer, cluster_coupling, group_coupling, group_transfer, top_coupling,
    group_moments, pairs, cluster_target, group_target, top_target,
    sems,
):
    gx = lax.axis_index("gx")
    top = gx // 4

    loads = [
        pltpu.make_async_copy(source_ref, landing, sems.at[n])
        for n, (source_ref, landing) in enumerate(
            (
                (pairs_vmem, pairs),
                (cluster_target_hbm, cluster_target),
                (group_target_hbm, group_target),
                (top_target_hbm, top_target),
                (cluster_transfer_hbm, cluster_transfer),
                (cluster_coupling_hbm, cluster_coupling),
                (group_coupling_hbm, group_coupling),
                (group_transfer_hbm, group_transfer),
                (top_coupling_hbm.at[top], top_coupling),
            )
        )
    ]
    for copy in loads:
        copy.start()

    for k in range(GROUP):
        parts[k] = jnp.zeros((POINTS, 128), F32)
    loads[0].wait()

    def add_parts(g):
        for k in range(GROUP):
            near_total[pairs[0, g * GROUP + k] // 256] += parts[k]

    def listed_group(g):
        add_parts(jnp.maximum(g - 1, 0))
        for k in range(GROUP):
            code = pairs[0, g * GROUP + k]
            i, j = code // 256, code % 256
            square = jnp.dot(target[i], source[j], preferred_element_type=F32)
            parts[k] = folded(square, charges[pl.ds(j, 1), :])

    groups = (pairs[1, 0] + GROUP - 1) // GROUP

    @pl.loop(0, groups)
    def _(g):
        listed_group(g)

    add_parts(jnp.maximum(groups - 1, 0))

    unit = eye()
    for copy in loads[1:]:
        copy.wait()

    quarter = DEVICES // 4
    group_moments[...] = sum(every[pl.ds(k * quarter, quarter), 0, :][:, RANK:] for k in range(4))
    def masked(t):
        return jnp.where(t >= 0, 1.0, 0.0).astype(F32), jnp.maximum(t, 0)

    total = jnp.zeros((RANK, RANK), F32)
    for f in range(4):
        weight, t = masked(top_target[f, top])
        lifted = jnp.zeros((RANK, RANK), F32)
        for k in range(4):
            g = 4 * t + k
            lifted = lifted + group_transfer[g] * to_column(group_moments[pl.ds(g, 1), :], unit)
        total = total + top_coupling[f] * (jnp.sum(lifted, axis=0, keepdims=True) * weight)
    top_local = to_row(jnp.sum(total, axis=1, keepdims=True), unit)
    total = group_transfer[gx] * top_local
    for f in range(8):
        weight, t = masked(group_target[0, f])
        total = total + group_coupling[0, f] * (group_moments[pl.ds(t, 1), :] * weight)
    group_local = to_row(jnp.sum(total, axis=1, keepdims=True), unit)
    total = cluster_transfer[0] * group_local
    for f in range(8):
        weight, t = masked(cluster_target[0, f])
        total = total + cluster_coupling[0, f] * (every[(t % 4) * quarter + t // 4, :, :RANK] * weight)
    cluster_local = to_row(jnp.sum(total, axis=1, keepdims=True), unit)

    near_columns[...] = jnp.zeros((POINTS, 128), F32)

    @pl.loop(0, LEAVES // CHUNK)
    def _(c):
        rows = []
        for k in range(CHUNK):
            i = c * CHUNK + k
            total = transfer[i] * cluster_local + far_total[i]
            leaf_local = jnp.sum(total, axis=1, keepdims=True)
            rows.append(jnp.sum(bases[i] * leaf_local, axis=0, keepdims=True))
        near_columns[...] += lane_sums(near_total.at[pl.ds(c * CHUNK, CHUNK)], c * CHUNK)
        out[pl.ds(pl.multiple_of(c * CHUNK, CHUNK), CHUNK), :] = jnp.concatenate(rows, axis=0)

    out[...] += near_columns[...].T[:LEAVES] * INVERSE_FOUR_PI


def local(
    charges, points, leaf_bases, leaf_transfer, near_target, far_target, leaf_coupling, cluster_transfer,
    cluster_target, cluster_coupling, group_transfer, group_target, group_coupling, top_target, top_coupling,
):
    vmem = pl.BlockSpec(memory_space=pltpu.VMEM)
    anywhere = pl.BlockSpec(memory_space=pl.ANY)
    dma = pltpu.SemaphoreType.DMA

    def in_hbm(*arrays):
        return [pltpu.with_memory_space_constraint(array, pltpu.HBM) for array in arrays]

    handed = pl.pallas_call(
        exchange_kernel,
        out_shape=(
            pltpu.VMEM((3 * LEAVES + 1, TERMS, POINTS), BF16),
            pltpu.VMEM((LEAVES, POINTS, TERMS), BF16),
            pltpu.VMEM((3 * LEAVES + 8, POINTS), F32),
            pltpu.VMEM((DEVICES, 1, 2 * RANK), F32),
            pltpu.VMEM((2, PAIRS + 128), jnp.int32),
            pltpu.VMEM((LEAVES, RANK, POINTS), F32),
            pltpu.VMEM((LEAVES, RANK, RANK), F32),
            pltpu.VMEM((LEAVES, POINTS, 128), F32),
            pltpu.VMEM((LEAVES, RANK, RANK), F32),
        ),
        in_specs=[anywhere] * 8,
        out_specs=[vmem] * 9,
        scratch_shapes=[
            pltpu.VMEM((LEAVES * FAR, RANK, RANK), F32),
            pltpu.VMEM((LEAVES, FAR), jnp.int32),
            pltpu.SMEM((LEAVES, FAR), jnp.int32),
            pltpu.VMEM((5 * LEAVES + 8, RANK), F32),
            pltpu.VMEM((8, 128), jnp.int32),
            pltpu.SMEM((8, 128), jnp.int32),
            pltpu.VMEM((4, LEAVES, POINTS), F32),
            pltpu.VMEM((NEAR, LEAVES), jnp.int32),
            pltpu.VMEM((FAR, LEAVES), jnp.int32),
            pltpu.VMEM((1, RANK, RANK), F32),
            pltpu.VMEM((2, 4, LEAVES, POINTS), F32),
            pltpu.VMEM((5, LEAVES // 2, 2 * RANK), F32),
            pltpu.VMEM((DEVICES, 1, 2 * RANK), F32),
            dma((LEAVES // CHUNK,)),
            dma,
            dma,
            dma((2, LEAVES // CHUNK)),
            dma((5,)),
            dma((HALO_PARTS, 2)),
            dma((HALO_PARTS, 2)),
            dma((4,)),
            dma((4,)),
            dma((len(STAGES), 8)),
            dma((len(STAGES), 8)),
        ],
        compiler_params=pltpu.CompilerParams(
            collective_id=0, has_side_effects=True, vmem_limit_bytes=36 << 20
        ),
        name="exchange",
    )(
        *in_hbm(
            charges,
            jnp.transpose(points, (1, 0, 2)),
            near_target.T,
            far_target.T,
            cluster_transfer,
            jnp.swapaxes(leaf_bases, 1, 2),
            leaf_transfer,
            leaf_coupling.reshape(LEAVES * FAR, RANK, RANK),
        )
    )
    return pl.pallas_call(
        local_kernel,
        out_shape=(jax.ShapeDtypeStruct((LEAVES, POINTS), F32), pltpu.VMEM((LEAVES, POINTS, 128), F32)),
        in_specs=[vmem] * 9 + [anywhere] * 8,
        out_specs=[vmem] * 2,
        input_output_aliases={7: 1},
        scratch_shapes=[
            pltpu.VMEM((GROUP, POINTS, 128), F32),
            pltpu.VMEM((POINTS, 128), F32),
            pltpu.VMEM((1, RANK, RANK), F32),
            pltpu.VMEM((1, 8, RANK, RANK), F32),
            pltpu.VMEM((1, 8, RANK, RANK), F32),
            pltpu.VMEM((32, RANK, RANK), F32),
            pltpu.VMEM((4, RANK, RANK), F32),
            pltpu.VMEM((32, RANK), F32),
            pltpu.SMEM((2, PAIRS + 128), jnp.int32),
            pltpu.SMEM((1, 8), jnp.int32),
            pltpu.SMEM((1, 8), jnp.int32),
            pltpu.SMEM((4, 8), jnp.int32),
            dma((9,)),
        ],
        compiler_params=pltpu.CompilerParams(vmem_limit_bytes=36 << 20),
        name="local",
    )(
        *[pltpu.with_memory_space_constraint(array, pltpu.VMEM) for array in handed],
        *in_hbm(
            cluster_target,
            group_target,
            top_target.T,
            cluster_transfer,
            cluster_coupling,
            group_coupling,
            group_transfer,
            top_coupling,
        ),
    )[0]


def solution(mesh):
    leaf = ("gx", "gy")
    return jax.shard_map(
        local,
        mesh=mesh,
        in_specs=(
            P(leaf, None),
            P(leaf, None, None),
            P(leaf, None, None),
            P(leaf, None, None),
            P(leaf, None),
            P(leaf, None),
            P(leaf, None, None, None),
            P(leaf, None, None),
            P(leaf, None),
            P(leaf, None, None, None),
            P(),
            P("gx", None),
            P("gx", None, None, None),
            P(),
            P(),
        ),
        out_specs=P(leaf, None),
        check_vma=False,
    )
```

```python
import functools
import math

import jax
import jax.numpy as jnp
from jax import lax
from jax.experimental import pallas as pl
from jax.experimental.pallas import tpu as pltpu
from jax.sharding import PartitionSpec as P

MESH = pl.DeviceIdType.MESH
F32 = jnp.float32
BF16 = jnp.bfloat16
SMOOTHING = 0.01
INVERSE_FOUR_PI = 1.0 / (4.0 * math.pi)

LEAVES = 64
POINTS = 256
RANK = 64
NEAR = 8
FAR = 16
TERMS = 32
PAIRS = LEAVES * NEAR
GROUP = 16
OWN = 2
CHUNK = 8
DEVICES = 128
STAGES = ((1, 8), (8, 4), (32, 4))
HALO_PARTS = 2
BLANK = 3 * LEAVES


def split3(value):
    high = value.astype(BF16).astype(F32)
    rest = value - high
    middle = rest.astype(BF16).astype(F32)
    low = (rest - middle).astype(BF16).astype(F32)
    return high, middle, low


def centred(points):
    shifted = [p - 1.0 for p in points]
    norm = shifted[0] * shifted[0] + shifted[1] * shifted[1] + shifted[2] * shifted[2]
    return [split3(u) for u in shifted], norm


def source_terms(parts, norm):
    rows = []
    for high, middle, low in parts:
        high, middle, low = -2.0 * high, -2.0 * middle, -2.0 * low
        rows += [high, high, high, middle, middle, low]
    one = jnp.ones_like(norm)
    return rows + list(split3(norm + SMOOTHING)) + [one, one, one]


def target_terms(parts, norm):
    rows = []
    for high, middle, low in parts:
        rows += [high, middle, low, high, middle, high]
    one = jnp.ones_like(norm)
    return rows + [one, one, one] + list(split3(norm))


def by_leaf(rows):
    blank = jnp.zeros_like(rows[0])
    return jnp.swapaxes(jnp.stack(rows + [blank] * (TERMS - len(rows)), axis=0), 0, 1)


def eye():
    shape = (RANK, RANK)
    return (lax.broadcasted_iota(jnp.int32, shape, 0) == lax.broadcasted_iota(jnp.int32, shape, 1)).astype(F32)


def to_column(row, unit):
    return jnp.sum(unit * row, axis=1, keepdims=True)


def to_row(column, unit):
    return jnp.sum(unit * column, axis=0, keepdims=True)


def lane_sums(parts, first):
    odd = lax.broadcasted_iota(jnp.int32, (POINTS, 128), 1) % 2
    source = lax.broadcasted_iota(jnp.int32, (256, 128), 0)
    column = lax.broadcasted_iota(jnp.int32, (256, 128), 1) - first
    total = None
    for k in range(0, CHUNK, 4):
        halves = []
        for n in (k, k + 2):
            here, there = parts[n], parts[n + 1]
            halves.append(jnp.where(odd == 0, here, there) + pltpu.roll(jnp.where(odd == 0, there, here), 127, axis=1))
        values = jnp.concatenate(halves, axis=1)
        high = values.astype(BF16)
        low = (values - high.astype(F32)).astype(BF16)
        ones = jnp.where(k + source // 128 * 2 + source % 2 == column, 1.0, 0.0).astype(BF16)
        for piece in (high, low):
            term = jnp.dot(piece, ones, preferred_element_type=F32)
            total = term if total is None else total + term
    return total


def folded(square, charge):
    weighted = lax.rsqrt(square) * charge
    return weighted[:, :128] + weighted[:, 128:]


def exchange_kernel(
    charges_hbm, points_hbm, near_hbm, far_hbm, cluster_transfer_hbm, bases_hbm, transfer_hbm, coupling_hbm,
    source_out, target_out, charge_out, every_out, pair_out, bases, transfer, near_out, far_out,
    coupling, far_vector, far_rows, moment_rows, choice_vector, choice, own, near, far, cluster_transfer, halo, window, every,
    coupling_sems, far_sem, choice_sem, load_sems, small_sems, halo_send, halo_recv, moment_send, moment_recv, every_send, every_recv,
):
    gx, gy = lax.axis_index("gx"), lax.axis_index("gy")
    device = gx * 4 + gy

    def place(index):
        return (index // 4, index % 4)

    def beside(distance):
        return place((device + distance + DEVICES) % DEVICES)

    chunks = LEAVES // CHUNK
    lower = device < DEVICES // 2
    sooner = jnp.where(lower, chunks, 0)
    own_limit = jnp.where(lower, OWN, 1)

    def load_copies(c):
        span = pl.ds(c * CHUNK, CHUNK)
        return (
            pltpu.make_async_copy(bases_hbm.at[span], bases.at[span], load_sems.at[0, c]),
            pltpu.make_async_copy(transfer_hbm.at[span], transfer.at[span], load_sems.at[1, c]),
        )

    small = [
        pltpu.make_async_copy(source, landing, small_sems.at[n])
        for n, (source, landing) in enumerate(
            (
                (charges_hbm, own.at[0]),
                (points_hbm, own.at[pl.ds(1, 3)]),
                (near_hbm, near),
                (far_hbm, far),
                (cluster_transfer_hbm, cluster_transfer),
            )
        )
    ]
    for copy in small:
        copy.start()

    @pl.loop(0, chunks)
    def _(c):
        for copy in load_copies(c):
            copy.start()

    def coupling_copy(c):
        span = pl.ds(c * CHUNK * FAR, CHUNK * FAR)
        return pltpu.make_async_copy(coupling_hbm.at[span], coupling.at[span], coupling_sems.at[c])

    @pl.loop(0, chunks)
    def _(c):
        coupling_copy(c).start()

    barrier = pltpu.get_barrier_semaphore()
    for distance in (1, -1, 2, -2):
        pl.semaphore_signal(barrier, inc=1, device_id=beside(distance), device_id_type=MESH)

    row = gy * (DEVICES // 4) + gx

    def mate(stage, k):
        unit, count = STAGES[stage]
        position = (row // unit) % count
        there = row + ((position + k) % count - position) * unit
        return (there % (DEVICES // 4), there // (DEVICES // 4))

    for stage in range(len(STAGES)):

        @pl.loop(1, STAGES[stage][1])
        def _(k):
            pl.semaphore_signal(barrier, inc=1, device_id=mate(stage, k), device_id_type=MESH)

    for copy in small:
        copy.wait()
    far_targets = far[...]
    far_vector[...] = jnp.where(far_targets >= 0, far_targets - (device - 2) * LEAVES, 5 * LEAVES).T
    far_copy = pltpu.make_async_copy(far_vector, far_rows, far_sem)
    far_copy.start()

    slots = near[...]
    local_slots = slots - device * LEAVES
    is_here = jnp.where((local_slots >= 0) & (local_slots < LEAVES), 1, 0)
    live_rows = []
    own_before = jnp.zeros((1, LEAVES), jnp.int32)
    chosen = [jnp.full((1, LEAVES), BLANK, jnp.int32) for _ in range(OWN)]
    for s in range(NEAR):
        is_own = is_here[s : s + 1] > 0
        for n in range(OWN):
            chosen[n] = jnp.where(is_own & (own_before == n) & (n < own_limit), local_slots[s : s + 1] + LEAVES, chosen[n])
        left = jnp.where(is_own & (own_before < own_limit), 0.0, 1.0)
        live_rows.append(jnp.where(slots[s : s + 1] >= 0, left, 0.0))
        own_before = own_before + is_here[s : s + 1]
    for n in range(OWN):
        choice_vector[n : n + 1, 0:LEAVES] = chosen[n]
    choice_copy = pltpu.make_async_copy(choice_vector, choice, choice_sem)
    choice_copy.start()
    live = jnp.concatenate(live_rows, axis=0)
    before = (
        lax.broadcasted_iota(jnp.int32, (LEAVES, LEAVES), 0) < lax.broadcasted_iota(jnp.int32, (LEAVES, LEAVES), 1)
    ).astype(BF16)
    rank_in_slot = jnp.dot(live.astype(BF16), before, preferred_element_type=F32)
    in_slot = jnp.sum(live, axis=1, keepdims=True)
    leaf_row = lax.broadcasted_iota(jnp.int32, (1, LEAVES), 1)
    code = (leaf_row * 256 + slots - (device - 1) * LEAVES).astype(F32)
    position_row = lax.broadcasted_iota(jnp.int32, (1, PAIRS), 1).astype(F32)
    found = jnp.zeros((LEAVES, PAIRS), F32)
    start = jnp.zeros((1, 1), F32)
    positions = []
    for s in range(NEAR):
        positions.append(jnp.where(live[s : s + 1] > 0, rank_in_slot[s : s + 1] + start, -1.0))
        start = start + in_slot[s : s + 1]
    table = jnp.concatenate(positions + [code], axis=0).T
    for s in range(NEAR):
        found = jnp.where(table[:, s : s + 1] == position_row, table[:, NEAR + s : NEAR + s + 1], found)
    pairs = jnp.sum(found, axis=0, keepdims=True)
    pair_out[0:1, 0:PAIRS] = jnp.where(position_row < start, pairs, float(BLANK)).astype(jnp.int32)
    pair_out[0:1, PAIRS:] = jnp.full((1, 128), BLANK, jnp.int32)
    pair_out[1:2, 0:128] = jnp.broadcast_to(start.astype(jnp.int32), (1, 128))
    def own_terms(c):
        span = pl.ds(pl.multiple_of(c * CHUNK, CHUNK), CHUNK)
        parts, norm = centred([own[n, span, :] for n in range(1, 4)])
        source_out[pl.ds(LEAVES + c * CHUNK, CHUNK)] = by_leaf(source_terms(parts, norm)).astype(BF16)
        target = by_leaf(target_terms(parts, norm)).astype(BF16)
        for k in range(CHUNK):
            target_out[c * CHUNK + k] = target[k].T

    pl.loop(0, sooner)(own_terms)
    charge_out[LEAVES : 2 * LEAVES] = own[0]
    charge_out[3 * LEAVES :] = jnp.zeros((8, POINTS), F32)
    term = lax.broadcasted_iota(jnp.int32, (TERMS, POINTS), 0)
    source_out[BLANK] = jnp.where(term == 18, 1.0, 0.0).astype(BF16)

    lane = lax.broadcasted_iota(jnp.int32, (RANK, LEAVES), 1)

    def moment_chunk(c, carry):
        columns, total = carry
        for copy in load_copies(c):
            copy.wait()
        weights = own[0, pl.ds(pl.multiple_of(c * CHUNK, CHUNK), CHUNK), :]
        for k in range(CHUNK):
            product = bases[c * CHUNK + k] * weights[k : k + 1, :]
            column = jnp.sum(product[:, :128] + product[:, 128:], axis=1, keepdims=True)
            columns = jnp.where(lane == c * CHUNK + k, column, columns)
            total = total + transfer[c * CHUNK + k] * column
        return columns, total

    carry = lax.fori_loop(
        0, sooner, moment_chunk, (jnp.zeros((RANK, LEAVES), F32), jnp.zeros((RANK, RANK), F32))
    )
    pl.semaphore_wait(barrier, 4 + sum(count - 1 for _, count in STAGES))

    part_leaves = LEAVES // HALO_PARTS
    copies_of_halo = [
        [
            pltpu.make_async_remote_copy(
                src_ref=own.at[:, pl.ds(part * part_leaves, part_leaves)],
                dst_ref=halo.at[side, :, pl.ds(part * part_leaves, part_leaves)],
                send_sem=halo_send.at[part, side],
                recv_sem=halo_recv.at[part, side],
                device_id=beside(distance),
                device_id_type=MESH,
            )
            for side, distance in ((0, 1), (1, -1))
        ]
        for part in range(HALO_PARTS)
    ]
    for copy in copies_of_halo[0]:
        copy.start()

    columns, total = lax.fori_loop(sooner, chunks, moment_chunk, carry)
    rows = columns.T
    window[2] = jnp.concatenate([rows[: LEAVES // 2], rows[LEAVES // 2 :]], axis=1)
    unit = eye()
    cluster_row = jnp.sum(total, axis=0, keepdims=True)
    lifted_row = jnp.sum(cluster_transfer[0] * to_column(cluster_row, unit), axis=0, keepdims=True)
    every[row, 0:1, 0:RANK] = cluster_row
    every[row, 0:1, RANK : 2 * RANK] = lifted_row

    def every_copy(stage, k):
        unit, _ = STAGES[stage]
        rows = pl.ds((row // unit) * unit, unit)
        return pltpu.make_async_remote_copy(
            src_ref=every.at[rows],
            dst_ref=every.at[rows],
            send_sem=every_send.at[stage, k],
            recv_sem=every_recv.at[stage, k],
            device_id=mate(stage, k),
            device_id_type=MESH,
        )

    def start_stage(stage):
        for k in range(1, STAGES[stage][1]):
            every_copy(stage, k).start()

    def finish_stage(stage):
        for k in range(1, STAGES[stage][1]):
            every_copy(stage, k).wait_recv()

    start_stage(0)

    def moment_copies():
        copies = []
        for n, distance in enumerate((2, 1, -1, -2)):
            slot = (0, 1, 3, 4)[n]
            copies.append(
                pltpu.make_async_remote_copy(
                    src_ref=window.at[2],
                    dst_ref=window.at[slot],
                    send_sem=moment_send.at[n],
                    recv_sem=moment_recv.at[n],
                    device_id=beside(distance),
                    device_id_type=MESH,
                )
            )
        return copies

    moments = moment_copies()
    for copy in moments:
        copy.start()
    for copies in copies_of_halo[1:]:
        for copy in copies:
            copy.start()

    pl.loop(sooner, chunks)(own_terms)

    choice_copy.wait()

    for n in range(OWN):

        @pl.loop(0, LEAVES // GROUP if n == 0 else jnp.where(lower, LEAVES // GROUP, 0))
        def _(g):
            for k in range(GROUP):
                i = g * GROUP + k
                j = jnp.clip(choice[n, i], 0, BLANK)
                square = jnp.dot(target_out[i], source_out[j], preferred_element_type=F32)
                part = folded(square, charge_out[pl.ds(j, 1), :])
                if n == 0:
                    near_out[i] = part
                else:
                    near_out[i] += part

            if n == 0:

                @pl.when(g == 1)
                def _():
                    finish_stage(0)
                    start_stage(1)

    for copy in moments:
        copy.wait_recv()
    for n in range(5):
        moment_rows[n * LEAVES : n * LEAVES + LEAVES // 2] = window[n][:, :RANK]
        moment_rows[n * LEAVES + LEAVES // 2 : (n + 1) * LEAVES] = window[n][:, RANK:]
    moment_rows[5 * LEAVES :] = jnp.zeros((8, RANK), F32)
    far_copy.wait()

    def far_chunk(c):
        coupling_copy(c).wait()
        for k in range(CHUNK):
            i = c * CHUNK + k
            total = None
            for f in range(FAR):
                slot = jnp.clip(far_rows[i, f], 0, 5 * LEAVES)
                term = coupling[i * FAR + f] * moment_rows[pl.ds(slot, 1), :]
                total = term if total is None else total + term
            far_out[i] = total

    def far_chunks(first, last):
        pl.loop(first, last)(far_chunk)

    far_chunks(0, 3)
    finish_stage(1)
    start_stage(2)
    far_chunks(3, 5)

    for part in range(HALO_PARTS):
        for side in range(2):
            copies_of_halo[part][side].wait_recv()
            first = 2 * LEAVES * side

            @pl.loop(part * part_leaves // CHUNK, (part + 1) * part_leaves // CHUNK)
            def _(c):
                span = pl.ds(pl.multiple_of(c * CHUNK, CHUNK), CHUNK)
                parts, norm = centred([halo[side, n, span, :] for n in range(1, 4)])
                source_out[pl.ds(first + c * CHUNK, CHUNK)] = by_leaf(source_terms(parts, norm)).astype(BF16)

    charge_out[0:LEAVES] = halo[0, 0]
    charge_out[2 * LEAVES : 3 * LEAVES] = halo[1, 0]

    far_chunks(5, chunks)

    finish_stage(2)
    every_out[...] = every[...]

    for stage in range(len(STAGES)):
        for k in range(1, STAGES[stage][1]):
            every_copy(stage, k).wait_send()
    for copy in sum(copies_of_halo, []) + moments:
        copy.wait_send()


def local_kernel(
    source, target, charges, every, pairs_vmem, bases, transfer, near_first, far_total,
    cluster_target_hbm, group_target_hbm, top_target_hbm, cluster_transfer_hbm, cluster_coupling_hbm,
    group_coupling_hbm, group_transfer_hbm, top_coupling_hbm,
    out, near_total,
    parts, near_columns, cluster_transfer, cluster_coupling, group_coupling, group_transfer, top_coupling,
    group_moments, pairs, cluster_target, group_target, top_target,
    sems,
):
    gx = lax.axis_index("gx")
    top = gx // 4

    loads = [
        pltpu.make_async_copy(source_ref, landing, sems.at[n])
        for n, (source_ref, landing) in enumerate(
            (
                (pairs_vmem, pairs),
                (cluster_target_hbm, cluster_target),
                (group_target_hbm, group_target),
                (top_target_hbm, top_target),
                (cluster_transfer_hbm, cluster_transfer),
                (cluster_coupling_hbm, cluster_coupling),
                (group_coupling_hbm, group_coupling),
                (group_transfer_hbm, group_transfer),
                (top_coupling_hbm.at[top], top_coupling),
            )
        )
    ]
    for copy in loads:
        copy.start()

    for k in range(GROUP):
        parts[k] = jnp.zeros((POINTS, 128), F32)
    loads[0].wait()

    def add_parts(g):
        for k in range(GROUP):
            near_total[pairs[0, g * GROUP + k] // 256] += parts[k]

    def listed_group(g):
        add_parts(jnp.maximum(g - 1, 0))
        for k in range(GROUP):
            code = pairs[0, g * GROUP + k]
            i, j = code // 256, code % 256
            square = jnp.dot(target[i], source[j], preferred_element_type=F32)
            parts[k] = folded(square, charges[pl.ds(j, 1), :])

    groups = (pairs[1, 0] + GROUP - 1) // GROUP

    @pl.loop(0, groups)
    def _(g):
        listed_group(g)

    add_parts(jnp.maximum(groups - 1, 0))

    unit = eye()
    for copy in loads[1:]:
        copy.wait()

    quarter = DEVICES // 4
    group_moments[...] = sum(every[pl.ds(k * quarter, quarter), 0, :][:, RANK:] for k in range(4))
    def masked(t):
        return jnp.where(t >= 0, 1.0, 0.0).astype(F32), jnp.maximum(t, 0)

    total = jnp.zeros((RANK, RANK), F32)
    for f in range(4):
        weight, t = masked(top_target[f, top])
        lifted = jnp.zeros((RANK, RANK), F32)
        for k in range(4):
            g = 4 * t + k
            lifted = lifted + group_transfer[g] * to_column(group_moments[pl.ds(g, 1), :], unit)
        total = total + top_coupling[f] * (jnp.sum(lifted, axis=0, keepdims=True) * weight)
    top_local = to_row(jnp.sum(total, axis=1, keepdims=True), unit)
    total = group_transfer[gx] * top_local
    for f in range(8):
        weight, t = masked(group_target[0, f])
        total = total + group_coupling[0, f] * (group_moments[pl.ds(t, 1), :] * weight)
    group_local = to_row(jnp.sum(total, axis=1, keepdims=True), unit)
    total = cluster_transfer[0] * group_local
    for f in range(8):
        weight, t = masked(cluster_target[0, f])
        total = total + cluster_coupling[0, f] * (every[(t % 4) * quarter + t // 4, :, :RANK] * weight)
    cluster_local = to_row(jnp.sum(total, axis=1, keepdims=True), unit)

    near_columns[...] = jnp.zeros((POINTS, 128), F32)

    @pl.loop(0, LEAVES // CHUNK)
    def _(c):
        rows = []
        for k in range(CHUNK):
            i = c * CHUNK + k
            total = transfer[i] * cluster_local + far_total[i]
            leaf_local = jnp.sum(total, axis=1, keepdims=True)
            rows.append(jnp.sum(bases[i] * leaf_local, axis=0, keepdims=True))
        near_columns[...] += lane_sums(near_total.at[pl.ds(c * CHUNK, CHUNK)], c * CHUNK)
        out[pl.ds(pl.multiple_of(c * CHUNK, CHUNK), CHUNK), :] = jnp.concatenate(rows, axis=0)

    out[...] += near_columns[...].T[:LEAVES] * INVERSE_FOUR_PI


def local(
    charges, points, leaf_bases, leaf_transfer, near_target, far_target, leaf_coupling, cluster_transfer,
    cluster_target, cluster_coupling, group_transfer, group_target, group_coupling, top_target, top_coupling,
):
    vmem = pl.BlockSpec(memory_space=pltpu.VMEM)
    anywhere = pl.BlockSpec(memory_space=pl.ANY)
    dma = pltpu.SemaphoreType.DMA

    def in_hbm(*arrays):
        return [pltpu.with_memory_space_constraint(array, pltpu.HBM) for array in arrays]

    handed = pl.pallas_call(
        exchange_kernel,
        out_shape=(
            pltpu.VMEM((3 * LEAVES + 1, TERMS, POINTS), BF16),
            pltpu.VMEM((LEAVES, POINTS, TERMS), BF16),
            pltpu.VMEM((3 * LEAVES + 8, POINTS), F32),
            pltpu.VMEM((DEVICES, 1, 2 * RANK), F32),
            pltpu.VMEM((2, PAIRS + 128), jnp.int32),
            pltpu.VMEM((LEAVES, RANK, POINTS), F32),
            pltpu.VMEM((LEAVES, RANK, RANK), F32),
            pltpu.VMEM((LEAVES, POINTS, 128), F32),
            pltpu.VMEM((LEAVES, RANK, RANK), F32),
        ),
        in_specs=[anywhere] * 8,
        out_specs=[vmem] * 9,
        scratch_shapes=[
            pltpu.VMEM((LEAVES * FAR, RANK, RANK), F32),
            pltpu.VMEM((LEAVES, FAR), jnp.int32),
            pltpu.SMEM((LEAVES, FAR), jnp.int32),
            pltpu.VMEM((5 * LEAVES + 8, RANK), F32),
            pltpu.VMEM((8, 128), jnp.int32),
            pltpu.SMEM((8, 128), jnp.int32),
            pltpu.VMEM((4, LEAVES, POINTS), F32),
            pltpu.VMEM((NEAR, LEAVES), jnp.int32),
            pltpu.VMEM((FAR, LEAVES), jnp.int32),
            pltpu.VMEM((1, RANK, RANK), F32),
            pltpu.VMEM((2, 4, LEAVES, POINTS), F32),
            pltpu.VMEM((5, LEAVES // 2, 2 * RANK), F32),
            pltpu.VMEM((DEVICES, 1, 2 * RANK), F32),
            dma((LEAVES // CHUNK,)),
            dma,
            dma,
            dma((2, LEAVES // CHUNK)),
            dma((5,)),
            dma((HALO_PARTS, 2)),
            dma((HALO_PARTS, 2)),
            dma((4,)),
            dma((4,)),
            dma((len(STAGES), 8)),
            dma((len(STAGES), 8)),
        ],
        compiler_params=pltpu.CompilerParams(
            collective_id=0, has_side_effects=True, vmem_limit_bytes=36 << 20
        ),
        name="exchange",
    )(
        *in_hbm(
            charges,
            jnp.transpose(points, (1, 0, 2)),
            near_target.T,
            far_target.T,
            cluster_transfer,
            jnp.swapaxes(leaf_bases, 1, 2),
            leaf_transfer,
            leaf_coupling.reshape(LEAVES * FAR, RANK, RANK),
        )
    )
    return pl.pallas_call(
        local_kernel,
        out_shape=(jax.ShapeDtypeStruct((LEAVES, POINTS), F32), pltpu.VMEM((LEAVES, POINTS, 128), F32)),
        in_specs=[vmem] * 9 + [anywhere] * 8,
        out_specs=[vmem] * 2,
        input_output_aliases={7: 1},
        scratch_shapes=[
            pltpu.VMEM((GROUP, POINTS, 128), F32),
            pltpu.VMEM((POINTS, 128), F32),
            pltpu.VMEM((1, RANK, RANK), F32),
            pltpu.VMEM((1, 8, RANK, RANK), F32),
            pltpu.VMEM((1, 8, RANK, RANK), F32),
            pltpu.VMEM((32, RANK, RANK), F32),
            pltpu.VMEM((4, RANK, RANK), F32),
            pltpu.VMEM((32, RANK), F32),
            pltpu.SMEM((2, PAIRS + 128), jnp.int32),
            pltpu.SMEM((1, 8), jnp.int32),
            pltpu.SMEM((1, 8), jnp.int32),
            pltpu.SMEM((4, 8), jnp.int32),
            dma((9,)),
        ],
        compiler_params=pltpu.CompilerParams(vmem_limit_bytes=36 << 20),
        name="local",
    )(
        *[pltpu.with_memory_space_constraint(array, pltpu.VMEM) for array in handed],
        *in_hbm(
            cluster_target,
            group_target,
            top_target.T,
            cluster_transfer,
            cluster_coupling,
            group_coupling,
            group_transfer,
            top_coupling,
        ),
    )[0]


def solution(mesh):
    leaf = ("gx", "gy")
    return jax.shard_map(
        local,
        mesh=mesh,
        in_specs=(
            P(leaf, None),
            P(leaf, None, None),
            P(leaf, None, None),
            P(leaf, None, None),
            P(leaf, None),
            P(leaf, None),
            P(leaf, None, None, None),
            P(leaf, None, None),
            P(leaf, None),
            P(leaf, None, None, None),
            P(),
            P("gx", None),
            P("gx", None, None, None),
            P(),
            P(),
        ),
        out_specs=P(leaf, None),
        check_vma=False,
    )
```

```python
import functools
import math

import jax
import jax.numpy as jnp
from jax import lax
from jax.experimental import pallas as pl
from jax.experimental.pallas import tpu as pltpu
from jax.sharding import PartitionSpec as P

MESH = pl.DeviceIdType.MESH
F32 = jnp.float32
BF16 = jnp.bfloat16
SMOOTHING = 0.01
INVERSE_FOUR_PI = 1.0 / (4.0 * math.pi)

LEAVES = 64
POINTS = 256
RANK = 64
NEAR = 8
FAR = 16
TERMS = 32
PAIRS = LEAVES * NEAR
GROUP = 32
LAST_GROUP = 16
EXCHANGED = 48
OWN = 2
CHUNK = 8
DEVICES = 128
STAGES = ((1, 8), (8, 4), (32, 4))
HALO_PARTS = 2
BLANK = 3 * LEAVES


def split3(value):
    high = value.astype(BF16).astype(F32)
    rest = value - high
    middle = rest.astype(BF16).astype(F32)
    low = (rest - middle).astype(BF16).astype(F32)
    return high, middle, low


def centred(points):
    shifted = [p - 1.0 for p in points]
    norm = shifted[0] * shifted[0] + shifted[1] * shifted[1] + shifted[2] * shifted[2]
    return [split3(u) for u in shifted], norm


def source_terms(parts, norm):
    rows = []
    for high, middle, low in parts:
        high, middle, low = -2.0 * high, -2.0 * middle, -2.0 * low
        rows += [high, high, high, middle, middle, low]
    one = jnp.ones_like(norm)
    return rows + list(split3(norm + SMOOTHING)) + [one, one, one]


def target_terms(parts, norm):
    rows = []
    for high, middle, low in parts:
        rows += [high, middle, low, high, middle, high]
    one = jnp.ones_like(norm)
    return rows + [one, one, one] + list(split3(norm))


def by_leaf(rows):
    blank = jnp.zeros_like(rows[0])
    return jnp.swapaxes(jnp.stack(rows + [blank] * (TERMS - len(rows)), axis=0), 0, 1)


def eye():
    shape = (RANK, RANK)
    return (lax.broadcasted_iota(jnp.int32, shape, 0) == lax.broadcasted_iota(jnp.int32, shape, 1)).astype(F32)


def to_column(row, unit):
    return jnp.sum(unit * row, axis=1, keepdims=True)


def to_row(column, unit):
    return jnp.sum(unit * column, axis=0, keepdims=True)


def lane_sums(parts, first):
    odd = lax.broadcasted_iota(jnp.int32, (POINTS, 128), 1) % 2
    source = lax.broadcasted_iota(jnp.int32, (256, 128), 0)
    column = lax.broadcasted_iota(jnp.int32, (256, 128), 1) - first
    total = None
    for k in range(0, CHUNK, 4):
        halves = []
        for n in (k, k + 2):
            here, there = parts[n], parts[n + 1]
            halves.append(jnp.where(odd == 0, here, there) + pltpu.roll(jnp.where(odd == 0, there, here), 127, axis=1))
        values = jnp.concatenate(halves, axis=1)
        high = values.astype(BF16)
        low = (values - high.astype(F32)).astype(BF16)
        ones = jnp.where(k + source // 128 * 2 + source % 2 == column, 1.0, 0.0).astype(BF16)
        for piece in (high, low):
            term = jnp.dot(piece, ones, preferred_element_type=F32)
            total = term if total is None else total + term
    return total


def folded(square, charge):
    weighted = lax.rsqrt(square) * charge
    return weighted[:, :128] + weighted[:, 128:]


def exchange_kernel(
    charges_hbm, points_hbm, near_hbm, far_hbm, cluster_transfer_hbm, bases_hbm, transfer_hbm, coupling_hbm,
    source_out, target_out, charge_out, every_out, pair_out, bases, transfer, near_out, far_out, far_vector, moment_rows,
    coupling, far_rows, choice_vector, choice, own, near, far, cluster_transfer, halo, window, every,
    coupling_sems, far_sem, choice_sem, load_sems, small_sems, halo_send, halo_recv, moment_send, moment_recv, every_send, every_recv,
):
    gx, gy = lax.axis_index("gx"), lax.axis_index("gy")
    device = gx * 4 + gy

    def place(index):
        return (index // 4, index % 4)

    def beside(distance):
        return place((device + distance + DEVICES) % DEVICES)

    chunks = LEAVES // CHUNK
    lateness = (gx // 2) % 4 + gx // 8 + 2 * gy
    terms_before = jnp.where(lateness <= 6, chunks, 0)
    moments_before = jnp.where(lateness <= 4, chunks, 0)
    own_limit = jnp.where(lateness <= 8, OWN, 1)

    def load_copies(c):
        span = pl.ds(c * CHUNK, CHUNK)
        return (
            pltpu.make_async_copy(bases_hbm.at[span], bases.at[span], load_sems.at[0, c]),
            pltpu.make_async_copy(transfer_hbm.at[span], transfer.at[span], load_sems.at[1, c]),
        )

    small = [
        pltpu.make_async_copy(source, landing, small_sems.at[n])
        for n, (source, landing) in enumerate(
            (
                (charges_hbm, own.at[0]),
                (points_hbm, own.at[pl.ds(1, 3)]),
                (near_hbm, near),
                (far_hbm, far),
                (cluster_transfer_hbm, cluster_transfer),
            )
        )
    ]
    for copy in small:
        copy.start()

    @pl.loop(0, chunks)
    def _(c):
        for copy in load_copies(c):
            copy.start()

    def coupling_copy(c):
        span = pl.ds(c * CHUNK * FAR, CHUNK * FAR)
        return pltpu.make_async_copy(coupling_hbm.at[span], coupling.at[span], coupling_sems.at[c])

    far_chunk_count = EXCHANGED // CHUNK

    @pl.loop(0, far_chunk_count)
    def _(c):
        coupling_copy(c).start()

    barrier = pltpu.get_barrier_semaphore()
    for distance in (1, -1, 2, -2):
        pl.semaphore_signal(barrier, inc=1, device_id=beside(distance), device_id_type=MESH)

    row = gy * (DEVICES // 4) + gx

    def mate(stage, k):
        unit, count = STAGES[stage]
        position = (row // unit) % count
        there = row + ((position + k) % count - position) * unit
        return (there % (DEVICES // 4), there // (DEVICES // 4))

    for stage in range(len(STAGES)):

        @pl.loop(1, STAGES[stage][1])
        def _(k):
            pl.semaphore_signal(barrier, inc=1, device_id=mate(stage, k), device_id_type=MESH)

    for copy in small:
        copy.wait()
    far_targets = far[...]
    far_vector[...] = jnp.where(far_targets >= 0, far_targets - (device - 2) * LEAVES, 5 * LEAVES).T
    far_copy = pltpu.make_async_copy(far_vector, far_rows, far_sem)
    far_copy.start()

    slots = near[...]
    local_slots = slots - device * LEAVES
    is_here = jnp.where((local_slots >= 0) & (local_slots < LEAVES), 1, 0)
    live_rows = []
    own_before = jnp.zeros((1, LEAVES), jnp.int32)
    chosen = [jnp.full((1, LEAVES), BLANK, jnp.int32) for _ in range(OWN)]
    for s in range(NEAR):
        is_own = is_here[s : s + 1] > 0
        for n in range(OWN):
            chosen[n] = jnp.where(is_own & (own_before == n) & (n < own_limit), local_slots[s : s + 1] + LEAVES, chosen[n])
        left = jnp.where(is_own & (own_before < own_limit), 0.0, 1.0)
        live_rows.append(jnp.where(slots[s : s + 1] >= 0, left, 0.0))
        own_before = own_before + is_here[s : s + 1]
    for n in range(OWN):
        choice_vector[n : n + 1, 0:LEAVES] = chosen[n]
    choice_copy = pltpu.make_async_copy(choice_vector, choice, choice_sem)
    choice_copy.start()
    live = jnp.concatenate(live_rows, axis=0)
    before = (
        lax.broadcasted_iota(jnp.int32, (LEAVES, LEAVES), 0) < lax.broadcasted_iota(jnp.int32, (LEAVES, LEAVES), 1)
    ).astype(BF16)
    rank_in_slot = jnp.dot(live.astype(BF16), before, preferred_element_type=F32)
    in_slot = jnp.sum(live, axis=1, keepdims=True)
    leaf_row = lax.broadcasted_iota(jnp.int32, (1, LEAVES), 1)
    code = (leaf_row * 256 + slots - (device - 1) * LEAVES).astype(F32)
    position_row = lax.broadcasted_iota(jnp.int32, (1, PAIRS), 1).astype(F32)
    found = jnp.zeros((LEAVES, PAIRS), F32)
    start = jnp.zeros((1, 1), F32)
    positions = []
    for s in range(NEAR):
        positions.append(jnp.where(live[s : s + 1] > 0, rank_in_slot[s : s + 1] + start, -1.0))
        start = start + in_slot[s : s + 1]
    table = jnp.concatenate(positions + [code], axis=0).T
    for s in range(NEAR):
        found = jnp.where(table[:, s : s + 1] == position_row, table[:, NEAR + s : NEAR + s + 1], found)
    pairs = jnp.sum(found, axis=0, keepdims=True)
    pair_out[0:1, 0:PAIRS] = jnp.where(position_row < start, pairs, float(BLANK)).astype(jnp.int32)
    pair_out[0:1, PAIRS:] = jnp.full((1, 128), BLANK, jnp.int32)
    pair_out[1:2, 0:128] = jnp.broadcast_to(start.astype(jnp.int32), (1, 128))
    def own_terms(c):
        span = pl.ds(pl.multiple_of(c * CHUNK, CHUNK), CHUNK)
        parts, norm = centred([own[n, span, :] for n in range(1, 4)])
        source_out[pl.ds(LEAVES + c * CHUNK, CHUNK)] = by_leaf(source_terms(parts, norm)).astype(BF16)
        target = by_leaf(target_terms(parts, norm)).astype(BF16)
        for k in range(CHUNK):
            target_out[c * CHUNK + k] = target[k].T

    pl.loop(0, terms_before)(own_terms)
    charge_out[LEAVES : 2 * LEAVES] = own[0]
    charge_out[3 * LEAVES :] = jnp.zeros((8, POINTS), F32)
    term = lax.broadcasted_iota(jnp.int32, (TERMS, POINTS), 0)
    source_out[BLANK] = jnp.where(term == 18, 1.0, 0.0).astype(BF16)

    lane = lax.broadcasted_iota(jnp.int32, (RANK, LEAVES), 1)

    def moment_chunk(c, carry):
        columns, total = carry
        for copy in load_copies(c):
            copy.wait()
        weights = own[0, pl.ds(pl.multiple_of(c * CHUNK, CHUNK), CHUNK), :]
        for k in range(CHUNK):
            product = bases[c * CHUNK + k] * weights[k : k + 1, :]
            column = jnp.sum(product[:, :128] + product[:, 128:], axis=1, keepdims=True)
            columns = jnp.where(lane == c * CHUNK + k, column, columns)
            total = total + transfer[c * CHUNK + k] * column
        return columns, total

    carry = lax.fori_loop(
        0, moments_before, moment_chunk, (jnp.zeros((RANK, LEAVES), F32), jnp.zeros((RANK, RANK), F32))
    )
    pl.semaphore_wait(barrier, 4 + sum(count - 1 for _, count in STAGES))

    part_leaves = LEAVES // HALO_PARTS
    copies_of_halo = [
        [
            pltpu.make_async_remote_copy(
                src_ref=own.at[:, pl.ds(part * part_leaves, part_leaves)],
                dst_ref=halo.at[side, :, pl.ds(part * part_leaves, part_leaves)],
                send_sem=halo_send.at[part, side],
                recv_sem=halo_recv.at[part, side],
                device_id=beside(distance),
                device_id_type=MESH,
            )
            for side, distance in ((0, 1), (1, -1))
        ]
        for part in range(HALO_PARTS)
    ]
    for copy in copies_of_halo[0]:
        copy.start()

    columns, total = lax.fori_loop(moments_before, chunks, moment_chunk, carry)
    rows = columns.T
    window[2] = jnp.concatenate([rows[: LEAVES // 2], rows[LEAVES // 2 :]], axis=1)
    unit = eye()
    cluster_row = jnp.sum(total, axis=0, keepdims=True)
    lifted_row = jnp.sum(cluster_transfer[0] * to_column(cluster_row, unit), axis=0, keepdims=True)
    every[row, 0:1, 0:RANK] = cluster_row
    every[row, 0:1, RANK : 2 * RANK] = lifted_row

    def every_copy(stage, k):
        unit, _ = STAGES[stage]
        rows = pl.ds((row // unit) * unit, unit)
        return pltpu.make_async_remote_copy(
            src_ref=every.at[rows],
            dst_ref=every.at[rows],
            send_sem=every_send.at[stage, k],
            recv_sem=every_recv.at[stage, k],
            device_id=mate(stage, k),
            device_id_type=MESH,
        )

    def start_stage(stage):
        for k in range(1, STAGES[stage][1]):
            every_copy(stage, k).start()

    def finish_stage(stage):
        for k in range(1, STAGES[stage][1]):
            every_copy(stage, k).wait_recv()

    start_stage(0)

    def moment_copies():
        copies = []
        for n, distance in enumerate((2, 1, -1, -2)):
            slot = (0, 1, 3, 4)[n]
            copies.append(
                pltpu.make_async_remote_copy(
                    src_ref=window.at[2],
                    dst_ref=window.at[slot],
                    send_sem=moment_send.at[n],
                    recv_sem=moment_recv.at[n],
                    device_id=beside(distance),
                    device_id_type=MESH,
                )
            )
        return copies

    moments = moment_copies()
    for copy in moments:
        copy.start()
    for copies in copies_of_halo[1:]:
        for copy in copies:
            copy.start()

    pl.loop(terms_before, chunks)(own_terms)

    choice_copy.wait()

    for n in range(OWN):

        @pl.loop(0, LEAVES // GROUP if n == 0 else jnp.where(own_limit > n, LEAVES // GROUP, 0))
        def _(g):
            for k in range(GROUP):
                i = g * GROUP + k
                j = jnp.clip(choice[n, i], 0, BLANK)
                square = jnp.dot(target_out[i], source_out[j], preferred_element_type=F32)
                part = folded(square, charge_out[pl.ds(j, 1), :])
                if n == 0:
                    near_out[i] = part
                else:
                    near_out[i] += part

            if n == 0:

                @pl.when(g == 0)
                def _():
                    finish_stage(0)
                    start_stage(1)

    for copy in moments:
        copy.wait_recv()
    for n in range(5):
        moment_rows[n * LEAVES : n * LEAVES + LEAVES // 2] = window[n][:, :RANK]
        moment_rows[n * LEAVES + LEAVES // 2 : (n + 1) * LEAVES] = window[n][:, RANK:]
    moment_rows[5 * LEAVES :] = jnp.zeros((8, RANK), F32)
    far_copy.wait()

    def far_chunk(c):
        coupling_copy(c).wait()
        for k in range(CHUNK):
            i = c * CHUNK + k
            total = None
            for f in range(FAR):
                slot = jnp.clip(far_rows[i, f], 0, 5 * LEAVES)
                term = coupling[i * FAR + f] * moment_rows[pl.ds(slot, 1), :]
                total = term if total is None else total + term
            far_out[i] = total

    def far_chunks(first, last):
        pl.loop(first, last)(far_chunk)

    far_chunks(0, 2)
    finish_stage(1)
    start_stage(2)
    far_chunks(2, 4)

    for part in range(HALO_PARTS):
        for side in range(2):
            copies_of_halo[part][side].wait_recv()
            first = 2 * LEAVES * side

            @pl.loop(part * part_leaves // CHUNK, (part + 1) * part_leaves // CHUNK)
            def _(c):
                span = pl.ds(pl.multiple_of(c * CHUNK, CHUNK), CHUNK)
                parts, norm = centred([halo[side, n, span, :] for n in range(1, 4)])
                source_out[pl.ds(first + c * CHUNK, CHUNK)] = by_leaf(source_terms(parts, norm)).astype(BF16)

    charge_out[0:LEAVES] = halo[0, 0]
    charge_out[2 * LEAVES : 3 * LEAVES] = halo[1, 0]

    far_chunks(4, far_chunk_count)

    finish_stage(2)
    every_out[...] = every[...]

    for stage in range(len(STAGES)):
        for k in range(1, STAGES[stage][1]):
            every_copy(stage, k).wait_send()
    for copy in sum(copies_of_halo, []) + moments:
        copy.wait_send()


def local_kernel(
    source, target, charges, every, pairs_vmem, bases, transfer, near_first, far_first, far_vmem, moments,
    cluster_target_hbm, group_target_hbm, top_target_hbm, cluster_transfer_hbm, cluster_coupling_hbm,
    group_coupling_hbm, group_transfer_hbm, top_coupling_hbm, coupling_hbm,
    out, near_total, far_total,
    coupling, far_rows, parts, near_columns, cluster_transfer, cluster_coupling, group_coupling, group_transfer, top_coupling,
    group_moments, pairs, cluster_target, group_target, top_target,
    sems,
):
    gx = lax.axis_index("gx")
    top = gx // 4

    loads = [
        pltpu.make_async_copy(source_ref, landing, sems.at[n])
        for n, (source_ref, landing) in enumerate(
            (
                (pairs_vmem, pairs),
                (far_vmem, far_rows),
                (cluster_target_hbm, cluster_target),
                (group_target_hbm, group_target),
                (top_target_hbm, top_target),
                (cluster_transfer_hbm, cluster_transfer),
                (cluster_coupling_hbm, cluster_coupling),
                (group_coupling_hbm, group_coupling),
                (group_transfer_hbm, group_transfer),
                (top_coupling_hbm.at[top], top_coupling),
                (coupling_hbm.at[pl.ds(EXCHANGED * FAR, (LEAVES - EXCHANGED) * FAR)], coupling),
            )
        )
    ]
    for copy in loads:
        copy.start()

    for k in range(GROUP):
        parts[k] = jnp.zeros((POINTS, 128), F32)
    loads[0].wait()

    def add_parts(first, count):
        for k in range(count):
            near_total[pairs[0, first + k] // 256] += parts[k]

    def listed_pairs(first, count):
        for k in range(count):
            code = pairs[0, first + k]
            i, j = code // 256, code % 256
            square = jnp.dot(target[i], source[j], preferred_element_type=F32)
            parts[k] = folded(square, charges[pl.ds(j, 1), :])

    live = pairs[1, 0]
    groups = (live + GROUP - LAST_GROUP - 1) // GROUP

    @pl.loop(0, groups)
    def _(g):
        add_parts(jnp.maximum(g - 1, 0) * GROUP, GROUP)
        listed_pairs(g * GROUP, GROUP)

    add_parts(jnp.maximum(groups - 1, 0) * GROUP, GROUP)

    @pl.when(live > groups * GROUP)
    def _():
        listed_pairs(groups * GROUP, LAST_GROUP)
        add_parts(groups * GROUP, LAST_GROUP)

    unit = eye()
    for copy in loads[1:]:
        copy.wait()

    @pl.loop(0, (LEAVES - EXCHANGED) // CHUNK)
    def _(c):
        for k in range(CHUNK):
            i = c * CHUNK + k
            total = None
            for f in range(FAR):
                term = coupling[i * FAR + f] * moments[pl.ds(far_rows[EXCHANGED + i, f], 1), :]
                total = term if total is None else total + term
            far_total[EXCHANGED + i] = total


    quarter = DEVICES // 4
    group_moments[...] = sum(every[pl.ds(k * quarter, quarter), 0, :][:, RANK:] for k in range(4))
    def masked(t):
        return jnp.where(t >= 0, 1.0, 0.0).astype(F32), jnp.maximum(t, 0)

    total = jnp.zeros((RANK, RANK), F32)
    for f in range(4):
        weight, t = masked(top_target[f, top])
        lifted = jnp.zeros((RANK, RANK), F32)
        for k in range(4):
            g = 4 * t + k
            lifted = lifted + group_transfer[g] * to_column(group_moments[pl.ds(g, 1), :], unit)
        total = total + top_coupling[f] * (jnp.sum(lifted, axis=0, keepdims=True) * weight)
    top_local = to_row(jnp.sum(total, axis=1, keepdims=True), unit)
    total = group_transfer[gx] * top_local
    for f in range(8):
        weight, t = masked(group_target[0, f])
        total = total + group_coupling[0, f] * (group_moments[pl.ds(t, 1), :] * weight)
    group_local = to_row(jnp.sum(total, axis=1, keepdims=True), unit)
    total = cluster_transfer[0] * group_local
    for f in range(8):
        weight, t = masked(cluster_target[0, f])
        total = total + cluster_coupling[0, f] * (every[(t % 4) * quarter + t // 4, :, :RANK] * weight)
    cluster_local = to_row(jnp.sum(total, axis=1, keepdims=True), unit)

    near_columns[...] = jnp.zeros((POINTS, 128), F32)

    @pl.loop(0, LEAVES // CHUNK)
    def _(c):
        rows = []
        for k in range(CHUNK):
            i = c * CHUNK + k
            total = transfer[i] * cluster_local + far_total[i]
            leaf_local = jnp.sum(total, axis=1, keepdims=True)
            rows.append(jnp.sum(bases[i] * leaf_local, axis=0, keepdims=True))
        near_columns[...] += lane_sums(near_total.at[pl.ds(c * CHUNK, CHUNK)], c * CHUNK)
        out[pl.ds(pl.multiple_of(c * CHUNK, CHUNK), CHUNK), :] = jnp.concatenate(rows, axis=0)

    out[...] += near_columns[...].T[:LEAVES] * INVERSE_FOUR_PI


def local(
    charges, points, leaf_bases, leaf_transfer, near_target, far_target, leaf_coupling, cluster_transfer,
    cluster_target, cluster_coupling, group_transfer, group_target, group_coupling, top_target, top_coupling,
):
    vmem = pl.BlockSpec(memory_space=pltpu.VMEM)
    anywhere = pl.BlockSpec(memory_space=pl.ANY)
    dma = pltpu.SemaphoreType.DMA

    def in_hbm(*arrays):
        return [pltpu.with_memory_space_constraint(array, pltpu.HBM) for array in arrays]

    handed = pl.pallas_call(
        exchange_kernel,
        out_shape=(
            pltpu.VMEM((3 * LEAVES + 1, TERMS, POINTS), BF16),
            pltpu.VMEM((LEAVES, POINTS, TERMS), BF16),
            pltpu.VMEM((3 * LEAVES + 8, POINTS), F32),
            pltpu.VMEM((DEVICES, 1, 2 * RANK), F32),
            pltpu.VMEM((2, PAIRS + 128), jnp.int32),
            pltpu.VMEM((LEAVES, RANK, POINTS), F32),
            pltpu.VMEM((LEAVES, RANK, RANK), F32),
            pltpu.VMEM((LEAVES, POINTS, 128), F32),
            pltpu.VMEM((LEAVES, RANK, RANK), F32),
            pltpu.VMEM((LEAVES, FAR), jnp.int32),
            pltpu.VMEM((5 * LEAVES + 8, RANK), F32),
        ),
        in_specs=[anywhere] * 8,
        out_specs=[vmem] * 11,
        scratch_shapes=[
            pltpu.VMEM((EXCHANGED * FAR, RANK, RANK), F32),
            pltpu.SMEM((LEAVES, FAR), jnp.int32),
            pltpu.VMEM((8, 128), jnp.int32),
            pltpu.SMEM((8, 128), jnp.int32),
            pltpu.VMEM((4, LEAVES, POINTS), F32),
            pltpu.VMEM((NEAR, LEAVES), jnp.int32),
            pltpu.VMEM((FAR, LEAVES), jnp.int32),
            pltpu.VMEM((1, RANK, RANK), F32),
            pltpu.VMEM((2, 4, LEAVES, POINTS), F32),
            pltpu.VMEM((5, LEAVES // 2, 2 * RANK), F32),
            pltpu.VMEM((DEVICES, 1, 2 * RANK), F32),
            dma((LEAVES // CHUNK,)),
            dma,
            dma,
            dma((2, LEAVES // CHUNK)),
            dma((5,)),
            dma((HALO_PARTS, 2)),
            dma((HALO_PARTS, 2)),
            dma((4,)),
            dma((4,)),
            dma((len(STAGES), 8)),
            dma((len(STAGES), 8)),
        ],
        compiler_params=pltpu.CompilerParams(
            collective_id=0, has_side_effects=True, vmem_limit_bytes=30 << 20
        ),
        name="exchange",
    )(
        *in_hbm(
            charges,
            jnp.transpose(points, (1, 0, 2)),
            near_target.T,
            far_target.T,
            cluster_transfer,
            jnp.swapaxes(leaf_bases, 1, 2),
            leaf_transfer,
            leaf_coupling.reshape(LEAVES * FAR, RANK, RANK),
        )
    )
    return pl.pallas_call(
        local_kernel,
        out_shape=(
            jax.ShapeDtypeStruct((LEAVES, POINTS), F32),
            pltpu.VMEM((LEAVES, POINTS, 128), F32),
            pltpu.VMEM((LEAVES, RANK, RANK), F32),
        ),
        in_specs=[vmem] * 11 + [anywhere] * 9,
        out_specs=[vmem] * 3,
        input_output_aliases={7: 1, 8: 2},
        scratch_shapes=[
            pltpu.VMEM(((LEAVES - EXCHANGED) * FAR, RANK, RANK), F32),
            pltpu.SMEM((LEAVES, FAR), jnp.int32),
            pltpu.VMEM((GROUP, POINTS, 128), F32),
            pltpu.VMEM((POINTS, 128), F32),
            pltpu.VMEM((1, RANK, RANK), F32),
            pltpu.VMEM((1, 8, RANK, RANK), F32),
            pltpu.VMEM((1, 8, RANK, RANK), F32),
            pltpu.VMEM((32, RANK, RANK), F32),
            pltpu.VMEM((4, RANK, RANK), F32),
            pltpu.VMEM((32, RANK), F32),
            pltpu.SMEM((2, PAIRS + 128), jnp.int32),
            pltpu.SMEM((1, 8), jnp.int32),
            pltpu.SMEM((1, 8), jnp.int32),
            pltpu.SMEM((4, 8), jnp.int32),
            dma((11,)),
        ],
        compiler_params=pltpu.CompilerParams(vmem_limit_bytes=30 << 20),
        name="local",
    )(
        *[pltpu.with_memory_space_constraint(array, pltpu.VMEM) for array in handed],
        *in_hbm(
            cluster_target,
            group_target,
            top_target.T,
            cluster_transfer,
            cluster_coupling,
            group_coupling,
            group_transfer,
            top_coupling,
            leaf_coupling.reshape(LEAVES * FAR, RANK, RANK),
        ),
    )[0]


def solution(mesh):
    leaf = ("gx", "gy")
    return jax.shard_map(
        local,
        mesh=mesh,
        in_specs=(
            P(leaf, None),
            P(leaf, None, None),
            P(leaf, None, None),
            P(leaf, None, None),
            P(leaf, None),
            P(leaf, None),
            P(leaf, None, None, None),
            P(leaf, None, None),
            P(leaf, None),
            P(leaf, None, None, None),
            P(),
            P("gx", None),
            P("gx", None, None, None),
            P(),
            P(),
        ),
        out_specs=P(leaf, None),
        check_vma=False,
    )
```

```python
import functools
import math

import jax
import jax.numpy as jnp
from jax import lax
from jax.experimental import pallas as pl
from jax.experimental.pallas import tpu as pltpu
from jax.sharding import PartitionSpec as P

MESH = pl.DeviceIdType.MESH
F32 = jnp.float32
BF16 = jnp.bfloat16
SMOOTHING = 0.01
INVERSE_FOUR_PI = 1.0 / (4.0 * math.pi)

LEAVES = 64
POINTS = 256
RANK = 64
NEAR = 8
FAR = 16
TERMS = 32
PAIRS = LEAVES * NEAR
GROUP = 32
LAST_GROUP = 16
EXCHANGED = 48
OWN = 2
CHUNK = 8
DEVICES = 128
STAGES = ((1, 8), (8, 4), (32, 4))
HALO_PARTS = 2
BLANK = 3 * LEAVES


def split3(value):
    high = value.astype(BF16).astype(F32)
    rest = value - high
    middle = rest.astype(BF16).astype(F32)
    low = (rest - middle).astype(BF16).astype(F32)
    return high, middle, low


def centred(points):
    shifted = [p - 1.0 for p in points]
    norm = shifted[0] * shifted[0] + shifted[1] * shifted[1] + shifted[2] * shifted[2]
    return [split3(u) for u in shifted], norm


def source_terms(parts, norm):
    rows = []
    for high, middle, low in parts:
        high, middle, low = -2.0 * high, -2.0 * middle, -2.0 * low
        rows += [high, high, high, middle, middle, low]
    one = jnp.ones_like(norm)
    return rows + list(split3(norm + SMOOTHING)) + [one, one, one]


def target_terms(parts, norm):
    rows = []
    for high, middle, low in parts:
        rows += [high, middle, low, high, middle, high]
    one = jnp.ones_like(norm)
    return rows + [one, one, one] + list(split3(norm))


def by_leaf(rows):
    blank = jnp.zeros_like(rows[0])
    return jnp.swapaxes(jnp.stack(rows + [blank] * (TERMS - len(rows)), axis=0), 0, 1)


def eye():
    shape = (RANK, RANK)
    return (lax.broadcasted_iota(jnp.int32, shape, 0) == lax.broadcasted_iota(jnp.int32, shape, 1)).astype(F32)


def to_column(row, unit):
    return jnp.sum(unit * row, axis=1, keepdims=True)


def to_row(column, unit):
    return jnp.sum(unit * column, axis=0, keepdims=True)


def lane_sums(parts, first):
    odd = lax.broadcasted_iota(jnp.int32, (POINTS, 128), 1) % 2
    source = lax.broadcasted_iota(jnp.int32, (256, 128), 0)
    column = lax.broadcasted_iota(jnp.int32, (256, 128), 1) - first
    total = None
    for k in range(0, CHUNK, 4):
        halves = []
        for n in (k, k + 2):
            here, there = parts[n], parts[n + 1]
            halves.append(jnp.where(odd == 0, here, there) + pltpu.roll(jnp.where(odd == 0, there, here), 127, axis=1))
        values = jnp.concatenate(halves, axis=1)
        high = values.astype(BF16)
        low = (values - high.astype(F32)).astype(BF16)
        ones = jnp.where(k + source // 128 * 2 + source % 2 == column, 1.0, 0.0).astype(BF16)
        for piece in (high, low):
            term = jnp.dot(piece, ones, preferred_element_type=F32)
            total = term if total is None else total + term
    return total


def folded(square, charge):
    weighted = lax.rsqrt(square) * charge
    return weighted[:, :128] + weighted[:, 128:]


def exchange_kernel(
    charges_hbm, points_hbm, near_hbm, far_hbm, cluster_transfer_hbm, bases_hbm, transfer_hbm, coupling_hbm,
    source_out, target_out, charge_out, every_out, pair_out, bases, transfer, near_out, far_out, far_vector, moment_rows,
    coupling, far_rows, choice_vector, choice, own, near, far, cluster_transfer, halo, window, every,
    coupling_sems, far_sem, choice_sem, load_sems, small_sems, halo_send, halo_recv, moment_send, moment_recv, every_send, every_recv,
):
    gx, gy = lax.axis_index("gx"), lax.axis_index("gy")
    device = gx * 4 + gy

    def place(index):
        return (index // 4, index % 4)

    def beside(distance):
        return place((device + distance + DEVICES) % DEVICES)

    chunks = LEAVES // CHUNK
    lateness = (gx // 2) % 4 + gx // 8 + 2 * gy
    terms_before = jnp.where(lateness <= 6, chunks, 0)
    moments_before = jnp.where(lateness <= 4, chunks, 0)
    own_limit = jnp.where(lateness <= 6, OWN, 1)

    def load_copies(c):
        span = pl.ds(c * CHUNK, CHUNK)
        return (
            pltpu.make_async_copy(bases_hbm.at[span], bases.at[span], load_sems.at[0, c]),
            pltpu.make_async_copy(transfer_hbm.at[span], transfer.at[span], load_sems.at[1, c]),
        )

    small = [
        pltpu.make_async_copy(source, landing, small_sems.at[n])
        for n, (source, landing) in enumerate(
            (
                (charges_hbm, own.at[0]),
                (points_hbm, own.at[pl.ds(1, 3)]),
                (near_hbm, near),
                (far_hbm, far),
                (cluster_transfer_hbm, cluster_transfer),
            )
        )
    ]
    for copy in small:
        copy.start()

    @pl.loop(0, chunks)
    def _(c):
        for copy in load_copies(c):
            copy.start()

    def coupling_copy(c):
        span = pl.ds(c * CHUNK * FAR, CHUNK * FAR)
        return pltpu.make_async_copy(coupling_hbm.at[span], coupling.at[span], coupling_sems.at[c])

    far_chunk_count = EXCHANGED // CHUNK

    barrier = pltpu.get_barrier_semaphore()
    for distance in (1, -1, 2, -2):
        pl.semaphore_signal(barrier, inc=1, device_id=beside(distance), device_id_type=MESH)

    row = gy * (DEVICES // 4) + gx

    def mate(stage, k):
        unit, count = STAGES[stage]
        position = (row // unit) % count
        there = row + ((position + k) % count - position) * unit
        return (there % (DEVICES // 4), there // (DEVICES // 4))

    for stage in range(len(STAGES)):

        @pl.loop(1, STAGES[stage][1])
        def _(k):
            pl.semaphore_signal(barrier, inc=1, device_id=mate(stage, k), device_id_type=MESH)

    for copy in small:
        copy.wait()
    far_targets = far[...]
    far_vector[...] = jnp.where(far_targets >= 0, far_targets - (device - 2) * LEAVES, 5 * LEAVES).T
    far_copy = pltpu.make_async_copy(far_vector, far_rows, far_sem)
    far_copy.start()

    slots = near[...]
    local_slots = slots - device * LEAVES
    is_here = jnp.where((local_slots >= 0) & (local_slots < LEAVES), 1, 0)
    live_rows = []
    own_before = jnp.zeros((1, LEAVES), jnp.int32)
    chosen = [jnp.full((1, LEAVES), BLANK, jnp.int32) for _ in range(OWN)]
    for s in range(NEAR):
        is_own = is_here[s : s + 1] > 0
        for n in range(OWN):
            chosen[n] = jnp.where(is_own & (own_before == n) & (n < own_limit), local_slots[s : s + 1] + LEAVES, chosen[n])
        left = jnp.where(is_own & (own_before < own_limit), 0.0, 1.0)
        live_rows.append(jnp.where(slots[s : s + 1] >= 0, left, 0.0))
        own_before = own_before + is_here[s : s + 1]
    for n in range(OWN):
        choice_vector[n : n + 1, 0:LEAVES] = chosen[n]
    choice_copy = pltpu.make_async_copy(choice_vector, choice, choice_sem)
    choice_copy.start()
    live = jnp.concatenate(live_rows, axis=0)
    before = (
        lax.broadcasted_iota(jnp.int32, (LEAVES, LEAVES), 0) < lax.broadcasted_iota(jnp.int32, (LEAVES, LEAVES), 1)
    ).astype(BF16)
    rank_in_slot = jnp.dot(live.astype(BF16), before, preferred_element_type=F32)
    in_slot = jnp.sum(live, axis=1, keepdims=True)
    leaf_row = lax.broadcasted_iota(jnp.int32, (1, LEAVES), 1)
    code = (leaf_row * 256 + slots - (device - 1) * LEAVES).astype(F32)
    position_row = lax.broadcasted_iota(jnp.int32, (1, PAIRS), 1).astype(F32)
    found = jnp.zeros((LEAVES, PAIRS), F32)
    start = jnp.zeros((1, 1), F32)
    positions = []
    for s in range(NEAR):
        positions.append(jnp.where(live[s : s + 1] > 0, rank_in_slot[s : s + 1] + start, -1.0))
        start = start + in_slot[s : s + 1]
    table = jnp.concatenate(positions + [code], axis=0).T
    for s in range(NEAR):
        found = jnp.where(table[:, s : s + 1] == position_row, table[:, NEAR + s : NEAR + s + 1], found)
    pairs = jnp.sum(found, axis=0, keepdims=True)
    pair_out[0:1, 0:PAIRS] = jnp.where(position_row < start, pairs, float(BLANK)).astype(jnp.int32)
    pair_out[0:1, PAIRS:] = jnp.full((1, 128), BLANK, jnp.int32)
    pair_out[1:2, 0:128] = jnp.broadcast_to(start.astype(jnp.int32), (1, 128))
    def own_terms(c):
        span = pl.ds(pl.multiple_of(c * CHUNK, CHUNK), CHUNK)
        parts, norm = centred([own[n, span, :] for n in range(1, 4)])
        source_out[pl.ds(LEAVES + c * CHUNK, CHUNK)] = by_leaf(source_terms(parts, norm)).astype(BF16)
        target = by_leaf(target_terms(parts, norm)).astype(BF16)
        for k in range(CHUNK):
            target_out[c * CHUNK + k] = target[k].T

    pl.loop(0, terms_before)(own_terms)
    charge_out[LEAVES : 2 * LEAVES] = own[0]
    charge_out[3 * LEAVES :] = jnp.zeros((8, POINTS), F32)
    term = lax.broadcasted_iota(jnp.int32, (TERMS, POINTS), 0)
    source_out[BLANK] = jnp.where(term == 18, 1.0, 0.0).astype(BF16)

    lane = lax.broadcasted_iota(jnp.int32, (RANK, LEAVES), 1)

    def moment_chunk(c, carry):
        columns, total = carry
        for copy in load_copies(c):
            copy.wait()
        weights = own[0, pl.ds(pl.multiple_of(c * CHUNK, CHUNK), CHUNK), :]
        for k in range(CHUNK):
            product = bases[c * CHUNK + k] * weights[k : k + 1, :]
            column = jnp.sum(product[:, :128] + product[:, 128:], axis=1, keepdims=True)
            columns = jnp.where(lane == c * CHUNK + k, column, columns)
            total = total + transfer[c * CHUNK + k] * column
        return columns, total

    carry = lax.fori_loop(
        0, moments_before, moment_chunk, (jnp.zeros((RANK, LEAVES), F32), jnp.zeros((RANK, RANK), F32))
    )
    pl.semaphore_wait(barrier, 4 + sum(count - 1 for _, count in STAGES))

    part_leaves = LEAVES // HALO_PARTS
    copies_of_halo = [
        [
            pltpu.make_async_remote_copy(
                src_ref=own.at[:, pl.ds(part * part_leaves, part_leaves)],
                dst_ref=halo.at[side, :, pl.ds(part * part_leaves, part_leaves)],
                send_sem=halo_send.at[part, side],
                recv_sem=halo_recv.at[part, side],
                device_id=beside(distance),
                device_id_type=MESH,
            )
            for side, distance in ((0, 1), (1, -1))
        ]
        for part in range(HALO_PARTS)
    ]
    for copy in copies_of_halo[0]:
        copy.start()

    columns, total = lax.fori_loop(moments_before, chunks, moment_chunk, carry)
    rows = columns.T
    window[2] = jnp.concatenate([rows[: LEAVES // 2], rows[LEAVES // 2 :]], axis=1)
    unit = eye()
    cluster_row = jnp.sum(total, axis=0, keepdims=True)
    lifted_row = jnp.sum(cluster_transfer[0] * to_column(cluster_row, unit), axis=0, keepdims=True)
    every[row, 0:1, 0:RANK] = cluster_row
    every[row, 0:1, RANK : 2 * RANK] = lifted_row

    def every_copy(stage, k):
        unit, _ = STAGES[stage]
        rows = pl.ds((row // unit) * unit, unit)
        return pltpu.make_async_remote_copy(
            src_ref=every.at[rows],
            dst_ref=every.at[rows],
            send_sem=every_send.at[stage, k],
            recv_sem=every_recv.at[stage, k],
            device_id=mate(stage, k),
            device_id_type=MESH,
        )

    def start_stage(stage):
        for k in range(1, STAGES[stage][1]):
            every_copy(stage, k).start()

    def finish_stage(stage):
        for k in range(1, STAGES[stage][1]):
            every_copy(stage, k).wait_recv()

    start_stage(0)

    @pl.loop(0, far_chunk_count)
    def _(c):
        coupling_copy(c).start()

    def moment_copies():
        copies = []
        for n, distance in enumerate((2, 1, -1, -2)):
            slot = (0, 1, 3, 4)[n]
            copies.append(
                pltpu.make_async_remote_copy(
                    src_ref=window.at[2],
                    dst_ref=window.at[slot],
                    send_sem=moment_send.at[n],
                    recv_sem=moment_recv.at[n],
                    device_id=beside(distance),
                    device_id_type=MESH,
                )
            )
        return copies

    moments = moment_copies()
    for copy in moments:
        copy.start()
    for copies in copies_of_halo[1:]:
        for copy in copies:
            copy.start()

    pl.loop(terms_before, chunks)(own_terms)

    choice_copy.wait()

    for n in range(OWN):

        @pl.loop(0, LEAVES // GROUP if n == 0 else jnp.where(own_limit > n, LEAVES // GROUP, 0))
        def _(g):
            for k in range(GROUP):
                i = g * GROUP + k
                j = jnp.clip(choice[n, i], 0, BLANK)
                square = jnp.dot(target_out[i], source_out[j], preferred_element_type=F32)
                part = folded(square, charge_out[pl.ds(j, 1), :])
                if n == 0:
                    near_out[i] = part
                else:
                    near_out[i] += part

            @pl.when(g == 0)
            def _():
                finish_stage(n)
                start_stage(n + 1)

    @pl.when(own_limit < 2)
    def _():
        finish_stage(1)
        start_stage(2)

    for copy in moments:
        copy.wait_recv()
    for n in range(5):
        moment_rows[n * LEAVES : n * LEAVES + LEAVES // 2] = window[n][:, :RANK]
        moment_rows[n * LEAVES + LEAVES // 2 : (n + 1) * LEAVES] = window[n][:, RANK:]
    moment_rows[5 * LEAVES :] = jnp.zeros((8, RANK), F32)
    far_copy.wait()

    def far_chunk(c):
        coupling_copy(c).wait()
        for k in range(CHUNK):
            i = c * CHUNK + k
            total = None
            for f in range(FAR):
                slot = jnp.clip(far_rows[i, f], 0, 5 * LEAVES)
                term = coupling[i * FAR + f] * moment_rows[pl.ds(slot, 1), :]
                total = term if total is None else total + term
            far_out[i] = total

    def far_chunks(first, last):
        pl.loop(first, last)(far_chunk)

    far_chunks(0, 4)

    for part in range(HALO_PARTS):
        for side in range(2):
            copies_of_halo[part][side].wait_recv()
            first = 2 * LEAVES * side

            @pl.loop(part * part_leaves // CHUNK, (part + 1) * part_leaves // CHUNK)
            def _(c):
                span = pl.ds(pl.multiple_of(c * CHUNK, CHUNK), CHUNK)
                parts, norm = centred([halo[side, n, span, :] for n in range(1, 4)])
                source_out[pl.ds(first + c * CHUNK, CHUNK)] = by_leaf(source_terms(parts, norm)).astype(BF16)

    charge_out[0:LEAVES] = halo[0, 0]
    charge_out[2 * LEAVES : 3 * LEAVES] = halo[1, 0]

    far_chunks(4, far_chunk_count)

    finish_stage(2)
    every_out[...] = every[...]

    for stage in range(len(STAGES)):
        for k in range(1, STAGES[stage][1]):
            every_copy(stage, k).wait_send()
    for copy in sum(copies_of_halo, []) + moments:
        copy.wait_send()


def local_kernel(
    source, target, charges, every, pairs_vmem, bases, transfer, near_first, far_first, far_vmem, moments,
    cluster_target_hbm, group_target_hbm, top_target_hbm, cluster_transfer_hbm, cluster_coupling_hbm,
    group_coupling_hbm, group_transfer_hbm, top_coupling_hbm, coupling_hbm,
    out, near_total, far_total,
    coupling, far_rows, parts, near_columns, cluster_transfer, cluster_coupling, group_coupling, group_transfer, top_coupling,
    group_moments, pairs, cluster_target, group_target, top_target,
    sems,
):
    gx = lax.axis_index("gx")
    top = gx // 4

    loads = [
        pltpu.make_async_copy(source_ref, landing, sems.at[n])
        for n, (source_ref, landing) in enumerate(
            (
                (pairs_vmem, pairs),
                (far_vmem, far_rows),
                (cluster_target_hbm, cluster_target),
                (group_target_hbm, group_target),
                (top_target_hbm, top_target),
                (cluster_transfer_hbm, cluster_transfer),
                (cluster_coupling_hbm, cluster_coupling),
                (group_coupling_hbm, group_coupling),
                (group_transfer_hbm, group_transfer),
                (top_coupling_hbm.at[top], top_coupling),
                (coupling_hbm.at[pl.ds(EXCHANGED * FAR, (LEAVES - EXCHANGED) * FAR)], coupling),
            )
        )
    ]
    for copy in loads:
        copy.start()

    for k in range(GROUP):
        parts[k] = jnp.zeros((POINTS, 128), F32)
    loads[0].wait()

    def add_parts(first, count):
        for k in range(count):
            near_total[pairs[0, first + k] // 256] += parts[k]

    def listed_pairs(first, count):
        for k in range(count):
            code = pairs[0, first + k]
            i, j = code // 256, code % 256
            square = jnp.dot(target[i], source[j], preferred_element_type=F32)
            parts[k] = folded(square, charges[pl.ds(j, 1), :])

    live = pairs[1, 0]
    groups = (live + GROUP - LAST_GROUP - 1) // GROUP

    @pl.loop(0, groups)
    def _(g):
        add_parts(jnp.maximum(g - 1, 0) * GROUP, GROUP)
        listed_pairs(g * GROUP, GROUP)

    last = jnp.maximum(groups - 1, 0) * GROUP

    @pl.when(live > groups * GROUP)
    def _():
        add_parts(last, GROUP)
        listed_pairs(groups * GROUP, LAST_GROUP)
        add_parts(groups * GROUP, LAST_GROUP)

    @pl.when(live <= groups * GROUP)
    def _():
        add_parts(last, GROUP)

    unit = eye()
    for copy in loads[1:]:
        copy.wait()

    @pl.loop(0, (LEAVES - EXCHANGED) // CHUNK)
    def _(c):
        for k in range(CHUNK):
            i = c * CHUNK + k
            total = None
            for f in range(FAR):
                term = coupling[i * FAR + f] * moments[pl.ds(far_rows[EXCHANGED + i, f], 1), :]
                total = term if total is None else total + term
            far_total[EXCHANGED + i] = total


    quarter = DEVICES // 4
    group_moments[...] = sum(every[pl.ds(k * quarter, quarter), 0, :][:, RANK:] for k in range(4))
    def masked(t):
        return jnp.where(t >= 0, 1.0, 0.0).astype(F32), jnp.maximum(t, 0)

    total = jnp.zeros((RANK, RANK), F32)
    for f in range(4):
        weight, t = masked(top_target[f, top])
        lifted = jnp.zeros((RANK, RANK), F32)
        for k in range(4):
            g = 4 * t + k
            lifted = lifted + group_transfer[g] * to_column(group_moments[pl.ds(g, 1), :], unit)
        total = total + top_coupling[f] * (jnp.sum(lifted, axis=0, keepdims=True) * weight)
    top_local = to_row(jnp.sum(total, axis=1, keepdims=True), unit)
    total = group_transfer[gx] * top_local
    for f in range(8):
        weight, t = masked(group_target[0, f])
        total = total + group_coupling[0, f] * (group_moments[pl.ds(t, 1), :] * weight)
    group_local = to_row(jnp.sum(total, axis=1, keepdims=True), unit)
    total = cluster_transfer[0] * group_local
    for f in range(8):
        weight, t = masked(cluster_target[0, f])
        total = total + cluster_coupling[0, f] * (every[(t % 4) * quarter + t // 4, :, :RANK] * weight)
    cluster_local = to_row(jnp.sum(total, axis=1, keepdims=True), unit)

    near_columns[...] = jnp.zeros((POINTS, 128), F32)

    @pl.loop(0, LEAVES // CHUNK)
    def _(c):
        rows = []
        for k in range(CHUNK):
            i = c * CHUNK + k
            total = transfer[i] * cluster_local + far_total[i]
            leaf_local = jnp.sum(total, axis=1, keepdims=True)
            rows.append(jnp.sum(bases[i] * leaf_local, axis=0, keepdims=True))
        near_columns[...] += lane_sums(near_total.at[pl.ds(c * CHUNK, CHUNK)], c * CHUNK)
        out[pl.ds(pl.multiple_of(c * CHUNK, CHUNK), CHUNK), :] = jnp.concatenate(rows, axis=0)

    out[...] += near_columns[...].T[:LEAVES] * INVERSE_FOUR_PI


def local(
    charges, points, leaf_bases, leaf_transfer, near_target, far_target, leaf_coupling, cluster_transfer,
    cluster_target, cluster_coupling, group_transfer, group_target, group_coupling, top_target, top_coupling,
):
    vmem = pl.BlockSpec(memory_space=pltpu.VMEM)
    anywhere = pl.BlockSpec(memory_space=pl.ANY)
    dma = pltpu.SemaphoreType.DMA

    def in_hbm(*arrays):
        return [pltpu.with_memory_space_constraint(array, pltpu.HBM) for array in arrays]

    handed = pl.pallas_call(
        exchange_kernel,
        out_shape=(
            pltpu.VMEM((3 * LEAVES + 1, TERMS, POINTS), BF16),
            pltpu.VMEM((LEAVES, POINTS, TERMS), BF16),
            pltpu.VMEM((3 * LEAVES + 8, POINTS), F32),
            pltpu.VMEM((DEVICES, 1, 2 * RANK), F32),
            pltpu.VMEM((2, PAIRS + 128), jnp.int32),
            pltpu.VMEM((LEAVES, RANK, POINTS), F32),
            pltpu.VMEM((LEAVES, RANK, RANK), F32),
            pltpu.VMEM((LEAVES, POINTS, 128), F32),
            pltpu.VMEM((LEAVES, RANK, RANK), F32),
            pltpu.VMEM((LEAVES, FAR), jnp.int32),
            pltpu.VMEM((5 * LEAVES + 8, RANK), F32),
        ),
        in_specs=[anywhere] * 8,
        out_specs=[vmem] * 11,
        scratch_shapes=[
            pltpu.VMEM((EXCHANGED * FAR, RANK, RANK), F32),
            pltpu.SMEM((LEAVES, FAR), jnp.int32),
            pltpu.VMEM((8, 128), jnp.int32),
            pltpu.SMEM((8, 128), jnp.int32),
            pltpu.VMEM((4, LEAVES, POINTS), F32),
            pltpu.VMEM((NEAR, LEAVES), jnp.int32),
            pltpu.VMEM((FAR, LEAVES), jnp.int32),
            pltpu.VMEM((1, RANK, RANK), F32),
            pltpu.VMEM((2, 4, LEAVES, POINTS), F32),
            pltpu.VMEM((5, LEAVES // 2, 2 * RANK), F32),
            pltpu.VMEM((DEVICES, 1, 2 * RANK), F32),
            dma((LEAVES // CHUNK,)),
            dma,
            dma,
            dma((2, LEAVES // CHUNK)),
            dma((5,)),
            dma((HALO_PARTS, 2)),
            dma((HALO_PARTS, 2)),
            dma((4,)),
            dma((4,)),
            dma((len(STAGES), 8)),
            dma((len(STAGES), 8)),
        ],
        compiler_params=pltpu.CompilerParams(
            collective_id=0, has_side_effects=True, vmem_limit_bytes=30 << 20
        ),
        name="exchange",
    )(
        *in_hbm(
            charges,
            jnp.transpose(points, (1, 0, 2)),
            near_target.T,
            far_target.T,
            cluster_transfer,
            jnp.swapaxes(leaf_bases, 1, 2),
            leaf_transfer,
            leaf_coupling.reshape(LEAVES * FAR, RANK, RANK),
        )
    )
    return pl.pallas_call(
        local_kernel,
        out_shape=(
            jax.ShapeDtypeStruct((LEAVES, POINTS), F32),
            pltpu.VMEM((LEAVES, POINTS, 128), F32),
            pltpu.VMEM((LEAVES, RANK, RANK), F32),
        ),
        in_specs=[vmem] * 11 + [anywhere] * 9,
        out_specs=[vmem] * 3,
        input_output_aliases={7: 1, 8: 2},
        scratch_shapes=[
            pltpu.VMEM(((LEAVES - EXCHANGED) * FAR, RANK, RANK), F32),
            pltpu.SMEM((LEAVES, FAR), jnp.int32),
            pltpu.VMEM((GROUP, POINTS, 128), F32),
            pltpu.VMEM((POINTS, 128), F32),
            pltpu.VMEM((1, RANK, RANK), F32),
            pltpu.VMEM((1, 8, RANK, RANK), F32),
            pltpu.VMEM((1, 8, RANK, RANK), F32),
            pltpu.VMEM((32, RANK, RANK), F32),
            pltpu.VMEM((4, RANK, RANK), F32),
            pltpu.VMEM((32, RANK), F32),
            pltpu.SMEM((2, PAIRS + 128), jnp.int32),
            pltpu.SMEM((1, 8), jnp.int32),
            pltpu.SMEM((1, 8), jnp.int32),
            pltpu.SMEM((4, 8), jnp.int32),
            dma((11,)),
        ],
        compiler_params=pltpu.CompilerParams(vmem_limit_bytes=30 << 20),
        name="local",
    )(
        *[pltpu.with_memory_space_constraint(array, pltpu.VMEM) for array in handed],
        *in_hbm(
            cluster_target,
            group_target,
            top_target.T,
            cluster_transfer,
            cluster_coupling,
            group_coupling,
            group_transfer,
            top_coupling,
            leaf_coupling.reshape(LEAVES * FAR, RANK, RANK),
        ),
    )[0]


def solution(mesh):
    leaf = ("gx", "gy")
    return jax.shard_map(
        local,
        mesh=mesh,
        in_specs=(
            P(leaf, None),
            P(leaf, None, None),
            P(leaf, None, None),
            P(leaf, None, None),
            P(leaf, None),
            P(leaf, None),
            P(leaf, None, None, None),
            P(leaf, None, None),
            P(leaf, None),
            P(leaf, None, None, None),
            P(),
            P("gx", None),
            P("gx", None, None, None),
            P(),
            P(),
        ),
        out_specs=P(leaf, None),
        check_vma=False,
    )
```

```python
import functools
import math

import jax
import jax.numpy as jnp
from jax import lax
from jax.experimental import pallas as pl
from jax.experimental.pallas import tpu as pltpu
from jax.sharding import PartitionSpec as P

MESH = pl.DeviceIdType.MESH
F32 = jnp.float32
BF16 = jnp.bfloat16
SMOOTHING = 0.01
INVERSE_FOUR_PI = 1.0 / (4.0 * math.pi)

LEAVES = 64
POINTS = 256
RANK = 64
NEAR = 8
FAR = 16
TERMS = 32
PAIRS = LEAVES * NEAR
GROUP = 32
LAST_GROUP = 16
EXCHANGED = 48
OWN = 3
CHUNK = 8
DEVICES = 128
STAGES = ((1, 8), (8, 4), (32, 4))
HALO_PARTS = 4
BLANK = 3 * LEAVES


def split3(value):
    high = value.astype(BF16).astype(F32)
    rest = value - high
    middle = rest.astype(BF16).astype(F32)
    low = (rest - middle).astype(BF16).astype(F32)
    return high, middle, low


def centred(points):
    shifted = [p - 1.0 for p in points]
    norm = shifted[0] * shifted[0] + shifted[1] * shifted[1] + shifted[2] * shifted[2]
    return [split3(u) for u in shifted], norm


def source_terms(parts, norm):
    rows = []
    for high, middle, low in parts:
        high, middle, low = -2.0 * high, -2.0 * middle, -2.0 * low
        rows += [high, high, high, middle, middle, low]
    one = jnp.ones_like(norm)
    return rows + list(split3(norm + SMOOTHING)) + [one, one, one]


def target_terms(parts, norm):
    rows = []
    for high, middle, low in parts:
        rows += [high, middle, low, high, middle, high]
    one = jnp.ones_like(norm)
    return rows + [one, one, one] + list(split3(norm))


def by_leaf(rows):
    blank = jnp.zeros_like(rows[0])
    return jnp.swapaxes(jnp.stack(rows + [blank] * (TERMS - len(rows)), axis=0), 0, 1)


def eye():
    shape = (RANK, RANK)
    return (lax.broadcasted_iota(jnp.int32, shape, 0) == lax.broadcasted_iota(jnp.int32, shape, 1)).astype(F32)


def to_column(row, unit):
    return jnp.sum(unit * row, axis=1, keepdims=True)


def to_row(column, unit):
    return jnp.sum(unit * column, axis=0, keepdims=True)


def lane_sums(parts, first):
    odd = lax.broadcasted_iota(jnp.int32, (POINTS, 128), 1) % 2
    source = lax.broadcasted_iota(jnp.int32, (256, 128), 0)
    column = lax.broadcasted_iota(jnp.int32, (256, 128), 1) - first
    total = None
    for k in range(0, CHUNK, 4):
        halves = []
        for n in (k, k + 2):
            here, there = parts[n], parts[n + 1]
            halves.append(jnp.where(odd == 0, here, there) + pltpu.roll(jnp.where(odd == 0, there, here), 127, axis=1))
        values = jnp.concatenate(halves, axis=1)
        high = values.astype(BF16)
        low = (values - high.astype(F32)).astype(BF16)
        ones = jnp.where(k + source // 128 * 2 + source % 2 == column, 1.0, 0.0).astype(BF16)
        for piece in (high, low):
            term = jnp.dot(piece, ones, preferred_element_type=F32)
            total = term if total is None else total + term
    return total


def folded(square, charge):
    weighted = lax.rsqrt(square) * charge
    return weighted[:, :128] + weighted[:, 128:]


def exchange_kernel(
    charges_hbm, points_hbm, near_hbm, far_hbm, cluster_transfer_hbm, bases_hbm, transfer_hbm, coupling_hbm,
    source_out, target_out, charge_out, every_out, pair_out, bases, transfer, near_out, far_out, far_vector, moment_rows,
    coupling, far_rows, choice_vector, choice, own, near, far, cluster_transfer, halo, window, every,
    coupling_sems, far_sem, choice_sem, load_sems, small_sems, halo_send, halo_recv, moment_send, moment_recv, every_send, every_recv,
):
    gx, gy = lax.axis_index("gx"), lax.axis_index("gy")
    device = gx * 4 + gy

    def place(index):
        return (index // 4, index % 4)

    def beside(distance):
        return place((device + distance + DEVICES) % DEVICES)

    chunks = LEAVES // CHUNK
    lateness = (gx // 2) % 4 + gx // 8 + 2 * gy
    terms_before = jnp.where(lateness <= 6, chunks, 0)
    moments_before = jnp.where(lateness <= 4, chunks, 0)
    own_limit = jnp.where(lateness <= 3, OWN, jnp.where(lateness <= 6, 2, 1))

    def load_copies(c):
        span = pl.ds(c * CHUNK, CHUNK)
        return (
            pltpu.make_async_copy(bases_hbm.at[span], bases.at[span], load_sems.at[0, c]),
            pltpu.make_async_copy(transfer_hbm.at[span], transfer.at[span], load_sems.at[1, c]),
        )

    small = [
        pltpu.make_async_copy(source, landing, small_sems.at[n])
        for n, (source, landing) in enumerate(
            (
                (charges_hbm, own.at[0]),
                (points_hbm, own.at[pl.ds(1, 3)]),
                (near_hbm, near),
                (far_hbm, far),
                (cluster_transfer_hbm, cluster_transfer),
            )
        )
    ]
    for copy in small:
        copy.start()

    @pl.loop(0, chunks)
    def _(c):
        for copy in load_copies(c):
            copy.start()

    def coupling_copy(c):
        span = pl.ds(c * CHUNK * FAR, CHUNK * FAR)
        return pltpu.make_async_copy(coupling_hbm.at[span], coupling.at[span], coupling_sems.at[c])

    far_chunk_count = EXCHANGED // CHUNK

    barrier = pltpu.get_barrier_semaphore()
    for distance in (1, -1, 2, -2):
        pl.semaphore_signal(barrier, inc=1, device_id=beside(distance), device_id_type=MESH)

    row = gy * (DEVICES // 4) + gx

    def mate(stage, k):
        unit, count = STAGES[stage]
        position = (row // unit) % count
        there = row + ((position + k) % count - position) * unit
        return (there % (DEVICES // 4), there // (DEVICES // 4))

    for stage in range(len(STAGES)):

        @pl.loop(1, STAGES[stage][1])
        def _(k):
            pl.semaphore_signal(barrier, inc=1, device_id=mate(stage, k), device_id_type=MESH)

    for copy in small:
        copy.wait()
    far_targets = far[...]
    far_vector[...] = jnp.where(far_targets >= 0, far_targets - (device - 2) * LEAVES, 5 * LEAVES).T
    far_copy = pltpu.make_async_copy(far_vector, far_rows, far_sem)
    far_copy.start()

    slots = near[...]
    local_slots = slots - device * LEAVES
    is_here = jnp.where((local_slots >= 0) & (local_slots < LEAVES), 1, 0)
    live_rows = []
    own_before = jnp.zeros((1, LEAVES), jnp.int32)
    chosen = [jnp.full((1, LEAVES), BLANK, jnp.int32) for _ in range(OWN)]
    for s in range(NEAR):
        is_own = is_here[s : s + 1] > 0
        for n in range(OWN):
            chosen[n] = jnp.where(is_own & (own_before == n) & (n < own_limit), local_slots[s : s + 1] + LEAVES, chosen[n])
        left = jnp.where(is_own & (own_before < own_limit), 0.0, 1.0)
        live_rows.append(jnp.where(slots[s : s + 1] >= 0, left, 0.0))
        own_before = own_before + is_here[s : s + 1]
    for n in range(OWN):
        choice_vector[n : n + 1, 0:LEAVES] = chosen[n]
    choice_copy = pltpu.make_async_copy(choice_vector, choice, choice_sem)
    choice_copy.start()
    live = jnp.concatenate(live_rows, axis=0)
    before = (
        lax.broadcasted_iota(jnp.int32, (LEAVES, LEAVES), 0) < lax.broadcasted_iota(jnp.int32, (LEAVES, LEAVES), 1)
    ).astype(BF16)
    rank_in_slot = jnp.dot(live.astype(BF16), before, preferred_element_type=F32)
    in_slot = jnp.sum(live, axis=1, keepdims=True)
    leaf_row = lax.broadcasted_iota(jnp.int32, (1, LEAVES), 1)
    code = (leaf_row * 256 + slots - (device - 1) * LEAVES).astype(F32)
    position_row = lax.broadcasted_iota(jnp.int32, (1, PAIRS), 1).astype(F32)
    found = jnp.zeros((LEAVES, PAIRS), F32)
    start = jnp.zeros((1, 1), F32)
    positions = []
    for s in range(NEAR):
        positions.append(jnp.where(live[s : s + 1] > 0, rank_in_slot[s : s + 1] + start, -1.0))
        start = start + in_slot[s : s + 1]
    table = jnp.concatenate(positions + [code], axis=0).T
    for s in range(NEAR):
        found = jnp.where(table[:, s : s + 1] == position_row, table[:, NEAR + s : NEAR + s + 1], found)
    pairs = jnp.sum(found, axis=0, keepdims=True)
    pair_out[0:1, 0:PAIRS] = jnp.where(position_row < start, pairs, float(BLANK)).astype(jnp.int32)
    pair_out[0:1, PAIRS:] = jnp.full((1, 128), BLANK, jnp.int32)
    pair_out[1:2, 0:128] = jnp.broadcast_to(start.astype(jnp.int32), (1, 128))
    def own_terms(c):
        span = pl.ds(pl.multiple_of(c * CHUNK, CHUNK), CHUNK)
        parts, norm = centred([own[n, span, :] for n in range(1, 4)])
        source_out[pl.ds(LEAVES + c * CHUNK, CHUNK)] = by_leaf(source_terms(parts, norm)).astype(BF16)
        target = by_leaf(target_terms(parts, norm)).astype(BF16)
        for k in range(CHUNK):
            target_out[c * CHUNK + k] = target[k].T

    pl.loop(0, terms_before)(own_terms)
    charge_out[LEAVES : 2 * LEAVES] = own[0]
    charge_out[3 * LEAVES :] = jnp.zeros((8, POINTS), F32)
    term = lax.broadcasted_iota(jnp.int32, (TERMS, POINTS), 0)
    source_out[BLANK] = jnp.where(term == 18, 1.0, 0.0).astype(BF16)

    lane = lax.broadcasted_iota(jnp.int32, (RANK, LEAVES), 1)

    def moment_chunk(c, carry):
        columns, total = carry
        for copy in load_copies(c):
            copy.wait()
        weights = own[0, pl.ds(pl.multiple_of(c * CHUNK, CHUNK), CHUNK), :]
        for k in range(CHUNK):
            product = bases[c * CHUNK + k] * weights[k : k + 1, :]
            column = jnp.sum(product[:, :128] + product[:, 128:], axis=1, keepdims=True)
            columns = jnp.where(lane == c * CHUNK + k, column, columns)
            total = total + transfer[c * CHUNK + k] * column
        return columns, total

    carry = lax.fori_loop(
        0, moments_before, moment_chunk, (jnp.zeros((RANK, LEAVES), F32), jnp.zeros((RANK, RANK), F32))
    )
    pl.semaphore_wait(barrier, 4 + sum(count - 1 for _, count in STAGES))

    part_leaves = LEAVES // HALO_PARTS
    copies_of_halo = [
        [
            pltpu.make_async_remote_copy(
                src_ref=own.at[:, pl.ds(part * part_leaves, part_leaves)],
                dst_ref=halo.at[side, :, pl.ds(part * part_leaves, part_leaves)],
                send_sem=halo_send.at[part, side],
                recv_sem=halo_recv.at[part, side],
                device_id=beside(distance),
                device_id_type=MESH,
            )
            for side, distance in ((0, 1), (1, -1))
        ]
        for part in range(HALO_PARTS)
    ]
    for copy in copies_of_halo[0]:
        copy.start()

    columns, total = lax.fori_loop(moments_before, chunks, moment_chunk, carry)
    rows = columns.T
    window[2] = jnp.concatenate([rows[: LEAVES // 2], rows[LEAVES // 2 :]], axis=1)
    unit = eye()
    cluster_row = jnp.sum(total, axis=0, keepdims=True)
    lifted_row = jnp.sum(cluster_transfer[0] * to_column(cluster_row, unit), axis=0, keepdims=True)
    every[row, 0:1, 0:RANK] = cluster_row
    every[row, 0:1, RANK : 2 * RANK] = lifted_row

    def every_copy(stage, k):
        unit, _ = STAGES[stage]
        rows = pl.ds((row // unit) * unit, unit)
        return pltpu.make_async_remote_copy(
            src_ref=every.at[rows],
            dst_ref=every.at[rows],
            send_sem=every_send.at[stage, k],
            recv_sem=every_recv.at[stage, k],
            device_id=mate(stage, k),
            device_id_type=MESH,
        )

    def start_stage(stage):
        for k in range(1, STAGES[stage][1]):
            every_copy(stage, k).start()

    def finish_stage(stage):
        for k in range(1, STAGES[stage][1]):
            every_copy(stage, k).wait_recv()

    def next_stage(stage):
        finish_stage(stage)
        start_stage(stage + 1)
        for copy in copies_of_halo[stage + 2]:
            copy.start()

    start_stage(0)

    @pl.loop(0, far_chunk_count)
    def _(c):
        coupling_copy(c).start()

    def moment_copies():
        copies = []
        for n, distance in enumerate((2, 1, -1, -2)):
            slot = (0, 1, 3, 4)[n]
            copies.append(
                pltpu.make_async_remote_copy(
                    src_ref=window.at[2],
                    dst_ref=window.at[slot],
                    send_sem=moment_send.at[n],
                    recv_sem=moment_recv.at[n],
                    device_id=beside(distance),
                    device_id_type=MESH,
                )
            )
        return copies

    moments = moment_copies()
    for copy in moments:
        copy.start()
    for copy in copies_of_halo[1]:
        copy.start()

    pl.loop(terms_before, chunks)(own_terms)

    choice_copy.wait()

    for n in range(OWN):

        @pl.loop(0, LEAVES // GROUP if n == 0 else jnp.where(own_limit > n, LEAVES // GROUP, 0))
        def _(g):
            for k in range(GROUP):
                i = g * GROUP + k
                j = jnp.clip(choice[n, i], 0, BLANK)
                square = jnp.dot(target_out[i], source_out[j], preferred_element_type=F32)
                part = folded(square, charge_out[pl.ds(j, 1), :])
                if n == 0:
                    near_out[i] = part
                else:
                    near_out[i] += part

            if n < 2:

                @pl.when(g == 0)
                def _():
                    next_stage(n)

    @pl.when(own_limit < 2)
    def _():
        next_stage(1)

    for copy in moments:
        copy.wait_recv()
    for n in range(5):
        moment_rows[n * LEAVES : n * LEAVES + LEAVES // 2] = window[n][:, :RANK]
        moment_rows[n * LEAVES + LEAVES // 2 : (n + 1) * LEAVES] = window[n][:, RANK:]
    moment_rows[5 * LEAVES :] = jnp.zeros((8, RANK), F32)
    far_copy.wait()

    def far_chunk(c):
        coupling_copy(c).wait()
        for k in range(CHUNK):
            i = c * CHUNK + k
            total = None
            for f in range(FAR):
                slot = jnp.clip(far_rows[i, f], 0, 5 * LEAVES)
                term = coupling[i * FAR + f] * moment_rows[pl.ds(slot, 1), :]
                total = term if total is None else total + term
            far_out[i] = total

    def far_chunks(first, last):
        pl.loop(first, last)(far_chunk)

    far_chunks(0, 4)

    for part in range(HALO_PARTS):
        for side in range(2):
            copies_of_halo[part][side].wait_recv()
            first = 2 * LEAVES * side

            @pl.loop(part * part_leaves // CHUNK, (part + 1) * part_leaves // CHUNK)
            def _(c):
                span = pl.ds(pl.multiple_of(c * CHUNK, CHUNK), CHUNK)
                parts, norm = centred([halo[side, n, span, :] for n in range(1, 4)])
                source_out[pl.ds(first + c * CHUNK, CHUNK)] = by_leaf(source_terms(parts, norm)).astype(BF16)

    charge_out[0:LEAVES] = halo[0, 0]
    charge_out[2 * LEAVES : 3 * LEAVES] = halo[1, 0]

    far_chunks(4, far_chunk_count)

    finish_stage(2)
    every_out[...] = every[...]

    for stage in range(len(STAGES)):
        for k in range(1, STAGES[stage][1]):
            every_copy(stage, k).wait_send()
    for copy in sum(copies_of_halo, []) + moments:
        copy.wait_send()


def local_kernel(
    source, target, charges, every, pairs_vmem, bases, transfer, near_first, far_first, far_vmem, moments,
    cluster_target_hbm, group_target_hbm, top_target_hbm, cluster_transfer_hbm, cluster_coupling_hbm,
    group_coupling_hbm, group_transfer_hbm, top_coupling_hbm, coupling_hbm,
    out, near_total, far_total,
    coupling, far_rows, parts, near_columns, cluster_transfer, cluster_coupling, group_coupling, group_transfer, top_coupling,
    group_moments, pairs, cluster_target, group_target, top_target,
    sems,
):
    gx = lax.axis_index("gx")
    top = gx // 4

    loads = [
        pltpu.make_async_copy(source_ref, landing, sems.at[n])
        for n, (source_ref, landing) in enumerate(
            (
                (pairs_vmem, pairs),
                (far_vmem, far_rows),
                (cluster_target_hbm, cluster_target),
                (group_target_hbm, group_target),
                (top_target_hbm, top_target),
                (cluster_transfer_hbm, cluster_transfer),
                (cluster_coupling_hbm, cluster_coupling),
                (group_coupling_hbm, group_coupling),
                (group_transfer_hbm, group_transfer),
                (top_coupling_hbm.at[top], top_coupling),
                (coupling_hbm.at[pl.ds(EXCHANGED * FAR, (LEAVES - EXCHANGED) * FAR)], coupling),
            )
        )
    ]
    for copy in loads:
        copy.start()

    for k in range(GROUP):
        parts[k] = jnp.zeros((POINTS, 128), F32)
    loads[0].wait()

    def add_parts(first, count):
        for k in range(count):
            near_total[pairs[0, first + k] // 256] += parts[k]

    def listed_pairs(first, count):
        for k in range(count):
            code = pairs[0, first + k]
            i, j = code // 256, code % 256
            square = jnp.dot(target[i], source[j], preferred_element_type=F32)
            parts[k] = folded(square, charges[pl.ds(j, 1), :])

    live = pairs[1, 0]
    groups = (live + GROUP - LAST_GROUP - 1) // GROUP

    @pl.loop(0, groups)
    def _(g):
        add_parts(jnp.maximum(g - 1, 0) * GROUP, GROUP)
        listed_pairs(g * GROUP, GROUP)

    last = jnp.maximum(groups - 1, 0) * GROUP

    @pl.when(live > groups * GROUP)
    def _():
        add_parts(last, GROUP)
        listed_pairs(groups * GROUP, LAST_GROUP)
        add_parts(groups * GROUP, LAST_GROUP)

    @pl.when(live <= groups * GROUP)
    def _():
        add_parts(last, GROUP)

    unit = eye()
    for copy in loads[1:]:
        copy.wait()

    @pl.loop(0, (LEAVES - EXCHANGED) // CHUNK)
    def _(c):
        for k in range(CHUNK):
            i = c * CHUNK + k
            total = None
            for f in range(FAR):
                term = coupling[i * FAR + f] * moments[pl.ds(far_rows[EXCHANGED + i, f], 1), :]
                total = term if total is None else total + term
            far_total[EXCHANGED + i] = total


    quarter = DEVICES // 4
    group_moments[...] = sum(every[pl.ds(k * quarter, quarter), 0, :][:, RANK:] for k in range(4))
    def masked(t):
        return jnp.where(t >= 0, 1.0, 0.0).astype(F32), jnp.maximum(t, 0)

    total = jnp.zeros((RANK, RANK), F32)
    for f in range(4):
        weight, t = masked(top_target[f, top])
        lifted = jnp.zeros((RANK, RANK), F32)
        for k in range(4):
            g = 4 * t + k
            lifted = lifted + group_transfer[g] * to_column(group_moments[pl.ds(g, 1), :], unit)
        total = total + top_coupling[f] * (jnp.sum(lifted, axis=0, keepdims=True) * weight)
    top_local = to_row(jnp.sum(total, axis=1, keepdims=True), unit)
    total = group_transfer[gx] * top_local
    for f in range(8):
        weight, t = masked(group_target[0, f])
        total = total + group_coupling[0, f] * (group_moments[pl.ds(t, 1), :] * weight)
    group_local = to_row(jnp.sum(total, axis=1, keepdims=True), unit)
    total = cluster_transfer[0] * group_local
    for f in range(8):
        weight, t = masked(cluster_target[0, f])
        total = total + cluster_coupling[0, f] * (every[(t % 4) * quarter + t // 4, :, :RANK] * weight)
    cluster_local = to_row(jnp.sum(total, axis=1, keepdims=True), unit)

    near_columns[...] = jnp.zeros((POINTS, 128), F32)

    @pl.loop(0, LEAVES // CHUNK)
    def _(c):
        rows = []
        for k in range(CHUNK):
            i = c * CHUNK + k
            total = transfer[i] * cluster_local + far_total[i]
            leaf_local = jnp.sum(total, axis=1, keepdims=True)
            rows.append(jnp.sum(bases[i] * leaf_local, axis=0, keepdims=True))
        near_columns[...] += lane_sums(near_total.at[pl.ds(c * CHUNK, CHUNK)], c * CHUNK)
        out[pl.ds(pl.multiple_of(c * CHUNK, CHUNK), CHUNK), :] = jnp.concatenate(rows, axis=0)

    out[...] += near_columns[...].T[:LEAVES] * INVERSE_FOUR_PI


def local(
    charges, points, leaf_bases, leaf_transfer, near_target, far_target, leaf_coupling, cluster_transfer,
    cluster_target, cluster_coupling, group_transfer, group_target, group_coupling, top_target, top_coupling,
):
    vmem = pl.BlockSpec(memory_space=pltpu.VMEM)
    anywhere = pl.BlockSpec(memory_space=pl.ANY)
    dma = pltpu.SemaphoreType.DMA

    def in_hbm(*arrays):
        return [pltpu.with_memory_space_constraint(array, pltpu.HBM) for array in arrays]

    handed = pl.pallas_call(
        exchange_kernel,
        out_shape=(
            pltpu.VMEM((3 * LEAVES + 1, TERMS, POINTS), BF16),
            pltpu.VMEM((LEAVES, POINTS, TERMS), BF16),
            pltpu.VMEM((3 * LEAVES + 8, POINTS), F32),
            pltpu.VMEM((DEVICES, 1, 2 * RANK), F32),
            pltpu.VMEM((2, PAIRS + 128), jnp.int32),
            pltpu.VMEM((LEAVES, RANK, POINTS), F32),
            pltpu.VMEM((LEAVES, RANK, RANK), F32),
            pltpu.VMEM((LEAVES, POINTS, 128), F32),
            pltpu.VMEM((LEAVES, RANK, RANK), F32),
            pltpu.VMEM((LEAVES, FAR), jnp.int32),
            pltpu.VMEM((5 * LEAVES + 8, RANK), F32),
        ),
        in_specs=[anywhere] * 8,
        out_specs=[vmem] * 11,
        scratch_shapes=[
            pltpu.VMEM((EXCHANGED * FAR, RANK, RANK), F32),
            pltpu.SMEM((LEAVES, FAR), jnp.int32),
            pltpu.VMEM((8, 128), jnp.int32),
            pltpu.SMEM((8, 128), jnp.int32),
            pltpu.VMEM((4, LEAVES, POINTS), F32),
            pltpu.VMEM((NEAR, LEAVES), jnp.int32),
            pltpu.VMEM((FAR, LEAVES), jnp.int32),
            pltpu.VMEM((1, RANK, RANK), F32),
            pltpu.VMEM((2, 4, LEAVES, POINTS), F32),
            pltpu.VMEM((5, LEAVES // 2, 2 * RANK), F32),
            pltpu.VMEM((DEVICES, 1, 2 * RANK), F32),
            dma((LEAVES // CHUNK,)),
            dma,
            dma,
            dma((2, LEAVES // CHUNK)),
            dma((5,)),
            dma((HALO_PARTS, 2)),
            dma((HALO_PARTS, 2)),
            dma((4,)),
            dma((4,)),
            dma((len(STAGES), 8)),
            dma((len(STAGES), 8)),
        ],
        compiler_params=pltpu.CompilerParams(
            collective_id=0, has_side_effects=True, vmem_limit_bytes=30 << 20
        ),
        name="exchange",
    )(
        *in_hbm(
            charges,
            jnp.transpose(points, (1, 0, 2)),
            near_target.T,
            far_target.T,
            cluster_transfer,
            jnp.swapaxes(leaf_bases, 1, 2),
            leaf_transfer,
            leaf_coupling.reshape(LEAVES * FAR, RANK, RANK),
        )
    )
    return pl.pallas_call(
        local_kernel,
        out_shape=(
            jax.ShapeDtypeStruct((LEAVES, POINTS), F32),
            pltpu.VMEM((LEAVES, POINTS, 128), F32),
            pltpu.VMEM((LEAVES, RANK, RANK), F32),
        ),
        in_specs=[vmem] * 11 + [anywhere] * 9,
        out_specs=[vmem] * 3,
        input_output_aliases={7: 1, 8: 2},
        scratch_shapes=[
            pltpu.VMEM(((LEAVES - EXCHANGED) * FAR, RANK, RANK), F32),
            pltpu.SMEM((LEAVES, FAR), jnp.int32),
            pltpu.VMEM((GROUP, POINTS, 128), F32),
            pltpu.VMEM((POINTS, 128), F32),
            pltpu.VMEM((1, RANK, RANK), F32),
            pltpu.VMEM((1, 8, RANK, RANK), F32),
            pltpu.VMEM((1, 8, RANK, RANK), F32),
            pltpu.VMEM((32, RANK, RANK), F32),
            pltpu.VMEM((4, RANK, RANK), F32),
            pltpu.VMEM((32, RANK), F32),
            pltpu.SMEM((2, PAIRS + 128), jnp.int32),
            pltpu.SMEM((1, 8), jnp.int32),
            pltpu.SMEM((1, 8), jnp.int32),
            pltpu.SMEM((4, 8), jnp.int32),
            dma((11,)),
        ],
        compiler_params=pltpu.CompilerParams(vmem_limit_bytes=30 << 20),
        name="local",
    )(
        *[pltpu.with_memory_space_constraint(array, pltpu.VMEM) for array in handed],
        *in_hbm(
            cluster_target,
            group_target,
            top_target.T,
            cluster_transfer,
            cluster_coupling,
            group_coupling,
            group_transfer,
            top_coupling,
            leaf_coupling.reshape(LEAVES * FAR, RANK, RANK),
        ),
    )[0]


def solution(mesh):
    leaf = ("gx", "gy")
    return jax.shard_map(
        local,
        mesh=mesh,
        in_specs=(
            P(leaf, None),
            P(leaf, None, None),
            P(leaf, None, None),
            P(leaf, None, None),
            P(leaf, None),
            P(leaf, None),
            P(leaf, None, None, None),
            P(leaf, None, None),
            P(leaf, None),
            P(leaf, None, None, None),
            P(),
            P("gx", None),
            P("gx", None, None, None),
            P(),
            P(),
        ),
        out_specs=P(leaf, None),
        check_vma=False,
    )
```

```python
import functools
import math

import jax
import jax.numpy as jnp
from jax import lax
from jax.experimental import pallas as pl
from jax.experimental.pallas import tpu as pltpu
from jax.sharding import PartitionSpec as P

MESH = pl.DeviceIdType.MESH
F32 = jnp.float32
BF16 = jnp.bfloat16
SMOOTHING = 0.01
INVERSE_FOUR_PI = 1.0 / (4.0 * math.pi)

LEAVES = 64
POINTS = 256
RANK = 64
NEAR = 8
FAR = 16
TERMS = 32
PAIRS = LEAVES * NEAR
GROUP = 32
LAST_GROUP = 16
EXCHANGED = 48
OWN = 2
CHUNK = 8
DEVICES = 128
STAGES = ((1, 8), (8, 4), (32, 4))
HALO_PARTS = 2
BLANK = 3 * LEAVES


def split3(value):
    high = value.astype(BF16).astype(F32)
    rest = value - high
    middle = rest.astype(BF16).astype(F32)
    low = (rest - middle).astype(BF16).astype(F32)
    return high, middle, low


def centred(points):
    shifted = [p - 1.0 for p in points]
    norm = shifted[0] * shifted[0] + shifted[1] * shifted[1] + shifted[2] * shifted[2]
    return [split3(u) for u in shifted], norm


def source_terms(parts, norm):
    rows = []
    for high, middle, low in parts:
        high, middle, low = -2.0 * high, -2.0 * middle, -2.0 * low
        rows += [high, high, high, middle, middle, low]
    one = jnp.ones_like(norm)
    return rows + list(split3(norm + SMOOTHING)) + [one, one, one]


def target_terms(parts, norm):
    rows = []
    for high, middle, low in parts:
        rows += [high, middle, low, high, middle, high]
    one = jnp.ones_like(norm)
    return rows + [one, one, one] + list(split3(norm))


def by_leaf(rows):
    blank = jnp.zeros_like(rows[0])
    return jnp.swapaxes(jnp.stack(rows + [blank] * (TERMS - len(rows)), axis=0), 0, 1)


def eye():
    shape = (RANK, RANK)
    return (lax.broadcasted_iota(jnp.int32, shape, 0) == lax.broadcasted_iota(jnp.int32, shape, 1)).astype(F32)


def to_column(row, unit):
    return jnp.sum(unit * row, axis=1, keepdims=True)


def to_row(column, unit):
    return jnp.sum(unit * column, axis=0, keepdims=True)


def lane_sums(parts, first):
    odd = lax.broadcasted_iota(jnp.int32, (POINTS, 128), 1) % 2
    source = lax.broadcasted_iota(jnp.int32, (256, 128), 0)
    column = lax.broadcasted_iota(jnp.int32, (256, 128), 1) - first
    total = None
    for k in range(0, CHUNK, 4):
        halves = []
        for n in (k, k + 2):
            here, there = parts[n], parts[n + 1]
            halves.append(jnp.where(odd == 0, here, there) + pltpu.roll(jnp.where(odd == 0, there, here), 127, axis=1))
        values = jnp.concatenate(halves, axis=1)
        high = values.astype(BF16)
        low = (values - high.astype(F32)).astype(BF16)
        ones = jnp.where(k + source // 128 * 2 + source % 2 == column, 1.0, 0.0).astype(BF16)
        for piece in (high, low):
            term = jnp.dot(piece, ones, preferred_element_type=F32)
            total = term if total is None else total + term
    return total


def folded(square, charge):
    weighted = lax.rsqrt(square) * charge
    return weighted[:, :128] + weighted[:, 128:]


def exchange_kernel(
    charges_hbm, points_hbm, near_hbm, far_hbm, cluster_transfer_hbm, bases_hbm, transfer_hbm, coupling_hbm,
    source_out, target_out, charge_out, every_out, pair_out, bases, transfer, near_out, far_out, far_vector, moment_rows,
    coupling, far_rows, choice_vector, choice, own, near, far, cluster_transfer, halo, window, every,
    coupling_sems, far_sem, choice_sem, load_sems, small_sems, halo_send, halo_recv, moment_send, moment_recv, every_send, every_recv,
):
    gx, gy = lax.axis_index("gx"), lax.axis_index("gy")
    device = gx * 4 + gy

    def place(index):
        return (index // 4, index % 4)

    def beside(distance):
        return place((device + distance + DEVICES) % DEVICES)

    chunks = LEAVES // CHUNK
    lateness = (gx // 2) % 4 + gx // 8 + 2 * gy
    terms_before = jnp.where(lateness <= 6, chunks, 0)
    moments_before = jnp.where(lateness <= 4, chunks, 0)
    own_limit = jnp.where(lateness <= 6, OWN, 1)

    def load_copies(c):
        span = pl.ds(c * CHUNK, CHUNK)
        return (
            pltpu.make_async_copy(bases_hbm.at[span], bases.at[span], load_sems.at[0, c]),
            pltpu.make_async_copy(transfer_hbm.at[span], transfer.at[span], load_sems.at[1, c]),
        )

    small = [
        pltpu.make_async_copy(source, landing, small_sems.at[n])
        for n, (source, landing) in enumerate(
            (
                (charges_hbm, own.at[0]),
                (points_hbm, own.at[pl.ds(1, 3)]),
                (near_hbm, near),
                (far_hbm, far),
                (cluster_transfer_hbm, cluster_transfer),
            )
        )
    ]
    for copy in small:
        copy.start()

    @pl.loop(0, chunks)
    def _(c):
        for copy in load_copies(c):
            copy.start()

    def coupling_copy(c):
        span = pl.ds(c * CHUNK * FAR, CHUNK * FAR)
        return pltpu.make_async_copy(coupling_hbm.at[span], coupling.at[span], coupling_sems.at[c])

    far_chunk_count = EXCHANGED // CHUNK

    barrier = pltpu.get_barrier_semaphore()
    for distance in (1, -1, 2, -2):
        pl.semaphore_signal(barrier, inc=1, device_id=beside(distance), device_id_type=MESH)

    row = gy * (DEVICES // 4) + gx

    def mate(stage, k):
        unit, count = STAGES[stage]
        position = (row // unit) % count
        there = row + ((position + k) % count - position) * unit
        return (there % (DEVICES // 4), there // (DEVICES // 4))

    for stage in range(len(STAGES)):

        @pl.loop(1, STAGES[stage][1])
        def _(k):
            pl.semaphore_signal(barrier, inc=1, device_id=mate(stage, k), device_id_type=MESH)

    for copy in small:
        copy.wait()
    far_targets = far[...]
    far_vector[...] = jnp.where(far_targets >= 0, far_targets - (device - 2) * LEAVES, 5 * LEAVES).T
    far_copy = pltpu.make_async_copy(far_vector, far_rows, far_sem)
    far_copy.start()

    slots = near[...]
    local_slots = slots - device * LEAVES
    is_here = jnp.where((local_slots >= 0) & (local_slots < LEAVES), 1, 0)
    live_rows = []
    own_before = jnp.zeros((1, LEAVES), jnp.int32)
    chosen = [jnp.full((1, LEAVES), BLANK, jnp.int32) for _ in range(OWN)]
    for s in range(NEAR):
        is_own = is_here[s : s + 1] > 0
        for n in range(OWN):
            chosen[n] = jnp.where(is_own & (own_before == n) & (n < own_limit), local_slots[s : s + 1] + LEAVES, chosen[n])
        left = jnp.where(is_own & (own_before < own_limit), 0.0, 1.0)
        live_rows.append(jnp.where(slots[s : s + 1] >= 0, left, 0.0))
        own_before = own_before + is_here[s : s + 1]
    for n in range(OWN):
        choice_vector[n : n + 1, 0:LEAVES] = chosen[n]
    choice_copy = pltpu.make_async_copy(choice_vector, choice, choice_sem)
    choice_copy.start()
    live = jnp.concatenate(live_rows, axis=0)
    before = (
        lax.broadcasted_iota(jnp.int32, (LEAVES, LEAVES), 0) < lax.broadcasted_iota(jnp.int32, (LEAVES, LEAVES), 1)
    ).astype(BF16)
    rank_in_slot = jnp.dot(live.astype(BF16), before, preferred_element_type=F32)
    in_slot = jnp.sum(live, axis=1, keepdims=True)
    leaf_row = lax.broadcasted_iota(jnp.int32, (1, LEAVES), 1)
    code = (leaf_row * 256 + slots - (device - 1) * LEAVES).astype(F32)
    position_row = lax.broadcasted_iota(jnp.int32, (1, PAIRS), 1).astype(F32)
    found = jnp.zeros((LEAVES, PAIRS), F32)
    start = jnp.zeros((1, 1), F32)
    positions = []
    for s in range(NEAR):
        positions.append(jnp.where(live[s : s + 1] > 0, rank_in_slot[s : s + 1] + start, -1.0))
        start = start + in_slot[s : s + 1]
    table = jnp.concatenate(positions + [code], axis=0).T
    for s in range(NEAR):
        found = jnp.where(table[:, s : s + 1] == position_row, table[:, NEAR + s : NEAR + s + 1], found)
    pairs = jnp.sum(found, axis=0, keepdims=True)
    pair_out[0:1, 0:PAIRS] = jnp.where(position_row < start, pairs, float(BLANK)).astype(jnp.int32)
    pair_out[0:1, PAIRS:] = jnp.full((1, 128), BLANK, jnp.int32)
    pair_out[1:2, 0:128] = jnp.broadcast_to(start.astype(jnp.int32), (1, 128))
    def own_terms(c):
        span = pl.ds(pl.multiple_of(c * CHUNK, CHUNK), CHUNK)
        parts, norm = centred([own[n, span, :] for n in range(1, 4)])
        source_out[pl.ds(LEAVES + c * CHUNK, CHUNK)] = by_leaf(source_terms(parts, norm)).astype(BF16)
        target = by_leaf(target_terms(parts, norm)).astype(BF16)
        for k in range(CHUNK):
            target_out[c * CHUNK + k] = target[k].T

    pl.loop(0, terms_before)(own_terms)
    charge_out[LEAVES : 2 * LEAVES] = own[0]
    charge_out[3 * LEAVES :] = jnp.zeros((8, POINTS), F32)
    term = lax.broadcasted_iota(jnp.int32, (TERMS, POINTS), 0)
    source_out[BLANK] = jnp.where(term == 18, 1.0, 0.0).astype(BF16)

    lane = lax.broadcasted_iota(jnp.int32, (RANK, LEAVES), 1)

    def moment_chunk(c, carry):
        columns, total = carry
        for copy in load_copies(c):
            copy.wait()
        weights = own[0, pl.ds(pl.multiple_of(c * CHUNK, CHUNK), CHUNK), :]
        for k in range(CHUNK):
            product = bases[c * CHUNK + k] * weights[k : k + 1, :]
            column = jnp.sum(product[:, :128] + product[:, 128:], axis=1, keepdims=True)
            columns = jnp.where(lane == c * CHUNK + k, column, columns)
            total = total + transfer[c * CHUNK + k] * column
        return columns, total

    carry = lax.fori_loop(
        0, moments_before, moment_chunk, (jnp.zeros((RANK, LEAVES), F32), jnp.zeros((RANK, RANK), F32))
    )
    pl.semaphore_wait(barrier, 4 + sum(count - 1 for _, count in STAGES))

    part_leaves = LEAVES // HALO_PARTS
    copies_of_halo = [
        [
            pltpu.make_async_remote_copy(
                src_ref=own.at[:, pl.ds(part * part_leaves, part_leaves)],
                dst_ref=halo.at[side, :, pl.ds(part * part_leaves, part_leaves)],
                send_sem=halo_send.at[part, side],
                recv_sem=halo_recv.at[part, side],
                device_id=beside(distance),
                device_id_type=MESH,
            )
            for side, distance in ((0, 1), (1, -1))
        ]
        for part in range(HALO_PARTS)
    ]
    for copy in copies_of_halo[0]:
        copy.start()

    columns, total = lax.fori_loop(moments_before, chunks, moment_chunk, carry)
    rows = columns.T
    window[2] = jnp.concatenate([rows[: LEAVES // 2], rows[LEAVES // 2 :]], axis=1)
    unit = eye()
    cluster_row = jnp.sum(total, axis=0, keepdims=True)
    lifted_row = jnp.sum(cluster_transfer[0] * to_column(cluster_row, unit), axis=0, keepdims=True)
    every[row, 0:1, 0:RANK] = cluster_row
    every[row, 0:1, RANK : 2 * RANK] = lifted_row

    def every_copy(stage, k):
        unit, _ = STAGES[stage]
        rows = pl.ds((row // unit) * unit, unit)
        return pltpu.make_async_remote_copy(
            src_ref=every.at[rows],
            dst_ref=every.at[rows],
            send_sem=every_send.at[stage, k],
            recv_sem=every_recv.at[stage, k],
            device_id=mate(stage, k),
            device_id_type=MESH,
        )

    def start_stage(stage):
        for k in range(1, STAGES[stage][1]):
            every_copy(stage, k).start()

    def finish_stage(stage):
        for k in range(1, STAGES[stage][1]):
            every_copy(stage, k).wait_recv()

    start_stage(0)

    @pl.loop(0, far_chunk_count)
    def _(c):
        coupling_copy(c).start()

    def moment_copies():
        copies = []
        for n, distance in enumerate((2, 1, -1, -2)):
            slot = (0, 1, 3, 4)[n]
            copies.append(
                pltpu.make_async_remote_copy(
                    src_ref=window.at[2],
                    dst_ref=window.at[slot],
                    send_sem=moment_send.at[n],
                    recv_sem=moment_recv.at[n],
                    device_id=beside(distance),
                    device_id_type=MESH,
                )
            )
        return copies

    moments = moment_copies()
    for copy in moments:
        copy.start()
    for copies in copies_of_halo[1:]:
        for copy in copies:
            copy.start()

    pl.loop(terms_before, chunks)(own_terms)

    choice_copy.wait()

    for n in range(OWN):

        @pl.loop(0, LEAVES // GROUP if n == 0 else jnp.where(own_limit > n, LEAVES // GROUP, 0))
        def _(g):
            for k in range(GROUP):
                i = g * GROUP + k
                j = jnp.clip(choice[n, i], 0, BLANK)
                square = jnp.dot(target_out[i], source_out[j], preferred_element_type=F32)
                part = folded(square, charge_out[pl.ds(j, 1), :])
                if n == 0:
                    near_out[i] = part
                else:
                    near_out[i] += part

            @pl.when(g == jnp.where(own_limit > 1, 1, 0))
            def _():
                finish_stage(n)
                start_stage(n + 1)

    @pl.when(own_limit < 2)
    def _():
        finish_stage(1)
        start_stage(2)

    for copy in moments:
        copy.wait_recv()
    for n in range(5):
        moment_rows[n * LEAVES : n * LEAVES + LEAVES // 2] = window[n][:, :RANK]
        moment_rows[n * LEAVES + LEAVES // 2 : (n + 1) * LEAVES] = window[n][:, RANK:]
    moment_rows[5 * LEAVES :] = jnp.zeros((8, RANK), F32)
    far_copy.wait()

    def far_chunk(c):
        coupling_copy(c).wait()
        for k in range(CHUNK):
            i = c * CHUNK + k
            total = None
            for f in range(FAR):
                slot = jnp.clip(far_rows[i, f], 0, 5 * LEAVES)
                term = coupling[i * FAR + f] * moment_rows[pl.ds(slot, 1), :]
                total = term if total is None else total + term
            far_out[i] = total

    def far_chunks(first, last):
        pl.loop(first, last)(far_chunk)

    far_chunks(0, 4)

    for part in range(HALO_PARTS):
        for side in range(2):
            copies_of_halo[part][side].wait_recv()
            first = 2 * LEAVES * side

            @pl.loop(part * part_leaves // CHUNK, (part + 1) * part_leaves // CHUNK)
            def _(c):
                span = pl.ds(pl.multiple_of(c * CHUNK, CHUNK), CHUNK)
                parts, norm = centred([halo[side, n, span, :] for n in range(1, 4)])
                source_out[pl.ds(first + c * CHUNK, CHUNK)] = by_leaf(source_terms(parts, norm)).astype(BF16)

    charge_out[0:LEAVES] = halo[0, 0]
    charge_out[2 * LEAVES : 3 * LEAVES] = halo[1, 0]

    far_chunks(4, far_chunk_count)

    finish_stage(2)
    every_out[...] = every[...]

    for stage in range(len(STAGES)):
        for k in range(1, STAGES[stage][1]):
            every_copy(stage, k).wait_send()
    for copy in sum(copies_of_halo, []) + moments:
        copy.wait_send()


def local_kernel(
    source, target, charges, every, pairs_vmem, bases, transfer, near_first, far_first, far_vmem, moments,
    cluster_target_hbm, group_target_hbm, top_target_hbm, cluster_transfer_hbm, cluster_coupling_hbm,
    group_coupling_hbm, group_transfer_hbm, top_coupling_hbm, coupling_hbm,
    out, near_total, far_total,
    coupling, far_rows, parts, near_columns, cluster_transfer, cluster_coupling, group_coupling, group_transfer, top_coupling,
    group_moments, pairs, cluster_target, group_target, top_target,
    sems,
):
    gx = lax.axis_index("gx")
    top = gx // 4

    loads = [
        pltpu.make_async_copy(source_ref, landing, sems.at[n])
        for n, (source_ref, landing) in enumerate(
            (
                (pairs_vmem, pairs),
                (far_vmem, far_rows),
                (cluster_target_hbm, cluster_target),
                (group_target_hbm, group_target),
                (top_target_hbm, top_target),
                (cluster_transfer_hbm, cluster_transfer),
                (cluster_coupling_hbm, cluster_coupling),
                (group_coupling_hbm, group_coupling),
                (group_transfer_hbm, group_transfer),
                (top_coupling_hbm.at[top], top_coupling),
                (coupling_hbm.at[pl.ds(EXCHANGED * FAR, (LEAVES - EXCHANGED) * FAR)], coupling),
            )
        )
    ]
    for copy in loads:
        copy.start()

    for k in range(GROUP):
        parts[k] = jnp.zeros((POINTS, 128), F32)
    loads[0].wait()

    def add_parts(first, count):
        for k in range(count):
            near_total[pairs[0, first + k] // 256] += parts[k]

    def listed_pairs(first, count):
        for k in range(count):
            code = pairs[0, first + k]
            i, j = code // 256, code % 256
            square = jnp.dot(target[i], source[j], preferred_element_type=F32)
            parts[k] = folded(square, charges[pl.ds(j, 1), :])

    live = pairs[1, 0]
    groups = (live + GROUP - LAST_GROUP - 1) // GROUP

    @pl.loop(0, groups)
    def _(g):
        add_parts(jnp.maximum(g - 1, 0) * GROUP, GROUP)
        listed_pairs(g * GROUP, GROUP)

    last = jnp.maximum(groups - 1, 0) * GROUP

    @pl.when(live > groups * GROUP)
    def _():
        add_parts(last, GROUP)
        listed_pairs(groups * GROUP, LAST_GROUP)
        add_parts(groups * GROUP, LAST_GROUP)

    @pl.when(live <= groups * GROUP)
    def _():
        add_parts(last, GROUP)

    unit = eye()
    for copy in loads[1:]:
        copy.wait()

    @pl.loop(0, (LEAVES - EXCHANGED) // CHUNK)
    def _(c):
        for k in range(CHUNK):
            i = c * CHUNK + k
            total = None
            for f in range(FAR):
                term = coupling[i * FAR + f] * moments[pl.ds(far_rows[EXCHANGED + i, f], 1), :]
                total = term if total is None else total + term
            far_total[EXCHANGED + i] = total


    quarter = DEVICES // 4
    group_moments[...] = sum(every[pl.ds(k * quarter, quarter), 0, :][:, RANK:] for k in range(4))
    def masked(t):
        return jnp.where(t >= 0, 1.0, 0.0).astype(F32), jnp.maximum(t, 0)

    total = jnp.zeros((RANK, RANK), F32)
    for f in range(4):
        weight, t = masked(top_target[f, top])
        lifted = jnp.zeros((RANK, RANK), F32)
        for k in range(4):
            g = 4 * t + k
            lifted = lifted + group_transfer[g] * to_column(group_moments[pl.ds(g, 1), :], unit)
        total = total + top_coupling[f] * (jnp.sum(lifted, axis=0, keepdims=True) * weight)
    top_local = to_row(jnp.sum(total, axis=1, keepdims=True), unit)
    total = group_transfer[gx] * top_local
    for f in range(8):
        weight, t = masked(group_target[0, f])
        total = total + group_coupling[0, f] * (group_moments[pl.ds(t, 1), :] * weight)
    group_local = to_row(jnp.sum(total, axis=1, keepdims=True), unit)
    total = cluster_transfer[0] * group_local
    for f in range(8):
        weight, t = masked(cluster_target[0, f])
        total = total + cluster_coupling[0, f] * (every[(t % 4) * quarter + t // 4, :, :RANK] * weight)
    cluster_local = to_row(jnp.sum(total, axis=1, keepdims=True), unit)

    near_columns[...] = jnp.zeros((POINTS, 128), F32)

    @pl.loop(0, LEAVES // CHUNK)
    def _(c):
        rows = []
        for k in range(CHUNK):
            i = c * CHUNK + k
            total = transfer[i] * cluster_local + far_total[i]
            leaf_local = jnp.sum(total, axis=1, keepdims=True)
            rows.append(jnp.sum(bases[i] * leaf_local, axis=0, keepdims=True))
        near_columns[...] += lane_sums(near_total.at[pl.ds(c * CHUNK, CHUNK)], c * CHUNK)
        out[pl.ds(pl.multiple_of(c * CHUNK, CHUNK), CHUNK), :] = jnp.concatenate(rows, axis=0)

    out[...] += near_columns[...].T[:LEAVES] * INVERSE_FOUR_PI


def local(
    charges, points, leaf_bases, leaf_transfer, near_target, far_target, leaf_coupling, cluster_transfer,
    cluster_target, cluster_coupling, group_transfer, group_target, group_coupling, top_target, top_coupling,
):
    vmem = pl.BlockSpec(memory_space=pltpu.VMEM)
    anywhere = pl.BlockSpec(memory_space=pl.ANY)
    dma = pltpu.SemaphoreType.DMA

    def in_hbm(*arrays):
        return [pltpu.with_memory_space_constraint(array, pltpu.HBM) for array in arrays]

    handed = pl.pallas_call(
        exchange_kernel,
        out_shape=(
            pltpu.VMEM((3 * LEAVES + 1, TERMS, POINTS), BF16),
            pltpu.VMEM((LEAVES, POINTS, TERMS), BF16),
            pltpu.VMEM((3 * LEAVES + 8, POINTS), F32),
            pltpu.VMEM((DEVICES, 1, 2 * RANK), F32),
            pltpu.VMEM((2, PAIRS + 128), jnp.int32),
            pltpu.VMEM((LEAVES, RANK, POINTS), F32),
            pltpu.VMEM((LEAVES, RANK, RANK), F32),
            pltpu.VMEM((LEAVES, POINTS, 128), F32),
            pltpu.VMEM((LEAVES, RANK, RANK), F32),
            pltpu.VMEM((LEAVES, FAR), jnp.int32),
            pltpu.VMEM((5 * LEAVES + 8, RANK), F32),
        ),
        in_specs=[anywhere] * 8,
        out_specs=[vmem] * 11,
        scratch_shapes=[
            pltpu.VMEM((EXCHANGED * FAR, RANK, RANK), F32),
            pltpu.SMEM((LEAVES, FAR), jnp.int32),
            pltpu.VMEM((8, 128), jnp.int32),
            pltpu.SMEM((8, 128), jnp.int32),
            pltpu.VMEM((4, LEAVES, POINTS), F32),
            pltpu.VMEM((NEAR, LEAVES), jnp.int32),
            pltpu.VMEM((FAR, LEAVES), jnp.int32),
            pltpu.VMEM((1, RANK, RANK), F32),
            pltpu.VMEM((2, 4, LEAVES, POINTS), F32),
            pltpu.VMEM((5, LEAVES // 2, 2 * RANK), F32),
            pltpu.VMEM((DEVICES, 1, 2 * RANK), F32),
            dma((LEAVES // CHUNK,)),
            dma,
            dma,
            dma((2, LEAVES // CHUNK)),
            dma((5,)),
            dma((HALO_PARTS, 2)),
            dma((HALO_PARTS, 2)),
            dma((4,)),
            dma((4,)),
            dma((len(STAGES), 8)),
            dma((len(STAGES), 8)),
        ],
        compiler_params=pltpu.CompilerParams(
            collective_id=0, has_side_effects=True, vmem_limit_bytes=30 << 20
        ),
        name="exchange",
    )(
        *in_hbm(
            charges,
            jnp.transpose(points, (1, 0, 2)),
            near_target.T,
            far_target.T,
            cluster_transfer,
            jnp.swapaxes(leaf_bases, 1, 2),
            leaf_transfer,
            leaf_coupling.reshape(LEAVES * FAR, RANK, RANK),
        )
    )
    return pl.pallas_call(
        local_kernel,
        out_shape=(
            jax.ShapeDtypeStruct((LEAVES, POINTS), F32),
            pltpu.VMEM((LEAVES, POINTS, 128), F32),
            pltpu.VMEM((LEAVES, RANK, RANK), F32),
        ),
        in_specs=[vmem] * 11 + [anywhere] * 9,
        out_specs=[vmem] * 3,
        input_output_aliases={7: 1, 8: 2},
        scratch_shapes=[
            pltpu.VMEM(((LEAVES - EXCHANGED) * FAR, RANK, RANK), F32),
            pltpu.SMEM((LEAVES, FAR), jnp.int32),
            pltpu.VMEM((GROUP, POINTS, 128), F32),
            pltpu.VMEM((POINTS, 128), F32),
            pltpu.VMEM((1, RANK, RANK), F32),
            pltpu.VMEM((1, 8, RANK, RANK), F32),
            pltpu.VMEM((1, 8, RANK, RANK), F32),
            pltpu.VMEM((32, RANK, RANK), F32),
            pltpu.VMEM((4, RANK, RANK), F32),
            pltpu.VMEM((32, RANK), F32),
            pltpu.SMEM((2, PAIRS + 128), jnp.int32),
            pltpu.SMEM((1, 8), jnp.int32),
            pltpu.SMEM((1, 8), jnp.int32),
            pltpu.SMEM((4, 8), jnp.int32),
            dma((11,)),
        ],
        compiler_params=pltpu.CompilerParams(vmem_limit_bytes=30 << 20),
        name="local",
    )(
        *[pltpu.with_memory_space_constraint(array, pltpu.VMEM) for array in handed],
        *in_hbm(
            cluster_target,
            group_target,
            top_target.T,
            cluster_transfer,
            cluster_coupling,
            group_coupling,
            group_transfer,
            top_coupling,
            leaf_coupling.reshape(LEAVES * FAR, RANK, RANK),
        ),
    )[0]


def solution(mesh):
    leaf = ("gx", "gy")
    return jax.shard_map(
        local,
        mesh=mesh,
        in_specs=(
            P(leaf, None),
            P(leaf, None, None),
            P(leaf, None, None),
            P(leaf, None, None),
            P(leaf, None),
            P(leaf, None),
            P(leaf, None, None, None),
            P(leaf, None, None),
            P(leaf, None),
            P(leaf, None, None, None),
            P(),
            P("gx", None),
            P("gx", None, None, None),
            P(),
            P(),
        ),
        out_specs=P(leaf, None),
        check_vma=False,
    )
```

```python
import functools
import math

import jax
import jax.numpy as jnp
from jax import lax
from jax.experimental import pallas as pl
from jax.experimental.pallas import tpu as pltpu
from jax.sharding import PartitionSpec as P

MESH = pl.DeviceIdType.MESH
F32 = jnp.float32
BF16 = jnp.bfloat16
SMOOTHING = 0.01
INVERSE_FOUR_PI = 1.0 / (4.0 * math.pi)

LEAVES = 64
POINTS = 256
RANK = 64
NEAR = 8
FAR = 16
TERMS = 32
PAIRS = LEAVES * NEAR
GROUP = 32
LAST_GROUP = 16
EXCHANGED = 48
OWN = 2
CHUNK = 8
DEVICES = 128
STAGES = ((1, 8), (8, 4), (32, 4))
HALO_PARTS = 2
BLANK = 3 * LEAVES


def split3(value):
    high = value.astype(BF16).astype(F32)
    rest = value - high
    middle = rest.astype(BF16).astype(F32)
    low = (rest - middle).astype(BF16).astype(F32)
    return high, middle, low


def centred(points):
    shifted = [p - 1.0 for p in points]
    norm = shifted[0] * shifted[0] + shifted[1] * shifted[1] + shifted[2] * shifted[2]
    return [split3(u) for u in shifted], norm


def source_terms(parts, norm):
    rows = []
    for high, middle, low in parts:
        high, middle, low = -2.0 * high, -2.0 * middle, -2.0 * low
        rows += [high, high, high, middle, middle, low]
    one = jnp.ones_like(norm)
    return rows + list(split3(norm + SMOOTHING)) + [one, one, one]


def target_terms(parts, norm):
    rows = []
    for high, middle, low in parts:
        rows += [high, middle, low, high, middle, high]
    one = jnp.ones_like(norm)
    return rows + [one, one, one] + list(split3(norm))


def by_leaf(rows):
    blank = jnp.zeros_like(rows[0])
    return jnp.swapaxes(jnp.stack(rows + [blank] * (TERMS - len(rows)), axis=0), 0, 1)


def eye():
    shape = (RANK, RANK)
    return (lax.broadcasted_iota(jnp.int32, shape, 0) == lax.broadcasted_iota(jnp.int32, shape, 1)).astype(F32)


def to_column(row, unit):
    return jnp.sum(unit * row, axis=1, keepdims=True)


def to_row(column, unit):
    return jnp.sum(unit * column, axis=0, keepdims=True)


def lane_sums(parts, first):
    odd = lax.broadcasted_iota(jnp.int32, (POINTS, 128), 1) % 2
    source = lax.broadcasted_iota(jnp.int32, (256, 128), 0)
    column = lax.broadcasted_iota(jnp.int32, (256, 128), 1) - first
    total = None
    for k in range(0, CHUNK, 4):
        halves = []
        for n in (k, k + 2):
            here, there = parts[n], parts[n + 1]
            halves.append(jnp.where(odd == 0, here, there) + pltpu.roll(jnp.where(odd == 0, there, here), 127, axis=1))
        values = jnp.concatenate(halves, axis=1)
        high = values.astype(BF16)
        low = (values - high.astype(F32)).astype(BF16)
        ones = jnp.where(k + source // 128 * 2 + source % 2 == column, 1.0, 0.0).astype(BF16)
        for piece in (high, low):
            term = jnp.dot(piece, ones, preferred_element_type=F32)
            total = term if total is None else total + term
    return total


def folded(square, charge):
    weighted = lax.rsqrt(square) * charge
    return weighted[:, :128] + weighted[:, 128:]


def exchange_kernel(
    charges_hbm, points_hbm, near_hbm, far_hbm, cluster_transfer_hbm, bases_hbm, transfer_hbm, coupling_hbm,
    source_out, target_out, charge_out, every_out, pair_out, bases, transfer, near_out, far_out, far_vector, moment_rows,
    coupling, far_rows, choice_vector, choice, own, near, far, cluster_transfer, halo, window, every,
    coupling_sems, far_sem, choice_sem, load_sems, small_sems, halo_send, halo_recv, moment_send, moment_recv, every_send, every_recv,
):
    gx, gy = lax.axis_index("gx"), lax.axis_index("gy")
    device = gx * 4 + gy

    def place(index):
        return (index // 4, index % 4)

    def beside(distance):
        return place((device + distance + DEVICES) % DEVICES)

    chunks = LEAVES // CHUNK
    lateness = (gx // 2) % 4 + gx // 8 + 2 * gy
    terms_before = jnp.where(lateness <= 6, chunks, 0)
    moments_before = jnp.where(lateness <= 4, chunks, 0)
    own_limit = jnp.where(lateness <= 6, OWN, 1)

    def load_copies(c):
        span = pl.ds(c * CHUNK, CHUNK)
        return (
            pltpu.make_async_copy(bases_hbm.at[span], bases.at[span], load_sems.at[0, c]),
            pltpu.make_async_copy(transfer_hbm.at[span], transfer.at[span], load_sems.at[1, c]),
        )

    small = [
        pltpu.make_async_copy(source, landing, small_sems.at[n])
        for n, (source, landing) in enumerate(
            (
                (charges_hbm, own.at[0]),
                (points_hbm, own.at[pl.ds(1, 3)]),
                (near_hbm, near),
                (far_hbm, far),
                (cluster_transfer_hbm, cluster_transfer),
            )
        )
    ]
    for copy in small:
        copy.start()

    @pl.loop(0, chunks)
    def _(c):
        for copy in load_copies(c):
            copy.start()

    def coupling_copy(c):
        span = pl.ds(c * CHUNK * FAR, CHUNK * FAR)
        return pltpu.make_async_copy(coupling_hbm.at[span], coupling.at[span], coupling_sems.at[c])

    far_chunk_count = EXCHANGED // CHUNK

    barrier = pltpu.get_barrier_semaphore()
    for distance in (1, -1, 2, -2):
        pl.semaphore_signal(barrier, inc=1, device_id=beside(distance), device_id_type=MESH)

    row = gy * (DEVICES // 4) + gx

    def mate(stage, k):
        unit, count = STAGES[stage]
        position = (row // unit) % count
        there = row + ((position + k) % count - position) * unit
        return (there % (DEVICES // 4), there // (DEVICES // 4))

    for stage in range(len(STAGES)):

        @pl.loop(1, STAGES[stage][1])
        def _(k):
            pl.semaphore_signal(barrier, inc=1, device_id=mate(stage, k), device_id_type=MESH)

    for copy in small:
        copy.wait()
    far_targets = far[...]
    far_vector[...] = jnp.where(far_targets >= 0, far_targets - (device - 2) * LEAVES, 5 * LEAVES).T
    far_copy = pltpu.make_async_copy(far_vector, far_rows, far_sem)
    far_copy.start()

    slots = near[...]
    local_slots = slots - device * LEAVES
    is_here = jnp.where((local_slots >= 0) & (local_slots < LEAVES), 1, 0)
    live_rows = []
    own_before = jnp.zeros((1, LEAVES), jnp.int32)
    chosen = [jnp.full((1, LEAVES), BLANK, jnp.int32) for _ in range(OWN)]
    for s in range(NEAR):
        is_own = is_here[s : s + 1] > 0
        for n in range(OWN):
            chosen[n] = jnp.where(is_own & (own_before == n) & (n < own_limit), local_slots[s : s + 1] + LEAVES, chosen[n])
        left = jnp.where(is_own & (own_before < own_limit), 0.0, 1.0)
        live_rows.append(jnp.where(slots[s : s + 1] >= 0, left, 0.0))
        own_before = own_before + is_here[s : s + 1]
    for n in range(OWN):
        choice_vector[n : n + 1, 0:LEAVES] = chosen[n]
    choice_copy = pltpu.make_async_copy(choice_vector, choice, choice_sem)
    choice_copy.start()
    live = jnp.concatenate(live_rows, axis=0)
    before = (
        lax.broadcasted_iota(jnp.int32, (LEAVES, LEAVES), 0) < lax.broadcasted_iota(jnp.int32, (LEAVES, LEAVES), 1)
    ).astype(BF16)
    rank_in_slot = jnp.dot(live.astype(BF16), before, preferred_element_type=F32)
    in_slot = jnp.sum(live, axis=1, keepdims=True)
    leaf_row = lax.broadcasted_iota(jnp.int32, (1, LEAVES), 1)
    code = (leaf_row * 256 + slots - (device - 1) * LEAVES).astype(F32)
    position_row = lax.broadcasted_iota(jnp.int32, (1, PAIRS), 1).astype(F32)
    found = jnp.zeros((LEAVES, PAIRS), F32)
    start = jnp.zeros((1, 1), F32)
    positions = []
    for s in range(NEAR):
        positions.append(jnp.where(live[s : s + 1] > 0, rank_in_slot[s : s + 1] + start, -1.0))
        start = start + in_slot[s : s + 1]
    table = jnp.concatenate(positions + [code], axis=0).T
    for s in range(NEAR):
        found = jnp.where(table[:, s : s + 1] == position_row, table[:, NEAR + s : NEAR + s + 1], found)
    pairs = jnp.sum(found, axis=0, keepdims=True)
    pair_out[0:1, 0:PAIRS] = jnp.where(position_row < start, pairs, float(BLANK)).astype(jnp.int32)
    pair_out[0:1, PAIRS:] = jnp.full((1, 128), BLANK, jnp.int32)
    pair_out[1:2, 0:128] = jnp.broadcast_to(start.astype(jnp.int32), (1, 128))
    def own_terms(c):
        span = pl.ds(pl.multiple_of(c * CHUNK, CHUNK), CHUNK)
        parts, norm = centred([own[n, span, :] for n in range(1, 4)])
        source_out[pl.ds(LEAVES + c * CHUNK, CHUNK)] = by_leaf(source_terms(parts, norm)).astype(BF16)
        target = by_leaf(target_terms(parts, norm)).astype(BF16)
        for k in range(CHUNK):
            target_out[c * CHUNK + k] = target[k].T

    pl.loop(0, terms_before)(own_terms)
    charge_out[LEAVES : 2 * LEAVES] = own[0]
    charge_out[3 * LEAVES :] = jnp.zeros((8, POINTS), F32)
    term = lax.broadcasted_iota(jnp.int32, (TERMS, POINTS), 0)
    source_out[BLANK] = jnp.where(term == 18, 1.0, 0.0).astype(BF16)

    lane = lax.broadcasted_iota(jnp.int32, (RANK, LEAVES), 1)

    def moment_chunk(c, carry):
        columns, total = carry
        for copy in load_copies(c):
            copy.wait()
        weights = own[0, pl.ds(pl.multiple_of(c * CHUNK, CHUNK), CHUNK), :]
        for k in range(CHUNK):
            product = bases[c * CHUNK + k] * weights[k : k + 1, :]
            column = jnp.sum(product[:, :128] + product[:, 128:], axis=1, keepdims=True)
            columns = jnp.where(lane == c * CHUNK + k, column, columns)
            total = total + transfer[c * CHUNK + k] * column
        return columns, total

    carry = lax.fori_loop(
        0, moments_before, moment_chunk, (jnp.zeros((RANK, LEAVES), F32), jnp.zeros((RANK, RANK), F32))
    )
    pl.semaphore_wait(barrier, 4 + sum(count - 1 for _, count in STAGES))

    part_leaves = LEAVES // HALO_PARTS
    copies_of_halo = [
        [
            pltpu.make_async_remote_copy(
                src_ref=own.at[:, pl.ds(part * part_leaves, part_leaves)],
                dst_ref=halo.at[side, :, pl.ds(part * part_leaves, part_leaves)],
                send_sem=halo_send.at[part, side],
                recv_sem=halo_recv.at[part, side],
                device_id=beside(distance),
                device_id_type=MESH,
            )
            for side, distance in ((0, 1), (1, -1))
        ]
        for part in range(HALO_PARTS)
    ]
    for copy in copies_of_halo[0]:
        copy.start()

    columns, total = lax.fori_loop(moments_before, chunks, moment_chunk, carry)
    rows = columns.T
    window[2] = jnp.concatenate([rows[: LEAVES // 2], rows[LEAVES // 2 :]], axis=1)
    unit = eye()
    cluster_row = jnp.sum(total, axis=0, keepdims=True)
    lifted_row = jnp.sum(cluster_transfer[0] * to_column(cluster_row, unit), axis=0, keepdims=True)
    every[row, 0:1, 0:RANK] = cluster_row
    every[row, 0:1, RANK : 2 * RANK] = lifted_row

    def every_copy(stage, k):
        unit, _ = STAGES[stage]
        rows = pl.ds((row // unit) * unit, unit)
        return pltpu.make_async_remote_copy(
            src_ref=every.at[rows],
            dst_ref=every.at[rows],
            send_sem=every_send.at[stage, k],
            recv_sem=every_recv.at[stage, k],
            device_id=mate(stage, k),
            device_id_type=MESH,
        )

    def start_stage(stage):
        for k in range(1, STAGES[stage][1]):
            every_copy(stage, k).start()

    def finish_stage(stage):
        for k in range(1, STAGES[stage][1]):
            every_copy(stage, k).wait_recv()

    start_stage(0)

    @pl.loop(0, far_chunk_count)
    def _(c):
        coupling_copy(c).start()

    def moment_copies():
        copies = []
        for n, distance in enumerate((2, 1, -1, -2)):
            slot = (0, 1, 3, 4)[n]
            copies.append(
                pltpu.make_async_remote_copy(
                    src_ref=window.at[2],
                    dst_ref=window.at[slot],
                    send_sem=moment_send.at[n],
                    recv_sem=moment_recv.at[n],
                    device_id=beside(distance),
                    device_id_type=MESH,
                )
            )
        return copies

    for copies in copies_of_halo[1:]:
        for copy in copies:
            copy.start()
    moments = moment_copies()
    for copy in moments:
        copy.start()

    pl.loop(terms_before, chunks)(own_terms)

    choice_copy.wait()

    for n in range(OWN):

        @pl.loop(0, LEAVES // GROUP if n == 0 else jnp.where(own_limit > n, LEAVES // GROUP, 0))
        def _(g):
            for k in range(GROUP):
                i = g * GROUP + k
                j = jnp.clip(choice[n, i], 0, BLANK)
                square = jnp.dot(target_out[i], source_out[j], preferred_element_type=F32)
                part = folded(square, charge_out[pl.ds(j, 1), :])
                if n == 0:
                    near_out[i] = part
                else:
                    near_out[i] += part

            @pl.when(g == jnp.where(own_limit > 1, 1, 0))
            def _():
                finish_stage(n)
                start_stage(n + 1)

    @pl.when(own_limit < 2)
    def _():
        finish_stage(1)
        start_stage(2)

    def neighbour_terms(part):
        for side in range(2):
            copies_of_halo[part][side].wait_recv()
            first = 2 * LEAVES * side

            @pl.loop(part * part_leaves // CHUNK, (part + 1) * part_leaves // CHUNK)
            def _(c):
                span = pl.ds(pl.multiple_of(c * CHUNK, CHUNK), CHUNK)
                parts, norm = centred([halo[side, n, span, :] for n in range(1, 4)])
                source_out[pl.ds(first + c * CHUNK, CHUNK)] = by_leaf(source_terms(parts, norm)).astype(BF16)

    neighbour_terms(0)

    for copy in moments:
        copy.wait_recv()
    for n in range(5):
        moment_rows[n * LEAVES : n * LEAVES + LEAVES // 2] = window[n][:, :RANK]
        moment_rows[n * LEAVES + LEAVES // 2 : (n + 1) * LEAVES] = window[n][:, RANK:]
    moment_rows[5 * LEAVES :] = jnp.zeros((8, RANK), F32)
    far_copy.wait()

    def far_chunk(c):
        coupling_copy(c).wait()
        for k in range(CHUNK):
            i = c * CHUNK + k
            total = None
            for f in range(FAR):
                slot = jnp.clip(far_rows[i, f], 0, 5 * LEAVES)
                term = coupling[i * FAR + f] * moment_rows[pl.ds(slot, 1), :]
                total = term if total is None else total + term
            far_out[i] = total

    def far_chunks(first, last):
        pl.loop(first, last)(far_chunk)

    far_chunks(0, 4)

    neighbour_terms(1)
    charge_out[0:LEAVES] = halo[0, 0]
    charge_out[2 * LEAVES : 3 * LEAVES] = halo[1, 0]

    far_chunks(4, far_chunk_count)

    finish_stage(2)
    every_out[...] = every[...]

    for stage in range(len(STAGES)):
        for k in range(1, STAGES[stage][1]):
            every_copy(stage, k).wait_send()
    for copy in sum(copies_of_halo, []) + moments:
        copy.wait_send()


def local_kernel(
    source, target, charges, every, pairs_vmem, bases, transfer, near_first, far_first, far_vmem, moments,
    cluster_target_hbm, group_target_hbm, top_target_hbm, cluster_transfer_hbm, cluster_coupling_hbm,
    group_coupling_hbm, group_transfer_hbm, top_coupling_hbm, coupling_hbm,
    out, near_total, far_total,
    coupling, far_rows, parts, near_columns, cluster_transfer, cluster_coupling, group_coupling, group_transfer, top_coupling,
    group_moments, pairs, cluster_target, group_target, top_target,
    sems,
):
    gx = lax.axis_index("gx")
    top = gx // 4

    loads = [
        pltpu.make_async_copy(source_ref, landing, sems.at[n])
        for n, (source_ref, landing) in enumerate(
            (
                (pairs_vmem, pairs),
                (far_vmem, far_rows),
                (cluster_target_hbm, cluster_target),
                (group_target_hbm, group_target),
                (top_target_hbm, top_target),
                (cluster_transfer_hbm, cluster_transfer),
                (cluster_coupling_hbm, cluster_coupling),
                (group_coupling_hbm, group_coupling),
                (group_transfer_hbm, group_transfer),
                (top_coupling_hbm.at[top], top_coupling),
                (coupling_hbm.at[pl.ds(EXCHANGED * FAR, (LEAVES - EXCHANGED) * FAR)], coupling),
            )
        )
    ]
    for copy in loads:
        copy.start()

    for k in range(GROUP):
        parts[k] = jnp.zeros((POINTS, 128), F32)
    loads[0].wait()

    def add_parts(first, count):
        for k in range(count):
            near_total[pairs[0, first + k] // 256] += parts[k]

    def listed_pairs(first, count):
        for k in range(count):
            code = pairs[0, first + k]
            i, j = code // 256, code % 256
            square = jnp.dot(target[i], source[j], preferred_element_type=F32)
            parts[k] = folded(square, charges[pl.ds(j, 1), :])

    live = pairs[1, 0]
    groups = (live + GROUP - LAST_GROUP - 1) // GROUP

    @pl.loop(0, groups)
    def _(g):
        add_parts(jnp.maximum(g - 1, 0) * GROUP, GROUP)
        listed_pairs(g * GROUP, GROUP)

    last = jnp.maximum(groups - 1, 0) * GROUP

    @pl.when(live > groups * GROUP)
    def _():
        add_parts(last, GROUP)
        listed_pairs(groups * GROUP, LAST_GROUP)
        add_parts(groups * GROUP, LAST_GROUP)

    @pl.when(live <= groups * GROUP)
    def _():
        add_parts(last, GROUP)

    unit = eye()
    for copy in loads[1:]:
        copy.wait()

    @pl.loop(0, (LEAVES - EXCHANGED) // CHUNK)
    def _(c):
        for k in range(CHUNK):
            i = c * CHUNK + k
            total = None
            for f in range(FAR):
                term = coupling[i * FAR + f] * moments[pl.ds(far_rows[EXCHANGED + i, f], 1), :]
                total = term if total is None else total + term
            far_total[EXCHANGED + i] = total


    quarter = DEVICES // 4
    group_moments[...] = sum(every[pl.ds(k * quarter, quarter), 0, :][:, RANK:] for k in range(4))
    def masked(t):
        return jnp.where(t >= 0, 1.0, 0.0).astype(F32), jnp.maximum(t, 0)

    total = jnp.zeros((RANK, RANK), F32)
    for f in range(4):
        weight, t = masked(top_target[f, top])
        lifted = jnp.zeros((RANK, RANK), F32)
        for k in range(4):
            g = 4 * t + k
            lifted = lifted + group_transfer[g] * to_column(group_moments[pl.ds(g, 1), :], unit)
        total = total + top_coupling[f] * (jnp.sum(lifted, axis=0, keepdims=True) * weight)
    top_local = to_row(jnp.sum(total, axis=1, keepdims=True), unit)
    total = group_transfer[gx] * top_local
    for f in range(8):
        weight, t = masked(group_target[0, f])
        total = total + group_coupling[0, f] * (group_moments[pl.ds(t, 1), :] * weight)
    group_local = to_row(jnp.sum(total, axis=1, keepdims=True), unit)
    total = cluster_transfer[0] * group_local
    for f in range(8):
        weight, t = masked(cluster_target[0, f])
        total = total + cluster_coupling[0, f] * (every[(t % 4) * quarter + t // 4, :, :RANK] * weight)
    cluster_local = to_row(jnp.sum(total, axis=1, keepdims=True), unit)

    near_columns[...] = jnp.zeros((POINTS, 128), F32)

    @pl.loop(0, LEAVES // CHUNK)
    def _(c):
        rows = []
        for k in range(CHUNK):
            i = c * CHUNK + k
            total = transfer[i] * cluster_local + far_total[i]
            leaf_local = jnp.sum(total, axis=1, keepdims=True)
            rows.append(jnp.sum(bases[i] * leaf_local, axis=0, keepdims=True))
        near_columns[...] += lane_sums(near_total.at[pl.ds(c * CHUNK, CHUNK)], c * CHUNK)
        out[pl.ds(pl.multiple_of(c * CHUNK, CHUNK), CHUNK), :] = jnp.concatenate(rows, axis=0)

    out[...] += near_columns[...].T[:LEAVES] * INVERSE_FOUR_PI


def local(
    charges, points, leaf_bases, leaf_transfer, near_target, far_target, leaf_coupling, cluster_transfer,
    cluster_target, cluster_coupling, group_transfer, group_target, group_coupling, top_target, top_coupling,
):
    vmem = pl.BlockSpec(memory_space=pltpu.VMEM)
    anywhere = pl.BlockSpec(memory_space=pl.ANY)
    dma = pltpu.SemaphoreType.DMA

    def in_hbm(*arrays):
        return [pltpu.with_memory_space_constraint(array, pltpu.HBM) for array in arrays]

    handed = pl.pallas_call(
        exchange_kernel,
        out_shape=(
            pltpu.VMEM((3 * LEAVES + 1, TERMS, POINTS), BF16),
            pltpu.VMEM((LEAVES, POINTS, TERMS), BF16),
            pltpu.VMEM((3 * LEAVES + 8, POINTS), F32),
            pltpu.VMEM((DEVICES, 1, 2 * RANK), F32),
            pltpu.VMEM((2, PAIRS + 128), jnp.int32),
            pltpu.VMEM((LEAVES, RANK, POINTS), F32),
            pltpu.VMEM((LEAVES, RANK, RANK), F32),
            pltpu.VMEM((LEAVES, POINTS, 128), F32),
            pltpu.VMEM((LEAVES, RANK, RANK), F32),
            pltpu.VMEM((LEAVES, FAR), jnp.int32),
            pltpu.VMEM((5 * LEAVES + 8, RANK), F32),
        ),
        in_specs=[anywhere] * 8,
        out_specs=[vmem] * 11,
        scratch_shapes=[
            pltpu.VMEM((EXCHANGED * FAR, RANK, RANK), F32),
            pltpu.SMEM((LEAVES, FAR), jnp.int32),
            pltpu.VMEM((8, 128), jnp.int32),
            pltpu.SMEM((8, 128), jnp.int32),
            pltpu.VMEM((4, LEAVES, POINTS), F32),
            pltpu.VMEM((NEAR, LEAVES), jnp.int32),
            pltpu.VMEM((FAR, LEAVES), jnp.int32),
            pltpu.VMEM((1, RANK, RANK), F32),
            pltpu.VMEM((2, 4, LEAVES, POINTS), F32),
            pltpu.VMEM((5, LEAVES // 2, 2 * RANK), F32),
            pltpu.VMEM((DEVICES, 1, 2 * RANK), F32),
            dma((LEAVES // CHUNK,)),
            dma,
            dma,
            dma((2, LEAVES // CHUNK)),
            dma((5,)),
            dma((HALO_PARTS, 2)),
            dma((HALO_PARTS, 2)),
            dma((4,)),
            dma((4,)),
            dma((len(STAGES), 8)),
            dma((len(STAGES), 8)),
        ],
        compiler_params=pltpu.CompilerParams(
            collective_id=0, has_side_effects=True, vmem_limit_bytes=30 << 20
        ),
        name="exchange",
    )(
        *in_hbm(
            charges,
            jnp.transpose(points, (1, 0, 2)),
            near_target.T,
            far_target.T,
            cluster_transfer,
            jnp.swapaxes(leaf_bases, 1, 2),
            leaf_transfer,
            leaf_coupling.reshape(LEAVES * FAR, RANK, RANK),
        )
    )
    return pl.pallas_call(
        local_kernel,
        out_shape=(
            jax.ShapeDtypeStruct((LEAVES, POINTS), F32),
            pltpu.VMEM((LEAVES, POINTS, 128), F32),
            pltpu.VMEM((LEAVES, RANK, RANK), F32),
        ),
        in_specs=[vmem] * 11 + [anywhere] * 9,
        out_specs=[vmem] * 3,
        input_output_aliases={7: 1, 8: 2},
        scratch_shapes=[
            pltpu.VMEM(((LEAVES - EXCHANGED) * FAR, RANK, RANK), F32),
            pltpu.SMEM((LEAVES, FAR), jnp.int32),
            pltpu.VMEM((GROUP, POINTS, 128), F32),
            pltpu.VMEM((POINTS, 128), F32),
            pltpu.VMEM((1, RANK, RANK), F32),
            pltpu.VMEM((1, 8, RANK, RANK), F32),
            pltpu.VMEM((1, 8, RANK, RANK), F32),
            pltpu.VMEM((32, RANK, RANK), F32),
            pltpu.VMEM((4, RANK, RANK), F32),
            pltpu.VMEM((32, RANK), F32),
            pltpu.SMEM((2, PAIRS + 128), jnp.int32),
            pltpu.SMEM((1, 8), jnp.int32),
            pltpu.SMEM((1, 8), jnp.int32),
            pltpu.SMEM((4, 8), jnp.int32),
            dma((11,)),
        ],
        compiler_params=pltpu.CompilerParams(vmem_limit_bytes=30 << 20),
        name="local",
    )(
        *[pltpu.with_memory_space_constraint(array, pltpu.VMEM) for array in handed],
        *in_hbm(
            cluster_target,
            group_target,
            top_target.T,
            cluster_transfer,
            cluster_coupling,
            group_coupling,
            group_transfer,
            top_coupling,
            leaf_coupling.reshape(LEAVES * FAR, RANK, RANK),
        ),
    )[0]


def solution(mesh):
    leaf = ("gx", "gy")
    return jax.shard_map(
        local,
        mesh=mesh,
        in_specs=(
            P(leaf, None),
            P(leaf, None, None),
            P(leaf, None, None),
            P(leaf, None, None),
            P(leaf, None),
            P(leaf, None),
            P(leaf, None, None, None),
            P(leaf, None, None),
            P(leaf, None),
            P(leaf, None, None, None),
            P(),
            P("gx", None),
            P("gx", None, None, None),
            P(),
            P(),
        ),
        out_specs=P(leaf, None),
        check_vma=False,
    )
```
